32 devices in a mesh: dp: 8 (over z, y), tensor: 4 (over x, core).
Axes of the slice: x: 2, y: 2, z: 4, core: 2. Of those that a mesh axis runs over, the one named last changes fastest.
Arguments:
- inputs: bfloat16 [16384, 1024], P(('dp', 'tensor')), may hold values from -6 to 6
- out_grad: bfloat16 [16384, 1024], P(('dp', 'tensor')), may hold values from -6 to 6
- owners: int32 [4, 4], replicated, may hold values from 0 to 7, as said below
- master_slots: float32 [8, 4096, 1024], P('dp', 'tensor'), may hold values from -0.1875 to 0.1875
- momentum_slots: float32 [8, 4096, 1024], P('dp', 'tensor'), may hold values from -224 to 224
- small_master: float32 [12288], P(('dp', 'tensor')), may hold values from -0.8 to 1.4, as said below
- small_first: float32 [12288], P(('dp', 'tensor')), may hold values from -80 to 80
- small_second: float32 [12288], P(('dp', 'tensor')), may hold values from 245.76 to 2457.6
Outputs:
- block_out: bfloat16 [16384, 1024], P(('dp', 'tensor'))
- input_grad: float32 [16384, 1024], P(('dp', 'tensor'))
- grad_slots: float32 [8, 4096, 1024], P('dp', 'tensor')
- momentum_new: float32 [8, 4096, 1024], P('dp', 'tensor')
- master_new: float32 [8, 4096, 1024], P('dp', 'tensor')
- small_grad: float32 [12288], P(('dp', 'tensor'))
- small_second_new: float32 [12288], P(('dp', 'tensor'))
- small_new: float32 [12288], P(('dp', 'tensor'))
The draws below stay inside these ranges and needn't reach their ends.
Inputs may be any that keep to these rules, and one draw needn't show every extreme that they name: For each tensor index t, owners[t, 0..3] name the devices of dp owning the query-key-value, output, feed-forward-in and feed-forward-out matrices of shard t; the four are different. Slots of devices that own nothing, and entries of a slot outside its matrix's shape, are not read. `small_master`: entries 0 to 1023 and 5120 to 6143 are LayerNorm gains, the rest biases.
All inputs are finite; a program needn't handle non-finite values.
Results may differ from the reference program's by a relative error of at most 0.017.
Values may be sent and summed in bfloat16 or wider, within the bound.
No kernel may reach another device: no remote copies, remote signals or barrier semaphores. Data moves between devices by JAX's collectives and lax.ppermute only.
A program may use at most 192 MiB of HBM per device.

```python
import math
import jax
import jax.numpy as jnp
from jax import lax

D = 1024
HEADS = 16
FF = 4096
SEQ = 1024
SEQS_DEV = 2
NS_STEPS = 5
STEP = 10
HEAD_DIM = 64
TOKENS = 16384
SMALL = 12288
N_DP = 8
N_TENSOR = 4


def draw_owners(key, part):
    key = jax.random.fold_in(key, 7)
    table_rows = [jax.random.permutation(jax.random.fold_in(key, tensor_idx), N_DP)[0:4] for tensor_idx in range(N_TENSOR)]
    return jnp.stack(table_rows).astype(jnp.int32)


def draw_small_master(key, part):
    key = jax.random.fold_in(key, 11)
    total = 8 * D + FF
    positions = jnp.arange(total)
    gain_pos = (positions < D) | (positions >= 5 * D) & (positions < 6 * D)
    noise = jnp.clip(jax.random.normal(key, (total,), jnp.float32), -4.0, 4.0)
    return jnp.where(gain_pos, 1.0 + 0.1 * noise, 0.2 * noise).astype(jnp.float32)


def levels(key, shape, shards, low, largest):
    gain = 1.0
    for position, shards_of in shards:
        steps = jax.random.uniform(jax.random.fold_in(jax.random.fold_in(key, 6), position), (shards_of,), jnp.float32, low / len(shards), largest / len(shards))
        gain = gain * jnp.repeat(jnp.exp(steps), shape[position] // shards_of).reshape((-1,) + (1,) * (len(shape) - 1 - position))
    return gain


def bell_draw(own_key, dims, scale, reach, shards=(), held_as=jnp.bfloat16):
    entries = jax.random.normal(own_key, dims, jnp.float32) * scale
    if len(shards) > 0:
        entries = levels(own_key, dims, shards, -0.22, 0.18) * entries
    return jnp.clip(entries, min=-reach, max=reach).astype(held_as)


def setup_inputs(seed: int = 0) -> dict:
    splits = jax.random.split(jax.random.key(seed), 9)
    return {
        "inputs": bell_draw(splits[0], (TOKENS, D), 1.0, 6.0, ((0, 32),)),
        "out_grad": bell_draw(splits[1], (TOKENS, D), 1.0, 6.0, ((0, 32),)),
        "owners": draw_owners(jax.random.fold_in(splits[8], 71), 0),
        "master_slots": bell_draw(splits[3], (N_DP, N_TENSOR * D, D), D ** -0.5, 0.1875, ((0, 8), (1, 4)), jnp.float32),
        "momentum_slots": bell_draw(splits[4], (N_DP, N_TENSOR * D, D), (0.3 * (SEQS_DEV * SEQ * N_DP) ** 0.5), 224.0, ((0, 8), (1, 4)), jnp.float32),
        "small_master": draw_small_master(jax.random.fold_in(splits[8], 71), 0),
        "small_first": bell_draw(splits[6], (SMALL,), (0.1 * (SEQS_DEV * SEQ * N_DP) ** 0.5), 80.0, ((0, 32),), jnp.float32),
        "small_second": jnp.clip(jnp.exp(math.log(2457.6) - 2.3025852 * jax.random.uniform(splits[7], (SMALL,), jnp.float32) ** levels(splits[7], (SMALL,), ((0, 32),), -0.2, 0.2)), 245.76, 2457.6),
    }


@jax.custom_vjp
def low(v):
    return lax.optimization_barrier(v.astype(jnp.bfloat16)).astype(jnp.float32)

@jax.custom_vjp
def low_back(v):
    return v

def low_keep(v):
    return (low(v), None)

def low_pass(kept, grad):
    return (grad,)

def back_keep(v):
    return (v, None)

def back_low(kept, grad):
    return (low(grad),)
low.defvjp(low_keep, low_pass)
low_back.defvjp(back_keep, back_low)
ln_eps = 1e-05
mom_decay = 0.95
ns_a = 3.4445
ns_b = -4.775
ns_c = 2.0315
muon_rate = 0.5
muon_decay = 0.01
beta_one = 0.9
beta_two = 0.95
adam_rate = 0.2
adam_eps = 1e-08
masked_score = -1e+30
highest = lax.Precision.HIGHEST

def matmul(left, right):
    return jnp.dot(left, right, precision=highest, preferred_element_type=jnp.float32)

def layer_norm(values, gain_vec, shift_vec):
    row_mean = lax.optimization_barrier(jnp.mean(values, axis=-1, keepdims=True))
    centred = values - row_mean
    spread = lax.optimization_barrier(jnp.mean(centred * centred, axis=-1, keepdims=True))
    return centred * lax.rsqrt(spread + ln_eps) * gain_vec + shift_vec

def attend_triple(triple):
    queries, keys_in, values_in = triple
    scores = jnp.einsum('qhd,khd->hqk', queries, keys_in, precision=highest) * HEAD_DIM ** (-0.5)
    scores = low_back(scores)
    length = queries.shape[0]
    causal = jnp.arange(length)[:, None] >= jnp.arange(length)[None, :]
    scores = jnp.where(causal[None], scores, masked_score)
    row_top = lax.optimization_barrier(jnp.max(scores, axis=-1, keepdims=True))
    shifted = jnp.exp(scores - row_top)
    attn_probs = low(shifted / lax.optimization_barrier(jnp.sum(shifted, axis=-1, keepdims=True)))
    return jnp.einsum('hqk,khd->qhd', attn_probs, values_in, precision=highest)

def forward(values_in, w_query, w_key, w_value, w_out, w_fc, w_proj, small_vec):
    gain_one = small_vec[0:D]
    shift_one = small_vec[D:2 * D]
    bias_query = small_vec[2 * D:3 * D]
    bias_value = small_vec[3 * D:4 * D]
    bias_out = small_vec[4 * D:5 * D]
    gain_two = small_vec[5 * D:6 * D]
    shift_two = small_vec[6 * D:7 * D]
    bias_fc = small_vec[7 * D:7 * D + FF]
    bias_proj = small_vec[7 * D + FF:]
    normed = low(layer_norm(values_in, gain_one, shift_one))
    queries = low_back(low(matmul(normed, w_query) + bias_query))
    keys_all = low_back(low(matmul(normed, w_key)))
    values_all = low_back(low(matmul(normed, w_value) + bias_value))
    seq_count = values_in.shape[0] // SEQ
    four_dims = (seq_count, SEQ, HEADS, HEAD_DIM)
    attended = lax.map(jax.checkpoint(attend_triple), (queries.reshape(four_dims), keys_all.reshape(four_dims), values_all.reshape(four_dims)))
    attended = low_back(low(attended.reshape(values_in.shape[0], D)))
    middle = values_in + low_back(matmul(attended, w_out)) + bias_out
    normed_two = low(layer_norm(middle, gain_two, shift_two))
    hidden_pre = low_back(matmul(normed_two, w_fc) + bias_fc)
    hidden_act = low(jax.nn.gelu(hidden_pre, approximate=True))
    return middle + low_back(matmul(hidden_act, w_proj)) + bias_proj

def newton_schulz(matrix):
    scaled = matrix / (jnp.sqrt(jnp.sum(matrix * matrix)) + 1e-07)
    iterate = scaled.astype(jnp.bfloat16)
    for ns_turn in range(NS_STEPS):
        gram_mat = jnp.einsum('ij,kj->ik', iterate, iterate, preferred_element_type=jnp.float32).astype(jnp.bfloat16)
        square = jnp.dot(gram_mat, gram_mat, preferred_element_type=jnp.float32)
        poly_mat = (ns_b * gram_mat.astype(jnp.float32) + ns_c * square).astype(jnp.bfloat16)
        iterate = (ns_a * iterate.astype(jnp.float32) + jnp.dot(poly_mat, iterate, preferred_element_type=jnp.float32)).astype(jnp.bfloat16)
    return iterate.astype(jnp.float32)

def muon_update(grad_slot, mom_slot, master_slot, valid):
    momentum = valid * (mom_decay * mom_slot + grad_slot)
    ortho = newton_schulz(momentum)
    fresh = valid * (master_slot * (1.0 - muon_rate * muon_decay) - muon_rate * ortho)
    return (grad_slot * valid, momentum, fresh)

def take_slot(slots, owner, tensor_idx):
    return lax.dynamic_slice(slots, (owner, jnp.int32(tensor_idx * D), jnp.int32(0)), (1, D, D))[0]

def put_slot(slots, content, owner, tensor_idx):
    return lax.dynamic_update_slice(slots, content[None], (owner, jnp.int32(tensor_idx * D), jnp.int32(0)))

def rounded(matrix):
    return matrix.astype(jnp.bfloat16).astype(jnp.float32)

def reference(inputs, out_grad, owners, master_slots, momentum_slots, small_master, small_first, small_second):
    head_width = D // N_TENSOR
    ff_width = FF // N_TENSOR
    slots = [[take_slot(master_slots, owners[tensor_idx, kind], tensor_idx) for kind in range(4)] for tensor_idx in range(N_TENSOR)]
    w_query = rounded(jnp.concatenate([slots[tensor_idx][0][:, 0:head_width] for tensor_idx in range(N_TENSOR)], axis=1))
    w_key = rounded(jnp.concatenate([slots[tensor_idx][0][:, head_width:2 * head_width] for tensor_idx in range(N_TENSOR)], axis=1))
    w_value = rounded(jnp.concatenate([slots[tensor_idx][0][:, 2 * head_width:3 * head_width] for tensor_idx in range(N_TENSOR)], axis=1))
    w_out = rounded(jnp.concatenate([slots[tensor_idx][1][0:head_width, :] for tensor_idx in range(N_TENSOR)], axis=0))
    w_fc = rounded(jnp.concatenate([slots[tensor_idx][2][:, 0:ff_width] for tensor_idx in range(N_TENSOR)], axis=1))
    w_proj = rounded(jnp.concatenate([slots[tensor_idx][3][0:ff_width, :] for tensor_idx in range(N_TENSOR)], axis=0))
    params = (w_query, w_key, w_value, w_out, w_fc, w_proj, small_master)
    total_seqs = TOKENS // SEQ
    per_batch = math.gcd(4, total_seqs)
    batch_count = total_seqs // per_batch
    inputs_f = inputs.astype(jnp.float32).reshape(batch_count, per_batch * SEQ, D)
    cotangent = out_grad.astype(jnp.float32).reshape(batch_count, per_batch * SEQ, D)

    def one_batch(carried, batch_pair):
        outputs, pullback = jax.vjp(forward, batch_pair[0], *params)
        gradients = pullback(batch_pair[1])
        carried = tuple((running + addend for running, addend in zip(carried, gradients[1:])))
        return (carried, (outputs.astype(jnp.bfloat16), gradients[0]))
    zero_init = tuple((jnp.zeros_like(member) for member in params))
    totals, (out_rows, in_grads) = lax.scan(one_batch, zero_init, (inputs_f, cotangent))
    block_out = out_rows.reshape(TOKENS, D)
    input_grad = in_grads.reshape(TOKENS, D)
    grad_query, grad_key, grad_value, grad_out, grad_fc, grad_proj, small_grad = totals
    first_new = beta_one * small_first + (1.0 - beta_one) * small_grad
    second_new = beta_two * small_second + (1.0 - beta_two) * small_grad * small_grad
    first_hat = first_new / (1.0 - beta_one ** STEP)
    second_hat = second_new / (1.0 - beta_two ** STEP)
    small_new = small_master - adam_rate * first_hat / (jnp.sqrt(second_hat) + adam_eps)
    col_ids = jnp.arange(D)
    mask_qkv = jnp.broadcast_to((col_ids < 3 * head_width)[None, :], (D, D)).astype(jnp.float32)
    mask_out = jnp.broadcast_to((col_ids < head_width)[:, None], (D, D)).astype(jnp.float32)
    full_mask = jnp.ones((D, D), jnp.float32)
    masks = (mask_qkv, mask_out, full_mask, full_mask)
    grad_slots = jnp.zeros_like(master_slots)
    momentum_new = jnp.zeros_like(master_slots)
    master_new = jnp.zeros_like(master_slots)
    for tensor_idx in range(N_TENSOR):
        low_col = tensor_idx * head_width
        high_col = low_col + head_width
        low_ff = tensor_idx * ff_width
        high_ff = low_ff + ff_width
        qkv_block = jnp.concatenate([grad_query[:, low_col:high_col], grad_key[:, low_col:high_col], grad_value[:, low_col:high_col]], axis=1)
        blocks = (jnp.pad(qkv_block, ((0, 0), (0, D - 3 * head_width))), jnp.pad(grad_out[low_col:high_col, :], ((0, D - head_width), (0, 0))), grad_fc[:, low_ff:high_ff], grad_proj[low_ff:high_ff, :])
        for kind in range(4):
            owner = owners[tensor_idx, kind]
            mom_old = take_slot(momentum_slots, owner, tensor_idx)
            grad_slot, mom_slot, fresh = muon_update(blocks[kind], mom_old, slots[tensor_idx][kind], masks[kind])
            grad_slots = put_slot(grad_slots, grad_slot, owner, tensor_idx)
            momentum_new = put_slot(momentum_new, mom_slot, owner, tensor_idx)
            master_new = put_slot(master_new, fresh, owner, tensor_idx)
    return (block_out, input_grad, grad_slots, momentum_new, master_new, small_grad, second_new, small_new)
```

```python
from functools import partial

import jax
import jax.numpy as jnp
from jax import lax
from jax.experimental import pallas as pl
from jax.experimental.pallas import tpu as pltpu
from jax.sharding import PartitionSpec as P

HEADS = 16
FF = 4096
SEQ = 1024
NS_STEPS = 5
STEP = 10
HEAD_DIM = 64

ln_eps = 1e-05
mom_decay = 0.95
ns_a = 3.4445
ns_b = -4.775
ns_c = 2.0315
muon_rate = 0.5
muon_decay = 0.01
beta_one = 0.9
beta_two = 0.95
adam_rate = 0.2
adam_eps = 1e-08
masked_score = -1e30
gelu_in = 0.7978845608028654
gelu_cube = 0.044715

CHUNKS = 2
TILE = 256
VMEM_GRANT = 48 * 1024 * 1024
BF16 = jnp.bfloat16
F32 = jnp.float32

NN = (((1,), (0,)), ((), ()))
NT = (((1,), (1,)), ((), ()))
TN = (((0,), (0,)), ((), ()))


def mm(left, right, dims=NN):
    return lax.dot_general(left, right, dims, preferred_element_type=F32)


def rows2(value):
    return value.reshape(-1, value.shape[-1])


def head_ids(shape):
    return lax.broadcasted_iota(jnp.int32, shape, 1) // HEAD_DIM


def causal_tile(tile):
    row = lax.broadcasted_iota(jnp.int32, (tile, tile), 0)
    col = lax.broadcasted_iota(jnp.int32, (tile, tile), 1)
    return row >= col


def attend_kernel(core_ref, q_ref, k_ref, v_ref, o_ref, lse_ref, *, subs, heads):
    core = core_ref[0]
    place = (core, 1 - core)
    width = q_ref.shape[-1]
    col_head = head_ids((TILE, width))
    lane = lax.broadcasted_iota(jnp.int32, (TILE, 128), 1)
    causal = causal_tile(TILE)
    per_half = k_ref.shape[2] // TILE
    for half in range(2):
        for at, sub in enumerate(subs):
            blk = per_half * half + sub
            rows = slice(at * TILE, (at + 1) * TILE)
            q_blk = q_ref[place[half], 0, rows, :]
            acc = jnp.zeros((TILE, width), F32)
            lse = jnp.zeros((TILE, 128), F32)
            for head in range(heads):
                q_one = jnp.where(col_head == head, q_blk, jnp.zeros_like(q_blk))
                scores = []
                for j in range(blk + 1):
                    cols = slice((j % per_half) * TILE, (j % per_half + 1) * TILE)
                    s = mm(q_one, k_ref[place[j // per_half], 0, cols, :], NT)
                    if j == blk:
                        s = jnp.where(causal, s, masked_score)
                    scores.append(s)
                top = scores[0]
                for s in scores[1:]:
                    top = jnp.maximum(top, s)
                top = jnp.max(top, axis=1, keepdims=True)
                total = jnp.zeros((TILE, TILE), F32)
                out = jnp.zeros((TILE, width), F32)
                for j in range(blk + 1):
                    cols = slice((j % per_half) * TILE, (j % per_half + 1) * TILE)
                    p = jnp.exp(scores[j] - top)
                    total = total + p
                    out = out + mm(p.astype(BF16), v_ref[place[j // per_half], 0, cols, :])
                total = jnp.sum(total, axis=1, keepdims=True)
                acc = jnp.where(col_head == head, out * (1.0 / total), acc)
                lse = jnp.where(lane == head, top + jnp.log(total), lse)
            o_ref[place[half], 0, rows, :] = acc.astype(BF16)
            lse_ref[place[half], 0, rows, :] = lse


def attend(core, qkv, chunk, chunks):
    _, seqs, rows, triple = qkv.shape
    width = triple // 3
    part = rows // chunks
    per = part // TILE
    subs = tuple(range(chunk * per, (chunk + 1) * per))
    return pl.pallas_call(
        partial(attend_kernel, subs=subs, heads=width // HEAD_DIM),
        grid_spec=pltpu.PrefetchScalarGridSpec(
            num_scalar_prefetch=1,
            grid=(seqs,),
            in_specs=[
                pl.BlockSpec((2, 1, part, width), lambda s, c: (0, s, chunk, 0)),
                pl.BlockSpec((2, 1, rows, width), lambda s, c: (0, s, 0, 1)),
                pl.BlockSpec((2, 1, rows, width), lambda s, c: (0, s, 0, 2)),
            ],
            out_specs=[
                pl.BlockSpec((2, 1, part, width), lambda s, c: (0, s, 0, 0)),
                pl.BlockSpec((2, 1, part, 128), lambda s, c: (0, s, 0, 0)),
            ],
        ),
        out_shape=[
            jax.ShapeDtypeStruct((2, seqs, part, width), BF16),
            jax.ShapeDtypeStruct((2, seqs, part, 128), F32),
        ],
        compiler_params=pltpu.CompilerParams(vmem_limit_bytes=VMEM_GRANT),
        cost_estimate=pl.CostEstimate(
            flops=10 * 10**9 // chunks, bytes_accessed=6 * 10**6, transcendentals=0
        ),
    )(core, qkv, qkv, qkv)


def attend_back_kernel(
    core_ref, q_ref, k_ref, v_ref, *refs, heads, chunks
):
    o_refs = refs[0:chunks]
    lse_refs = refs[chunks : 2 * chunks]
    do_ref = refs[2 * chunks]
    out_ref, dk_acc, dv_acc = refs[2 * chunks + 1 :]
    core = core_ref[0]
    place = (core, 1 - core)
    width = q_ref.shape[-1]
    col_head = head_ids((TILE, width))
    causal = causal_tile(TILE)
    per_half = k_ref.shape[2] // TILE
    per_chunk = per_half // chunks
    dk_acc[...] = jnp.zeros_like(dk_acc)
    dv_acc[...] = jnp.zeros_like(dv_acc)
    for half in range(2):
        for sub in range(per_half):
            blk = per_half * half + sub
            rows = slice(sub * TILE, (sub + 1) * TILE)
            inner = slice((sub % per_chunk) * TILE, (sub % per_chunk + 1) * TILE)
            q_blk = q_ref[place[half], 0, rows, :]
            do_blk = do_ref[place[half], 0, rows, :]
            o_blk = o_refs[sub // per_chunk][place[half], 0, inner, :]
            lse_blk = lse_refs[sub // per_chunk][place[half], 0, inner, :]
            overlap = do_blk.astype(F32) * o_blk.astype(F32)
            q_all, do_all, lse_all, delta_all = [], [], [], []
            for head in range(heads):
                mine = col_head == head
                q_all.append(jnp.where(mine, q_blk, jnp.zeros_like(q_blk)))
                do_all.append(jnp.where(mine, do_blk, jnp.zeros_like(do_blk)))
                lse_all.append(lse_blk[:, head : head + 1])
                delta_all.append(jnp.sum(jnp.where(mine, overlap, 0.0), axis=1, keepdims=True))
            q_cat = jnp.concatenate(q_all, axis=0)
            do_cat = jnp.concatenate(do_all, axis=0)
            dq = [jnp.zeros((TILE, width), F32) for _ in range(heads)]
            for j in range(blk + 1):
                cols = slice((j % per_half) * TILE, (j % per_half + 1) * TILE)
                k_blk = k_ref[place[j // per_half], 0, cols, :]
                v_blk = v_ref[place[j // per_half], 0, cols, :]
                p_all, ds_all = [], []
                for head in range(heads):
                    p = jnp.exp(mm(q_all[head], k_blk, NT) - lse_all[head])
                    if j == blk:
                        p = jnp.where(causal, p, 0.0)
                    dp = mm(do_all[head], v_blk, NT)
                    ds = (p * (dp - delta_all[head])).astype(BF16)
                    dq[head] = dq[head] + mm(ds, k_blk)
                    p_all.append(p.astype(BF16))
                    ds_all.append(ds)
                dk_acc[j] += mm(jnp.concatenate(ds_all, axis=0), q_cat, TN)
                dv_acc[j] += mm(jnp.concatenate(p_all, axis=0), do_cat, TN)
            total = dq[0]
            for head in range(1, heads):
                total = jnp.where(col_head == head, dq[head], total)
            out_ref[place[half], 0, rows, 0:width] = (total * HEAD_DIM**-0.5).astype(BF16)
    for j in range(2 * per_half):
        rows = slice((j % per_half) * TILE, (j % per_half + 1) * TILE)
        out_ref[place[j // per_half], 0, rows, width : 2 * width] = dk_acc[j].astype(BF16)
        out_ref[place[j // per_half], 0, rows, 2 * width :] = dv_acc[j].astype(BF16)


def attend_back(core, qkv, outs, lses, back):
    _, seqs, rows, triple = qkv.shape
    width = triple // 3
    chunks = len(outs)
    part = rows // chunks

    def block(size, cols, at):
        return pl.BlockSpec((2, 1, size, cols), lambda s, c: (0, s, 0, at))

    return pl.pallas_call(
        partial(attend_back_kernel, heads=width // HEAD_DIM, chunks=chunks),
        grid_spec=pltpu.PrefetchScalarGridSpec(
            num_scalar_prefetch=1,
            grid=(seqs,),
            in_specs=[block(rows, width, 0), block(rows, width, 1), block(rows, width, 2)]
            + [block(part, width, 0)] * chunks
            + [block(part, 128, 0)] * chunks
            + [block(rows, width, 0)],
            out_specs=block(rows, triple, 0),
            scratch_shapes=[pltpu.VMEM((2 * rows // TILE, TILE, width), F32)] * 2,
        ),
        out_shape=jax.ShapeDtypeStruct(qkv.shape, BF16),
        compiler_params=pltpu.CompilerParams(vmem_limit_bytes=VMEM_GRANT),
        cost_estimate=pl.CostEstimate(
            flops=25 * 10**9, bytes_accessed=12 * 10**6, transcendentals=0
        ),
    )(core, qkv, qkv, qkv, *outs, *lses, back)


def schulz_kernel(x_ref, o_ref, x_buf, gram, poly):
    size = x_ref.shape[0]
    tiles = size // TILE
    x_buf[0] = x_ref[...]

    def one_turn(turn, carry):
        now = lax.rem(turn, 2)
        later = 1 - now

        def gram_rows(r, c):
            rows = pl.ds(pl.multiple_of(r * TILE, TILE), TILE)
            gram[rows, :] = mm(x_buf[now, rows, :], x_buf[now], NT).astype(BF16)
            return c

        lax.fori_loop(0, tiles, gram_rows, 0)

        def poly_rows(r, c):
            rows = pl.ds(pl.multiple_of(r * TILE, TILE), TILE)
            mine = gram[rows, :]
            poly[rows, :] = (ns_b * mine.astype(F32) + ns_c * mm(mine, gram[...])).astype(BF16)
            return c

        lax.fori_loop(0, tiles, poly_rows, 0)

        def next_rows(r, c):
            rows = pl.ds(pl.multiple_of(r * TILE, TILE), TILE)
            x_buf[later, rows, :] = (
                ns_a * x_buf[now, rows, :].astype(F32) + mm(poly[rows, :], x_buf[now])
            ).astype(BF16)
            return c

        lax.fori_loop(0, tiles, next_rows, 0)
        return carry

    lax.fori_loop(0, NS_STEPS, one_turn, 0)
    o_ref[...] = x_buf[NS_STEPS % 2]


def newton_schulz(start):
    size = start.shape[0]
    return pl.pallas_call(
        schulz_kernel,
        in_specs=[pl.BlockSpec(memory_space=pltpu.VMEM)],
        out_specs=pl.BlockSpec(memory_space=pltpu.VMEM),
        out_shape=jax.ShapeDtypeStruct(start.shape, BF16),
        scratch_shapes=[
            pltpu.VMEM((2, size, size), BF16),
            pltpu.VMEM((size, size), BF16),
            pltpu.VMEM((size, size), BF16),
        ],
        compiler_params=pltpu.CompilerParams(vmem_limit_bytes=VMEM_GRANT),
        cost_estimate=pl.CostEstimate(
            flops=6 * NS_STEPS * size**3, bytes_accessed=4 * size * size, transcendentals=0
        ),
    )(start)


def swap(value, bit):
    count = lax.axis_size("tensor")
    return lax.ppermute(value, "tensor", [(i, i ^ bit) for i in range(count)])


def gather_pair(value):
    mine = jnp.stack([value, swap(value, 2)])
    return mine, swap(mine, 1)


def scatter_sum(keep_in, send_in, weight, dims):
    shape = keep_in.shape[:-1] + (-1,)
    send = mm(rows2(send_in), weight, dims).astype(BF16).reshape(shape)
    arrived = swap(send, 1)
    keep = mm(rows2(keep_in), weight, dims).reshape(shape)
    part = keep + arrived.astype(F32)
    far = swap(part[1].astype(BF16), 2)
    return part[0] + far.astype(F32)


def axis_bits(name):
    count = lax.axis_size(name)
    bits = []
    bit = 1
    while bit < count:
        bits.append(bit)
        bit *= 2
    return bits


def small_gather(value):
    piece = value.reshape(1, -1)
    for name in ("tensor", "dp"):
        index = lax.axis_index(name)
        count = lax.axis_size(name)
        for bit in axis_bits(name):
            other = lax.ppermute(piece, name, [(i, i ^ bit) for i in range(count)])
            upper = (index & bit) != 0
            piece = jnp.where(
                upper,
                jnp.concatenate([other, piece], axis=0),
                jnp.concatenate([piece, other], axis=0),
            )
    return piece.reshape(-1)


def small_scatter(value):
    for name in ("dp", "tensor"):
        index = lax.axis_index(name)
        count = lax.axis_size(name)
        for bit in reversed(axis_bits(name)):
            low, high = jnp.split(value, 2)
            upper = (index & bit) != 0
            give = jnp.where(upper, low, high)
            keep = jnp.where(upper, high, low)
            value = keep + lax.ppermute(give, name, [(i, i ^ bit) for i in range(count)])
    return value


def norm_parts(values):
    centred = values - jnp.mean(values, axis=-1, keepdims=True)
    spread = jnp.mean(centred * centred, axis=-1, keepdims=True)
    scale = lax.rsqrt(spread + ln_eps)
    return centred * scale, scale


def norm_back(unit, scale, gain_vec, grad):
    inner = grad * gain_vec
    return scale * (
        inner
        - jnp.mean(inner, axis=-1, keepdims=True)
        - unit * jnp.mean(inner * unit, axis=-1, keepdims=True)
    )


def per_device(
    inputs, out_grad, owners, master_slots, momentum_slots, small_master, small_first, small_second
):
    rows_dev, width = inputs.shape
    tensor_count = lax.axis_size("tensor")
    data_count = lax.axis_size("dp")
    tensor_idx = lax.axis_index("tensor")
    data_idx = lax.axis_index("dp")
    head_width = width // tensor_count
    ff_width = FF // tensor_count
    share = width // data_count
    share_out = head_width // data_count
    core = jnp.reshape(tensor_idx & 1, (1,)).astype(jnp.int32)
    owner_row = lax.dynamic_index_in_dim(owners, tensor_idx, 0, keepdims=False)
    owned = owner_row == data_idx
    slot_value = master_slots[0]

    slot_low = slot_value.astype(BF16)
    offer_out = jnp.pad(
        slot_low[:head_width].reshape(data_count, share_out, width),
        ((0, 0), (0, share - share_out), (0, 0)),
    )
    offer = jnp.where(owned[1], offer_out, slot_low.reshape(data_count, share, width))
    shares = lax.all_to_all(offer, "dp", 0, 0)

    def share_of(kind):
        return lax.dynamic_index_in_dim(shares, owner_row[kind], 0, keepdims=False)

    def gather_rows(value):
        return lax.all_gather(value, "dp", axis=0, tiled=True)

    w_qkv = gather_rows(share_of(0)[:, : 3 * head_width])
    w_out = gather_rows(share_of(1)[:share_out])
    w_proj = gather_rows(share_of(3))
    w_fc = gather_rows(share_of(2))

    params = small_gather(small_master)

    def own_slice(start, size):
        return lax.dynamic_slice_in_dim(params, start + tensor_idx * size, size, 0)

    gain_one = params[0:width]
    shift_one = params[width : 2 * width]
    bias_query = own_slice(2 * width, head_width)
    bias_value = own_slice(3 * width, head_width)
    bias_out = params[4 * width : 5 * width]
    gain_two = params[5 * width : 6 * width]
    shift_two = params[6 * width : 7 * width]
    bias_fc = own_slice(7 * width, ff_width)
    bias_proj = params[7 * width + FF :]

    rows_in = inputs.astype(F32)
    unit_one, scale_one = norm_parts(rows_in)
    normed = (unit_one * gain_one + shift_one).astype(BF16)
    normed_all = jnp.stack(gather_pair(normed))
    dy_pair = gather_pair(out_grad)
    bias_qkv = jnp.concatenate([bias_query, jnp.zeros_like(bias_query), bias_value])
    scale_qkv = jnp.where(jnp.arange(3 * head_width) < head_width, HEAD_DIM**-0.5, 1.0)
    qkv = ((mm(rows2(normed_all), w_qkv) + bias_qkv) * scale_qkv).astype(BF16)
    qkv = qkv.reshape(2, 2, rows_dev, 3 * head_width)
    back_act = [mm(rows2(dy), w_proj, NT).astype(BF16) for dy in dy_pair]

    part = rows_dev // CHUNKS
    mixed, log_sums = [], []
    for chunk in range(CHUNKS):
        mixed_one, sums_one = attend(core, qkv, chunk, CHUNKS)
        mixed.append(mixed_one)
        log_sums.append(sums_one)
    middles, branches, grad_proj, grad_fc, fc_bias_grad = [], [], 0.0, 0.0, 0.0
    back_normed_two, mine_two = [], []
    for chunk in range(CHUNKS):
        rows = slice(chunk * part, (chunk + 1) * part)
        branch = scatter_sum(mixed[chunk][0], mixed[chunk][1], w_out, NN)
        middle = rows_in[rows] + branch + bias_out
        unit_two, scale_two = norm_parts(middle)
        normed_two = (unit_two * gain_two + shift_two).astype(BF16)
        pair = gather_pair(normed_two)
        acts, backs = [], []
        for side in range(2):
            hidden = mm(rows2(pair[side]), w_fc) + bias_fc
            bent = jnp.tanh(gelu_in * (hidden + gelu_cube * hidden * hidden * hidden))
            act = (0.5 * hidden * (1.0 + bent)).astype(BF16)
            slope = 0.5 * (1.0 + bent) + 0.5 * hidden * (1.0 - bent * bent) * (
                gelu_in * (1.0 + 3.0 * gelu_cube * hidden * hidden)
            )
            dact = back_act[side].reshape(2, rows_dev, ff_width)[:, rows]
            back = (rows2(dact).astype(F32) * slope).astype(BF16)
            fc_bias_grad = fc_bias_grad + jnp.sum(back, axis=0, dtype=F32)
            acts.append(act)
            backs.append(back)
        shape = (2, part, ff_width)
        back_normed_two.append(
            scatter_sum(backs[0].reshape(shape), backs[1].reshape(shape), w_fc, NT)
        )
        branches.append(scatter_sum(acts[0].reshape(shape), acts[1].reshape(shape), w_proj, NN))
        for side in range(2):
            dy = dy_pair[side][:, rows]
            grad_proj = grad_proj + mm(acts[side], rows2(dy), TN)
            grad_fc = grad_fc + mm(rows2(pair[side]), backs[side], TN)
        middles.append(middle)
        mine_two.append((unit_two, scale_two))
    middle = jnp.concatenate(middles)
    block_out = (middle + jnp.concatenate(branches) + bias_proj).astype(BF16)

    def scatter_grad(value):
        return lax.psum_scatter(value.astype(BF16), "dp", scatter_dimension=0, tiled=True)

    share_proj = scatter_grad(grad_proj)
    share_fc = scatter_grad(grad_fc)

    back_middles, mid_pairs, gain_two_grad, shift_two_grad = [], [], 0.0, 0.0
    for chunk in range(CHUNKS):
        rows = slice(chunk * part, (chunk + 1) * part)
        unit_two, scale_two = mine_two[chunk]
        grad = back_normed_two[chunk]
        back_middle = out_grad[rows].astype(F32) + norm_back(unit_two, scale_two, gain_two, grad)
        gain_two_grad = gain_two_grad + jnp.sum(grad * unit_two, axis=0)
        shift_two_grad = shift_two_grad + jnp.sum(grad, axis=0)
        mid_pairs.append(gather_pair(back_middle.astype(BF16)))
        back_middles.append(back_middle)
    back_middle = jnp.concatenate(back_middles)
    proj_bias_grad = jnp.sum(out_grad, axis=0, dtype=F32)
    out_bias_grad = jnp.sum(back_middle, axis=0)
    back_mixed, grad_out = [], 0.0
    for side in range(2):
        sides = []
        for chunk in range(CHUNKS):
            mid = rows2(mid_pairs[chunk][side])
            sides.append(mm(mid, w_out, NT).astype(BF16).reshape(2, part, head_width))
            grad_out = grad_out + mm(rows2(mixed[chunk][side]), mid, TN)
        back_mixed.append(jnp.concatenate(sides, axis=1))
    back_qkv = attend_back(core, qkv, mixed, log_sums, jnp.stack(back_mixed))
    grad_qkv = mm(rows2(normed_all), rows2(back_qkv), TN)
    qkv_bias_grad = jnp.sum(back_qkv, axis=(0, 1, 2), dtype=F32)

    share_out_grad = scatter_grad(grad_out)
    share_qkv = scatter_grad(grad_qkv)
    back_normed = scatter_sum(back_qkv[0], back_qkv[1], w_qkv, NT)
    input_grad = back_middle + norm_back(unit_one, scale_one, gain_one, back_normed)
    gain_one_grad = jnp.sum(back_normed * unit_one, axis=0)
    shift_one_grad = jnp.sum(back_normed, axis=0)

    bundle = jnp.zeros((data_count, share, width), BF16)
    pieces = (
        jnp.pad(share_qkv, ((0, 0), (0, width - 3 * head_width))),
        jnp.pad(share_out_grad, ((0, share - share_out), (0, 0))),
        share_fc,
        share_proj,
    )
    for kind in range(4):
        bundle = lax.dynamic_update_index_in_dim(bundle, pieces[kind], owner_row[kind], 0)
    landed = lax.all_to_all(bundle, "dp", 0, 0)
    landed_out = jnp.pad(
        landed[:, :share_out].reshape(head_width, width), ((0, width - head_width), (0, 0))
    )
    chosen = jnp.where(owned[1], landed_out, landed.reshape(width, width)).astype(F32)

    full_grad = jnp.concatenate(
        [
            gain_one_grad,
            shift_one_grad,
            jnp.zeros((2 * width,), F32),
            out_bias_grad,
            gain_two_grad,
            shift_two_grad,
            jnp.zeros((FF,), F32),
            proj_bias_grad,
        ]
    )
    for grad, start, size in (
        (qkv_bias_grad[:head_width], 2 * width, head_width),
        (qkv_bias_grad[2 * head_width :], 3 * width, head_width),
        (fc_bias_grad, 7 * width, ff_width),
    ):
        full_grad = lax.dynamic_update_slice_in_dim(full_grad, grad, start + tensor_idx * size, 0)
    small_grad = small_scatter(full_grad)
    first_new = beta_one * small_first + (1.0 - beta_one) * small_grad
    second_new = beta_two * small_second + (1.0 - beta_two) * small_grad * small_grad
    first_hat = first_new / (1.0 - beta_one**STEP)
    second_hat = second_new / (1.0 - beta_two**STEP)
    small_new = small_master - adam_rate * first_hat / (jnp.sqrt(second_hat) + adam_eps)

    any_owned = jnp.any(owned)
    row_limit = jnp.where(owned[1], head_width, jnp.where(any_owned, width, 0))
    col_limit = jnp.where(owned[0], 3 * head_width, width)
    row_ids = lax.broadcasted_iota(jnp.int32, (width, width), 0)
    col_ids = lax.broadcasted_iota(jnp.int32, (width, width), 1)
    valid = (row_ids < row_limit) & (col_ids < col_limit)
    mom_slot = jnp.where(valid, mom_decay * momentum_slots[0] + chosen, 0.0)

    def run_owner(packed):
        momentum, master, keep = packed
        start = (momentum / (jnp.sqrt(jnp.sum(momentum * momentum)) + 1e-07)).astype(BF16)
        ortho = newton_schulz(start).astype(F32)
        return jnp.where(keep, master * (1.0 - muon_rate * muon_decay) - muon_rate * ortho, 0.0)

    def skip_owner(packed):
        return jnp.zeros_like(packed[1])

    fresh_slot = lax.cond(any_owned, run_owner, skip_owner, (mom_slot, slot_value, valid))
    return (
        block_out,
        input_grad,
        chosen[None],
        mom_slot[None],
        fresh_slot[None],
        small_grad,
        second_new,
        small_new,
    )


def solution(mesh):
    return jax.shard_map(
        per_device,
        mesh=mesh,
        in_specs=(
            P(("dp", "tensor"), None),
            P(("dp", "tensor"), None),
            P(),
            P("dp", "tensor", None),
            P("dp", "tensor", None),
            P(("dp", "tensor")),
            P(("dp", "tensor")),
            P(("dp", "tensor")),
        ),
        out_specs=(
            P(("dp", "tensor"), None),
            P(("dp", "tensor"), None),
            P("dp", "tensor", None),
            P("dp", "tensor", None),
            P("dp", "tensor", None),
            P(("dp", "tensor")),
            P(("dp", "tensor")),
            P(("dp", "tensor")),
        ),
        check_vma=False,
    )
```

```python
from functools import partial

import jax
import jax.numpy as jnp
from jax import lax
from jax.experimental import pallas as pl
from jax.experimental.pallas import tpu as pltpu
from jax.sharding import PartitionSpec as P

HEADS = 16
FF = 4096
SEQ = 1024
NS_STEPS = 5
STEP = 10
HEAD_DIM = 64

ln_eps = 1e-05
mom_decay = 0.95
ns_a = 3.4445
ns_b = -4.775
ns_c = 2.0315
muon_rate = 0.5
muon_decay = 0.01
beta_one = 0.9
beta_two = 0.95
adam_rate = 0.2
adam_eps = 1e-08
masked_score = -1e30
gelu_in = 0.7978845608028654
gelu_cube = 0.044715

CHUNKS = 2
TILE = 256
VMEM_GRANT = 48 * 1024 * 1024
BF16 = jnp.bfloat16
F32 = jnp.float32

NN = (((1,), (0,)), ((), ()))
NT = (((1,), (1,)), ((), ()))
TN = (((0,), (0,)), ((), ()))


def mm(left, right, dims=NN):
    return lax.dot_general(left, right, dims, preferred_element_type=F32)


def rows2(value):
    return value.reshape(-1, value.shape[-1])


def head_ids(shape):
    return lax.broadcasted_iota(jnp.int32, shape, 1) // HEAD_DIM


def causal_tile(tile):
    row = lax.broadcasted_iota(jnp.int32, (tile, tile), 0)
    col = lax.broadcasted_iota(jnp.int32, (tile, tile), 1)
    return row >= col


def attend_kernel(core_ref, q_ref, k_ref, v_ref, o_ref, lse_ref, *, subs, heads):
    core = core_ref[0]
    place = (core, 1 - core)
    width = q_ref.shape[-1]
    col_head = head_ids((TILE, width))
    lane = lax.broadcasted_iota(jnp.int32, (TILE, 128), 1)
    causal = causal_tile(TILE)
    per_half = k_ref.shape[2] // TILE
    for half in range(2):
        for at, sub in enumerate(subs):
            blk = per_half * half + sub
            rows = slice(at * TILE, (at + 1) * TILE)
            q_blk = q_ref[place[half], 0, rows, :]
            acc = jnp.zeros((TILE, width), F32)
            lse = jnp.zeros((TILE, 128), F32)
            for head in range(heads):
                q_one = jnp.where(col_head == head, q_blk, jnp.zeros_like(q_blk))
                scores = []
                for j in range(blk + 1):
                    cols = slice((j % per_half) * TILE, (j % per_half + 1) * TILE)
                    s = mm(q_one, k_ref[place[j // per_half], 0, cols, :], NT)
                    if j == blk:
                        s = jnp.where(causal, s, masked_score)
                    scores.append(s)
                top = scores[0]
                for s in scores[1:]:
                    top = jnp.maximum(top, s)
                top = jnp.max(top, axis=1, keepdims=True)
                total = jnp.zeros((TILE, TILE), F32)
                out = jnp.zeros((TILE, width), F32)
                for j in range(blk + 1):
                    cols = slice((j % per_half) * TILE, (j % per_half + 1) * TILE)
                    p = jnp.exp(scores[j] - top)
                    total = total + p
                    out = out + mm(p.astype(BF16), v_ref[place[j // per_half], 0, cols, :])
                total = jnp.sum(total, axis=1, keepdims=True)
                acc = jnp.where(col_head == head, out * (1.0 / total), acc)
                lse = jnp.where(lane == head, top + jnp.log(total), lse)
            o_ref[place[half], 0, rows, :] = acc.astype(BF16)
            lse_ref[place[half], 0, rows, :] = lse


def attend(core, qkv, chunk, chunks):
    _, seqs, rows, triple = qkv.shape
    width = triple // 3
    part = rows // chunks
    per = part // TILE
    subs = tuple(range(chunk * per, (chunk + 1) * per))
    return pl.pallas_call(
        partial(attend_kernel, subs=subs, heads=width // HEAD_DIM),
        grid_spec=pltpu.PrefetchScalarGridSpec(
            num_scalar_prefetch=1,
            grid=(seqs,),
            in_specs=[
                pl.BlockSpec((2, 1, part, width), lambda s, c: (0, s, chunk, 0)),
                pl.BlockSpec((2, 1, rows, width), lambda s, c: (0, s, 0, 1)),
                pl.BlockSpec((2, 1, rows, width), lambda s, c: (0, s, 0, 2)),
            ],
            out_specs=[
                pl.BlockSpec((2, 1, part, width), lambda s, c: (0, s, 0, 0)),
                pl.BlockSpec((2, 1, part, 128), lambda s, c: (0, s, 0, 0)),
            ],
        ),
        out_shape=[
            jax.ShapeDtypeStruct((2, seqs, part, width), BF16),
            jax.ShapeDtypeStruct((2, seqs, part, 128), F32),
        ],
        compiler_params=pltpu.CompilerParams(vmem_limit_bytes=VMEM_GRANT),
        cost_estimate=pl.CostEstimate(
            flops=10 * 10**9 // chunks, bytes_accessed=6 * 10**6, transcendentals=0
        ),
    )(core, qkv, qkv, qkv)


def attend_back_kernel(
    core_ref, q_ref, k_ref, v_ref, *refs, heads, chunks
):
    o_refs = refs[0:chunks]
    lse_refs = refs[chunks : 2 * chunks]
    do_refs = refs[2 * chunks : 3 * chunks]
    out_ref, dk_acc, dv_acc = refs[3 * chunks :]
    core = core_ref[0]
    place = (core, 1 - core)
    width = q_ref.shape[-1]
    col_head = head_ids((TILE, width))
    causal = causal_tile(TILE)
    per_half = k_ref.shape[2] // TILE
    per_chunk = per_half // chunks
    dk_acc[...] = jnp.zeros_like(dk_acc)
    dv_acc[...] = jnp.zeros_like(dv_acc)
    for half in range(2):
        for sub in range(per_half):
            blk = per_half * half + sub
            rows = slice(sub * TILE, (sub + 1) * TILE)
            inner = slice((sub % per_chunk) * TILE, (sub % per_chunk + 1) * TILE)
            q_blk = q_ref[place[half], 0, rows, :]
            do_blk = do_refs[sub // per_chunk][place[half], 0, inner, :]
            o_blk = o_refs[sub // per_chunk][place[half], 0, inner, :]
            lse_blk = lse_refs[sub // per_chunk][place[half], 0, inner, :]
            overlap = do_blk.astype(F32) * o_blk.astype(F32)
            q_all, do_all, lse_all, delta_all = [], [], [], []
            for head in range(heads):
                mine = col_head == head
                q_all.append(jnp.where(mine, q_blk, jnp.zeros_like(q_blk)))
                do_all.append(jnp.where(mine, do_blk, jnp.zeros_like(do_blk)))
                lse_all.append(lse_blk[:, head : head + 1])
                delta_all.append(jnp.sum(jnp.where(mine, overlap, 0.0), axis=1, keepdims=True))
            q_cat = jnp.concatenate(q_all, axis=0)
            do_cat = jnp.concatenate(do_all, axis=0)
            dq = [jnp.zeros((TILE, width), F32) for _ in range(heads)]
            for j in range(blk + 1):
                cols = slice((j % per_half) * TILE, (j % per_half + 1) * TILE)
                k_blk = k_ref[place[j // per_half], 0, cols, :]
                v_blk = v_ref[place[j // per_half], 0, cols, :]
                p_all, ds_all = [], []
                for head in range(heads):
                    p = jnp.exp(mm(q_all[head], k_blk, NT) - lse_all[head])
                    if j == blk:
                        p = jnp.where(causal, p, 0.0)
                    dp = mm(do_all[head], v_blk, NT)
                    ds = (p * (dp - delta_all[head])).astype(BF16)
                    dq[head] = dq[head] + mm(ds, k_blk)
                    p_all.append(p.astype(BF16))
                    ds_all.append(ds)
                dk_acc[j] += mm(jnp.concatenate(ds_all, axis=0), q_cat, TN)
                dv_acc[j] += mm(jnp.concatenate(p_all, axis=0), do_cat, TN)
            total = dq[0]
            for head in range(1, heads):
                total = jnp.where(col_head == head, dq[head], total)
            out_ref[place[half], 0, rows, 0:width] = (total * HEAD_DIM**-0.5).astype(BF16)
    for j in range(2 * per_half):
        rows = slice((j % per_half) * TILE, (j % per_half + 1) * TILE)
        out_ref[place[j // per_half], 0, rows, width : 2 * width] = dk_acc[j].astype(BF16)
        out_ref[place[j // per_half], 0, rows, 2 * width :] = dv_acc[j].astype(BF16)


def attend_back(core, qkv, outs, lses, back):
    _, seqs, rows, triple = qkv.shape
    width = triple // 3
    chunks = len(outs)
    part = rows // chunks

    def block(size, cols, at):
        return pl.BlockSpec((2, 1, size, cols), lambda s, c: (0, s, 0, at))

    return pl.pallas_call(
        partial(attend_back_kernel, heads=width // HEAD_DIM, chunks=chunks),
        grid_spec=pltpu.PrefetchScalarGridSpec(
            num_scalar_prefetch=1,
            grid=(seqs,),
            in_specs=[block(rows, width, 0), block(rows, width, 1), block(rows, width, 2)]
            + [block(part, width, 0)] * chunks
            + [block(part, 128, 0)] * chunks
            + [block(part, width, 0)] * chunks,
            out_specs=block(rows, triple, 0),
            scratch_shapes=[pltpu.VMEM((2 * rows // TILE, TILE, width), F32)] * 2,
        ),
        out_shape=jax.ShapeDtypeStruct(qkv.shape, BF16),
        compiler_params=pltpu.CompilerParams(vmem_limit_bytes=VMEM_GRANT),
        cost_estimate=pl.CostEstimate(
            flops=25 * 10**9, bytes_accessed=12 * 10**6, transcendentals=0
        ),
    )(core, qkv, qkv, qkv, *outs, *lses, *back)


def hidden_kernel(*refs):
    blocks = refs[0:4]
    w_ref, bias_ref, dact_ref, act_ref, back_ref, sum_ref, all_ref = refs[4:]
    rows = blocks[0].shape[0]
    value = jnp.concatenate([block[...] for block in blocks], axis=0)
    hidden = mm(value, w_ref[...]) + bias_ref[...]
    square = hidden * hidden
    bent = jnp.tanh(gelu_in * hidden * (1.0 + gelu_cube * square))
    half = 0.5 * (1.0 + bent)
    act_ref[...] = (hidden * half).astype(BF16)
    slope = half + 0.5 * hidden * (1.0 - bent * bent) * (
        gelu_in * (1.0 + 3.0 * gelu_cube * square)
    )
    back = (dact_ref[...].astype(F32) * slope).astype(BF16)
    back_ref[...] = back
    sum_ref[...] = jnp.sum(back.astype(F32), axis=0, keepdims=True)

    @pl.when(pl.program_id(0) == 0)
    def _():
        for at in range(4):
            all_ref[at * rows : (at + 1) * rows, :] = blocks[at][...]


def hidden_layer(blocks, weight, bias, dact):
    rows, width = blocks[0].shape
    cols = weight.shape[1]
    tile = min(256, cols)
    whole = pl.BlockSpec((rows, width), lambda n: (0, 0))
    column = pl.BlockSpec((4 * rows, tile), lambda n: (0, n))
    return pl.pallas_call(
        hidden_kernel,
        grid=(cols // tile,),
        in_specs=[whole] * 4
        + [
            pl.BlockSpec((width, tile), lambda n: (0, n)),
            pl.BlockSpec((1, tile), lambda n: (0, n)),
            column,
        ],
        out_specs=[
            column,
            column,
            pl.BlockSpec((1, tile), lambda n: (0, n)),
            pl.BlockSpec((4 * rows, width), lambda n: (0, 0)),
        ],
        out_shape=[
            jax.ShapeDtypeStruct((4 * rows, cols), BF16),
            jax.ShapeDtypeStruct((4 * rows, cols), BF16),
            jax.ShapeDtypeStruct((1, cols), F32),
            jax.ShapeDtypeStruct((4 * rows, width), BF16),
        ],
        compiler_params=pltpu.CompilerParams(vmem_limit_bytes=VMEM_GRANT),
        cost_estimate=pl.CostEstimate(
            flops=8 * rows * width * cols, bytes_accessed=12 * 10**6, transcendentals=0
        ),
    )(*blocks, weight, bias.reshape(1, -1), dact)


def reversed_bits(index, count):
    out = 0
    bit = 1
    while bit < count:
        out = 2 * out + (index & 1)
        index //= 2
        bit *= 2
    return out


def muon_kernel(
    limit_ref,
    landed_ref,
    mom_hbm,
    master_hbm,
    grad_out,
    mom_out,
    master_out,
    grad_buf,
    mom_buf,
    master_buf,
    x_buf,
    gram,
    poly,
    sems,
    *,
    out_rows,
):
    count, share, size = landed_ref.shape
    tile = 512
    tiles = size // tile
    load_mom = pltpu.make_async_copy(mom_hbm, mom_buf, sems.at[0])
    load_master = pltpu.make_async_copy(master_hbm, master_buf, sems.at[1])
    store_grad = pltpu.make_async_copy(grad_buf, grad_out, sems.at[2])
    store_mom = pltpu.make_async_copy(mom_buf, mom_out, sems.at[3])
    store_master = pltpu.make_async_copy(master_buf, master_out, sems.at[4])
    load_mom.start()
    load_master.start()
    row_limit = limit_ref[0]
    col_limit = limit_ref[1]
    is_out = limit_ref[2] == 1

    @pl.when(is_out)
    def _():
        grad_buf[...] = jnp.zeros_like(grad_buf)
        for src in range(count):
            at = reversed_bits(src, count)
            piece = landed_ref[src].astype(F32)
            grad_buf[at * out_rows : (at + 1) * out_rows, :] = piece[:out_rows]

    @pl.when(jnp.logical_not(is_out))
    def _():
        for src in range(count):
            at = reversed_bits(src, count)
            grad_buf[at * share : (at + 1) * share, :] = landed_ref[src].astype(F32)

    store_grad.start()
    load_mom.wait()
    block = 128

    def valid(r):
        row = lax.broadcasted_iota(jnp.int32, (block, size), 0) + r * block
        col = lax.broadcasted_iota(jnp.int32, (block, size), 1)
        return (row < row_limit) & (col < col_limit)

    def at_rows(r, step):
        return pl.ds(pl.multiple_of(r * step, step), step)

    def momentum_rows(r, total):
        rows = at_rows(r, block)
        value = jnp.where(valid(r), mom_decay * mom_buf[rows, :] + grad_buf[rows, :], 0.0)
        mom_buf[rows, :] = value
        return total + value * value

    total = lax.fori_loop(0, size // block, momentum_rows, jnp.zeros((block, size), F32))
    store_mom.start()
    scale = 1.0 / (jnp.sqrt(jnp.sum(total)) + 1e-07)

    def first_rows(r, carry):
        rows = at_rows(r, block)
        x_buf[0, rows, :] = (mom_buf[rows, :] * scale).astype(BF16)
        return carry

    lax.fori_loop(0, size // block, first_rows, 0)

    def one_turn(turn, carry):
        now = lax.rem(turn, 2)
        later = 1 - now

        def gram_rows(r, c):
            rows = at_rows(r, tile)
            gram[rows, :] = mm(x_buf[now, rows, :], x_buf[now], NT).astype(BF16)
            return c

        lax.fori_loop(0, tiles, gram_rows, 0)

        def poly_rows(r, c):
            rows = at_rows(r, tile)
            mine = gram[rows, :]
            poly[rows, :] = (ns_b * mine.astype(F32) + ns_c * mm(mine, gram[...])).astype(BF16)
            return c

        lax.fori_loop(0, tiles, poly_rows, 0)

        def next_rows(r, c):
            rows = at_rows(r, tile)
            x_buf[later, rows, :] = (
                ns_a * x_buf[now, rows, :].astype(F32) + mm(poly[rows, :], x_buf[now])
            ).astype(BF16)
            return c

        lax.fori_loop(0, tiles, next_rows, 0)
        return carry

    lax.fori_loop(0, jnp.where(row_limit > 0, NS_STEPS, 0), one_turn, 0)
    load_master.wait()

    def master_rows(r, carry):
        rows = at_rows(r, block)
        ortho = x_buf[NS_STEPS % 2, rows, :].astype(F32)
        fresh = master_buf[rows, :] * (1.0 - muon_rate * muon_decay) - muon_rate * ortho
        master_buf[rows, :] = jnp.where(valid(r), fresh, 0.0)
        return carry

    lax.fori_loop(0, size // block, master_rows, 0)
    store_master.start()
    store_grad.wait()
    store_mom.wait()
    store_master.wait()


def muon_update(limits, landed, momentum, master, out_rows):
    size = momentum.shape[0]
    shape = jax.ShapeDtypeStruct((size, size), F32)
    anywhere = pl.BlockSpec(memory_space=pl.ANY)
    return pl.pallas_call(
        partial(muon_kernel, out_rows=out_rows),
        in_specs=[
            pl.BlockSpec(memory_space=pltpu.SMEM),
            pl.BlockSpec(memory_space=pltpu.VMEM),
            anywhere,
            anywhere,
        ],
        out_specs=[anywhere] * 3,
        out_shape=[shape] * 3,
        scratch_shapes=[
            pltpu.VMEM((size, size), F32),
            pltpu.VMEM((size, size), F32),
            pltpu.VMEM((size, size), F32),
            pltpu.VMEM((2, size, size), BF16),
            pltpu.VMEM((size, size), BF16),
            pltpu.VMEM((size, size), BF16),
            pltpu.SemaphoreType.DMA((5,)),
        ],
        compiler_params=pltpu.CompilerParams(vmem_limit_bytes=VMEM_GRANT),
        cost_estimate=pl.CostEstimate(
            flops=6 * NS_STEPS * size**3, bytes_accessed=22 * size * size, transcendentals=0
        ),
    )(limits, landed, momentum, master)


def swap(value, bit):
    count = lax.axis_size("tensor")
    return lax.ppermute(value, "tensor", [(i, i ^ bit) for i in range(count)])


def gather_four(value):
    core_block = swap(value, 1)
    far_block = swap(value, 2)
    return value, far_block, core_block, swap(far_block, 1)


def scatter_sum(value, weight, dims):
    size = value.shape[0] // 4
    send = mm(value[2 * size :], weight, dims).astype(BF16)
    arrived = swap(send, 1)
    keep = mm(value[: 2 * size], weight, dims)
    part = keep + arrived.astype(F32)
    far = swap(part[size:].astype(BF16), 2)
    return part[:size] + far.astype(F32)


def data_swap(value, bit):
    count = lax.axis_size("dp")
    return lax.ppermute(value, "dp", [(i, i ^ bit) for i in range(count)])


def after(value, *others):
    return lax.optimization_barrier((value, *others))[0]


def gather_kinds(pieces):
    index = lax.axis_index("dp")
    before = []
    results = []
    for piece in pieces:
        done = []
        for at, bit in enumerate(reversed(axis_bits("dp"))):
            if before:
                piece = after(piece, before[at])
            other = data_swap(piece, bit)
            upper = (index & bit) != 0
            piece = jnp.where(
                upper,
                jnp.concatenate([other, piece], axis=0),
                jnp.concatenate([piece, other], axis=0),
            )
            done.append(other)
        before = done
        results.append(piece)
    return results


def halve(value, bit):
    half = value.shape[0] // 2
    upper = ((lax.axis_index("dp") & bit) != 0).astype(jnp.int32)
    give = lax.dynamic_slice_in_dim(value, (1 - upper) * half, half, 0)
    keep = lax.dynamic_slice_in_dim(value, upper * half, half, 0)
    return (keep.astype(F32) + data_swap(give, bit).astype(F32)).astype(BF16)


def halve_rest(value, done=1):
    for bit in axis_bits("dp")[done:]:
        value = halve(value, bit)
    return value


def axis_bits(name):
    count = lax.axis_size(name)
    bits = []
    bit = 1
    while bit < count:
        bits.append(bit)
        bit *= 2
    return bits


def small_gather(value):
    piece = value.reshape(1, -1)
    for name in ("tensor", "dp"):
        index = lax.axis_index(name)
        count = lax.axis_size(name)
        for bit in axis_bits(name):
            other = lax.ppermute(piece, name, [(i, i ^ bit) for i in range(count)])
            upper = (index & bit) != 0
            piece = jnp.where(
                upper,
                jnp.concatenate([other, piece], axis=0),
                jnp.concatenate([piece, other], axis=0),
            )
    return piece.reshape(-1)


def small_scatter(value):
    for name in ("dp", "tensor"):
        index = lax.axis_index(name)
        count = lax.axis_size(name)
        for bit in reversed(axis_bits(name)):
            low, high = jnp.split(value, 2)
            upper = (index & bit) != 0
            give = jnp.where(upper, low, high)
            keep = jnp.where(upper, high, low)
            value = keep + lax.ppermute(give, name, [(i, i ^ bit) for i in range(count)])
    return value


def norm_parts(values):
    centred = values - jnp.mean(values, axis=-1, keepdims=True)
    spread = jnp.mean(centred * centred, axis=-1, keepdims=True)
    scale = lax.rsqrt(spread + ln_eps)
    return centred * scale, scale


def norm_back(unit, scale, gain_vec, grad):
    inner = grad * gain_vec
    return scale * (
        inner
        - jnp.mean(inner, axis=-1, keepdims=True)
        - unit * jnp.mean(inner * unit, axis=-1, keepdims=True)
    )


def per_device(
    inputs, out_grad, owners, master_slots, momentum_slots, small_master, small_first, small_second
):
    rows_dev, width = inputs.shape
    tensor_count = lax.axis_size("tensor")
    data_count = lax.axis_size("dp")
    tensor_idx = lax.axis_index("tensor")
    data_idx = lax.axis_index("dp")
    head_width = width // tensor_count
    ff_width = FF // tensor_count
    share = width // data_count
    share_out = head_width // data_count
    core = jnp.reshape(tensor_idx & 1, (1,)).astype(jnp.int32)
    owner_row = lax.dynamic_index_in_dim(owners, tensor_idx, 0, keepdims=False)
    owned = owner_row == data_idx
    slot_value = master_slots[0]

    order = [reversed_bits(i, data_count) for i in range(data_count)]
    slot_low = slot_value.astype(BF16)
    offer_out = jnp.pad(
        slot_low[:head_width].reshape(data_count, share_out, width),
        ((0, 0), (0, share - share_out), (0, 0)),
    )
    offer = jnp.where(owned[1], offer_out, slot_low.reshape(data_count, share, width))
    shares = lax.all_to_all(jnp.concatenate([offer[i : i + 1] for i in order]), "dp", 0, 0)

    def share_of(kind):
        return lax.dynamic_index_in_dim(shares, owner_row[kind], 0, keepdims=False)

    w_qkv, w_out, w_proj, w_fc = gather_kinds(
        (share_of(0)[:, : 3 * head_width], share_of(1)[:share_out], share_of(3), share_of(2))
    )

    params = small_gather(small_master)

    def own_slice(start, size):
        return lax.dynamic_slice_in_dim(params, start + tensor_idx * size, size, 0)

    gain_one = params[0:width]
    shift_one = params[width : 2 * width]
    bias_query = own_slice(2 * width, head_width)
    bias_value = own_slice(3 * width, head_width)
    bias_out = params[4 * width : 5 * width]
    gain_two = params[5 * width : 6 * width]
    shift_two = params[6 * width : 7 * width]
    bias_fc = own_slice(7 * width, ff_width)
    bias_proj = params[7 * width + FF :]

    part = rows_dev // CHUNKS
    rows_of = [slice(chunk * part, (chunk + 1) * part) for chunk in range(CHUNKS)]
    rows_in = inputs.astype(F32)
    unit_one, scale_one = norm_parts(rows_in)
    unit_all, _ = norm_parts(jnp.concatenate(gather_four(inputs)).astype(F32))
    normed_all = (unit_all * gain_one + shift_one).astype(BF16)
    dy_all = [jnp.concatenate(gather_four(out_grad[rows])) for rows in rows_of]
    bias_qkv = jnp.concatenate([bias_query, jnp.zeros_like(bias_query), bias_value])
    scale_qkv = jnp.where(jnp.arange(3 * head_width) < head_width, HEAD_DIM**-0.5, 1.0)
    qkv = ((mm(normed_all, w_qkv) + bias_qkv) * scale_qkv).astype(BF16)
    qkv = qkv.reshape(2, 2, rows_dev, 3 * head_width)
    back_act = [mm(dy, w_proj, NT).astype(BF16) for dy in dy_all]

    mixed, log_sums = [], []
    for chunk in range(CHUNKS):
        mixed_one, sums_one = attend(core, qkv, chunk, CHUNKS)
        mixed.append(mixed_one)
        log_sums.append(sums_one)
    middles, branches, grad_proj, grad_fc, fc_bias_grad = [], [], 0.0, 0.0, 0.0
    back_normed_two, mine_two = [], []
    normed_two = None
    for chunk in range(CHUNKS):
        branch = scatter_sum(rows2(mixed[chunk]), w_out, NN)
        if chunk > 0:
            branch = after(branch, normed_two)
        middle = rows_in[rows_of[chunk]] + branch + bias_out
        unit_two, scale_two = norm_parts(middle)
        normed_two = (unit_two * gain_two + shift_two).astype(BF16)
        acts, backs, sums, normed_two_all = hidden_layer(
            gather_four(normed_two), w_fc, bias_fc, back_act[chunk]
        )
        fc_bias_grad = fc_bias_grad + sums[0]
        back_normed_two.append(scatter_sum(backs, w_fc, NT))
        branches.append(scatter_sum(acts, w_proj, NN))
        grad_proj = grad_proj + mm(acts, dy_all[chunk], TN)
        grad_fc = grad_fc + mm(normed_two_all, backs, TN)
        middles.append(middle)
        mine_two.append((unit_two, scale_two))
    middle = jnp.concatenate(middles)
    block_out = (middle + jnp.concatenate(branches) + bias_proj).astype(BF16)
    half_proj = halve(halve(grad_proj.astype(BF16), 1), 2)
    half_fc = halve(grad_fc.astype(BF16), 1)

    back_middles, back_mixed = [], []
    gain_two_grad, shift_two_grad, grad_out = 0.0, 0.0, 0.0
    back_low = None
    for chunk in range(CHUNKS):
        unit_two, scale_two = mine_two[chunk]
        grad = back_normed_two[chunk]
        if chunk > 0:
            grad = after(grad, back_low)
        back_middle = out_grad[rows_of[chunk]].astype(F32) + norm_back(
            unit_two, scale_two, gain_two, grad
        )
        back_low = back_middle.astype(BF16)
        mid = jnp.concatenate(gather_four(back_low))
        back_mixed.append(mm(mid, w_out, NT).astype(BF16).reshape(2, 2, part, head_width))
        grad_out = grad_out + mm(rows2(mixed[chunk]), mid, TN)
        gain_two_grad = gain_two_grad + jnp.sum(grad * unit_two, axis=0)
        shift_two_grad = shift_two_grad + jnp.sum(grad, axis=0)
        back_middles.append(back_middle)
    back_middle = jnp.concatenate(back_middles)
    proj_bias_grad = jnp.sum(out_grad, axis=0, dtype=F32)
    out_bias_grad = jnp.sum(back_middle, axis=0)
    back_mixed, half_proj, half_fc = lax.optimization_barrier((back_mixed, half_proj, half_fc))
    share_proj = halve_rest(half_proj, 2)
    share_fc = halve_rest(half_fc)
    back_qkv = attend_back(core, qkv, mixed, log_sums, back_mixed)
    grad_qkv = mm(normed_all, rows2(back_qkv), TN).astype(BF16)
    qkv_bias_grad = jnp.sum(back_qkv, axis=(0, 1, 2), dtype=F32)
    share_out_grad = halve_rest(halve(grad_out.astype(BF16), 1))
    share_qkv = halve_rest(halve(grad_qkv, 1))
    back_normed = scatter_sum(rows2(after(back_qkv, grad_qkv)), w_qkv, NT)
    input_grad = back_middle + norm_back(unit_one, scale_one, gain_one, back_normed)
    gain_one_grad = jnp.sum(back_normed * unit_one, axis=0)
    shift_one_grad = jnp.sum(back_normed, axis=0)

    bundle = jnp.zeros((data_count, share, width), BF16)
    pieces = (
        jnp.pad(share_qkv, ((0, 0), (0, width - 3 * head_width))),
        jnp.pad(share_out_grad, ((0, share - share_out), (0, 0))),
        share_fc,
        share_proj,
    )
    for kind in range(4):
        bundle = lax.dynamic_update_index_in_dim(bundle, pieces[kind], owner_row[kind], 0)
    landed = lax.all_to_all(bundle, "dp", 0, 0)
    full_grad = jnp.concatenate(
        [
            gain_one_grad,
            shift_one_grad,
            jnp.zeros((2 * width,), F32),
            out_bias_grad,
            gain_two_grad,
            shift_two_grad,
            jnp.zeros((FF,), F32),
            proj_bias_grad,
        ]
    )
    for grad, start, size in (
        (qkv_bias_grad[:head_width], 2 * width, head_width),
        (qkv_bias_grad[2 * head_width :], 3 * width, head_width),
        (fc_bias_grad, 7 * width, ff_width),
    ):
        full_grad = lax.dynamic_update_slice_in_dim(full_grad, grad, start + tensor_idx * size, 0)
    small_grad = small_scatter(full_grad)
    first_new = beta_one * small_first + (1.0 - beta_one) * small_grad
    second_new = beta_two * small_second + (1.0 - beta_two) * small_grad * small_grad
    first_hat = first_new / (1.0 - beta_one**STEP)
    second_hat = second_new / (1.0 - beta_two**STEP)
    small_new = small_master - adam_rate * first_hat / (jnp.sqrt(second_hat) + adam_eps)

    row_limit = jnp.where(owned[1], head_width, jnp.where(jnp.any(owned), width, 0))
    col_limit = jnp.where(owned[0], 3 * head_width, width)
    limits = jnp.stack([row_limit, col_limit, owned[1].astype(jnp.int32)]).astype(jnp.int32)
    grad_slot, mom_slot, fresh_slot = muon_update(
        limits, landed, momentum_slots[0], slot_value, share_out
    )
    return (
        block_out,
        input_grad,
        grad_slot[None],
        mom_slot[None],
        fresh_slot[None],
        small_grad,
        second_new,
        small_new,
    )


def solution(mesh):
    return jax.shard_map(
        per_device,
        mesh=mesh,
        in_specs=(
            P(("dp", "tensor"), None),
            P(("dp", "tensor"), None),
            P(),
            P("dp", "tensor", None),
            P("dp", "tensor", None),
            P(("dp", "tensor")),
            P(("dp", "tensor")),
            P(("dp", "tensor")),
        ),
        out_specs=(
            P(("dp", "tensor"), None),
            P(("dp", "tensor"), None),
            P("dp", "tensor", None),
            P("dp", "tensor", None),
            P("dp", "tensor", None),
            P(("dp", "tensor")),
            P(("dp", "tensor")),
            P(("dp", "tensor")),
        ),
        check_vma=False,
    )
```

```python
from functools import partial

import jax
import jax.numpy as jnp
from jax import lax
from jax.experimental import pallas as pl
from jax.experimental.pallas import tpu as pltpu
from jax.sharding import PartitionSpec as P

HEADS = 16
FF = 4096
SEQ = 1024
NS_STEPS = 5
STEP = 10
HEAD_DIM = 64

ln_eps = 1e-05
mom_decay = 0.95
ns_a = 3.4445
ns_b = -4.775
ns_c = 2.0315
muon_rate = 0.5
muon_decay = 0.01
beta_one = 0.9
beta_two = 0.95
adam_rate = 0.2
adam_eps = 1e-08
masked_score = -1e30
gelu_in = 0.7978845608028654
gelu_cube = 0.044715

CHUNKS = 2
TILE = 256
VMEM_GRANT = 48 * 1024 * 1024
BF16 = jnp.bfloat16
F32 = jnp.float32

NN = (((1,), (0,)), ((), ()))
NT = (((1,), (1,)), ((), ()))
TN = (((0,), (0,)), ((), ()))


def mm(left, right, dims=NN):
    return lax.dot_general(left, right, dims, preferred_element_type=F32)


def rows2(value):
    return value.reshape(-1, value.shape[-1])


def head_ids(shape):
    return lax.broadcasted_iota(jnp.int32, shape, 1) // HEAD_DIM


def causal_tile(tile):
    row = lax.broadcasted_iota(jnp.int32, (tile, tile), 0)
    col = lax.broadcasted_iota(jnp.int32, (tile, tile), 1)
    return row >= col


def attend_kernel(core_ref, q_ref, k_ref, v_ref, o_ref, lse_ref, *, subs, heads):
    core = core_ref[0]
    place = (core, 1 - core)
    width = q_ref.shape[-1]
    col_head = head_ids((TILE, width))
    lane = lax.broadcasted_iota(jnp.int32, (TILE, 128), 1)
    causal = causal_tile(TILE)
    per_half = k_ref.shape[2] // TILE
    for half in range(2):
        for at, sub in enumerate(subs):
            blk = per_half * half + sub
            rows = slice(at * TILE, (at + 1) * TILE)
            q_blk = q_ref[place[half], 0, rows, :]
            acc = jnp.zeros((TILE, width), F32)
            lse = jnp.zeros((TILE, 128), F32)
            for head in range(heads):
                q_one = jnp.where(col_head == head, q_blk, jnp.zeros_like(q_blk))
                scores = []
                for j in range(blk + 1):
                    cols = slice((j % per_half) * TILE, (j % per_half + 1) * TILE)
                    s = mm(q_one, k_ref[place[j // per_half], 0, cols, :], NT)
                    if j == blk:
                        s = jnp.where(causal, s, masked_score)
                    scores.append(s)
                top = scores[0]
                for s in scores[1:]:
                    top = jnp.maximum(top, s)
                top = jnp.max(top, axis=1, keepdims=True)
                total = jnp.zeros((TILE, TILE), F32)
                out = jnp.zeros((TILE, width), F32)
                for j in range(blk + 1):
                    cols = slice((j % per_half) * TILE, (j % per_half + 1) * TILE)
                    p = jnp.exp(scores[j] - top)
                    total = total + p
                    out = out + mm(p.astype(BF16), v_ref[place[j // per_half], 0, cols, :])
                total = jnp.sum(total, axis=1, keepdims=True)
                acc = jnp.where(col_head == head, out * (1.0 / total), acc)
                lse = jnp.where(lane == head, top + jnp.log(total), lse)
            o_ref[place[half], 0, rows, :] = acc.astype(BF16)
            lse_ref[place[half], 0, rows, :] = lse


def attend(core, qk, v, chunk, chunks):
    _, seqs, rows, width = v.shape
    part = rows // chunks
    per = part // TILE
    subs = tuple(range(chunk * per, (chunk + 1) * per))
    return pl.pallas_call(
        partial(attend_kernel, subs=subs, heads=width // HEAD_DIM),
        grid_spec=pltpu.PrefetchScalarGridSpec(
            num_scalar_prefetch=1,
            grid=(seqs,),
            in_specs=[
                pl.BlockSpec((2, 1, part, width), lambda s, c: (0, s, chunk, 0)),
                pl.BlockSpec((2, 1, rows, width), lambda s, c: (0, s, 0, 1)),
                pl.BlockSpec((2, 1, rows, width), lambda s, c: (0, s, 0, 0)),
            ],
            out_specs=[
                pl.BlockSpec((2, 1, part, width), lambda s, c: (0, s, 0, 0)),
                pl.BlockSpec((2, 1, part, 128), lambda s, c: (0, s, 0, 0)),
            ],
        ),
        out_shape=[
            jax.ShapeDtypeStruct((2, seqs, part, width), BF16),
            jax.ShapeDtypeStruct((2, seqs, part, 128), F32),
        ],
        compiler_params=pltpu.CompilerParams(vmem_limit_bytes=VMEM_GRANT),
        cost_estimate=pl.CostEstimate(
            flops=10 * 10**9 // chunks, bytes_accessed=6 * 10**6, transcendentals=0
        ),
    )(core, qk, qk, v)


def attend_back_kernel(
    core_ref, q_ref, k_ref, v_ref, *refs, heads, chunks
):
    o_refs = refs[0:chunks]
    lse_refs = refs[chunks : 2 * chunks]
    do_refs = refs[2 * chunks : 3 * chunks]
    out_ref, v_out_ref, dk_acc, dv_acc = refs[3 * chunks :]
    core = core_ref[0]
    place = (core, 1 - core)
    width = q_ref.shape[-1]
    col_head = head_ids((TILE, width))
    causal = causal_tile(TILE)
    per_half = k_ref.shape[2] // TILE
    per_chunk = per_half // chunks
    dk_acc[...] = jnp.zeros_like(dk_acc)
    dv_acc[...] = jnp.zeros_like(dv_acc)
    for half in range(2):
        for sub in range(per_half):
            blk = per_half * half + sub
            rows = slice(sub * TILE, (sub + 1) * TILE)
            inner = slice((sub % per_chunk) * TILE, (sub % per_chunk + 1) * TILE)
            q_blk = q_ref[place[half], 0, rows, :]
            do_blk = do_refs[sub // per_chunk][place[half], 0, inner, :]
            o_blk = o_refs[sub // per_chunk][place[half], 0, inner, :]
            lse_blk = lse_refs[sub // per_chunk][place[half], 0, inner, :]
            overlap = do_blk.astype(F32) * o_blk.astype(F32)
            q_all, do_all, lse_all, delta_all = [], [], [], []
            for head in range(heads):
                mine = col_head == head
                q_all.append(jnp.where(mine, q_blk, jnp.zeros_like(q_blk)))
                do_all.append(jnp.where(mine, do_blk, jnp.zeros_like(do_blk)))
                lse_all.append(lse_blk[:, head : head + 1])
                delta_all.append(jnp.sum(jnp.where(mine, overlap, 0.0), axis=1, keepdims=True))
            q_cat = jnp.concatenate(q_all, axis=0)
            do_cat = jnp.concatenate(do_all, axis=0)
            dq = [jnp.zeros((TILE, width), F32) for _ in range(heads)]
            for j in range(blk + 1):
                cols = slice((j % per_half) * TILE, (j % per_half + 1) * TILE)
                k_blk = k_ref[place[j // per_half], 0, cols, :]
                v_blk = v_ref[place[j // per_half], 0, cols, :]
                p_all, ds_all = [], []
                for head in range(heads):
                    p = jnp.exp(mm(q_all[head], k_blk, NT) - lse_all[head])
                    if j == blk:
                        p = jnp.where(causal, p, 0.0)
                    dp = mm(do_all[head], v_blk, NT)
                    ds = (p * (dp - delta_all[head])).astype(BF16)
                    dq[head] = dq[head] + mm(ds, k_blk)
                    p_all.append(p.astype(BF16))
                    ds_all.append(ds)
                dk_acc[j] += mm(jnp.concatenate(ds_all, axis=0), q_cat, TN)
                dv_acc[j] += mm(jnp.concatenate(p_all, axis=0), do_cat, TN)
            total = dq[0]
            for head in range(1, heads):
                total = jnp.where(col_head == head, dq[head], total)
            out_ref[place[half], 0, rows, 0:width] = (total * HEAD_DIM**-0.5).astype(BF16)
    for j in range(2 * per_half):
        rows = slice((j % per_half) * TILE, (j % per_half + 1) * TILE)
        out_ref[place[j // per_half], 0, rows, width : 2 * width] = dk_acc[j].astype(BF16)
        v_out_ref[place[j // per_half], 0, rows, :] = dv_acc[j].astype(BF16)


def attend_back(core, qk, v, outs, lses, back):
    _, seqs, rows, width = v.shape
    chunks = len(outs)
    part = rows // chunks

    def block(size, cols, at):
        return pl.BlockSpec((2, 1, size, cols), lambda s, c: (0, s, 0, at))

    return pl.pallas_call(
        partial(attend_back_kernel, heads=width // HEAD_DIM, chunks=chunks),
        grid_spec=pltpu.PrefetchScalarGridSpec(
            num_scalar_prefetch=1,
            grid=(seqs,),
            in_specs=[block(rows, width, 0), block(rows, width, 1), block(rows, width, 0)]
            + [block(part, width, 0)] * chunks
            + [block(part, 128, 0)] * chunks
            + [block(part, width, 0)] * chunks,
            out_specs=[block(rows, 2 * width, 0), block(rows, width, 0)],
            scratch_shapes=[pltpu.VMEM((2 * rows // TILE, TILE, width), F32)] * 2,
        ),
        out_shape=[jax.ShapeDtypeStruct(qk.shape, BF16), jax.ShapeDtypeStruct(v.shape, BF16)],
        compiler_params=pltpu.CompilerParams(vmem_limit_bytes=VMEM_GRANT),
        cost_estimate=pl.CostEstimate(
            flops=25 * 10**9, bytes_accessed=12 * 10**6, transcendentals=0
        ),
    )(core, qk, qk, v, *outs, *lses, *back)


def hidden_kernel(*refs):
    blocks = refs[0:4]
    w_ref, bias_ref, dact_ref, act_ref, back_ref, sum_ref, all_ref = refs[4:]
    rows = blocks[0].shape[0]
    value = jnp.concatenate([block[...] for block in blocks], axis=0)
    hidden = mm(value, w_ref[...]) + bias_ref[...]
    square = hidden * hidden
    bent = jnp.tanh(gelu_in * hidden * (1.0 + gelu_cube * square))
    half = 0.5 * (1.0 + bent)
    act_ref[...] = (hidden * half).astype(BF16)
    slope = half + 0.5 * hidden * (1.0 - bent * bent) * (
        gelu_in * (1.0 + 3.0 * gelu_cube * square)
    )
    back = (dact_ref[...].astype(F32) * slope).astype(BF16)
    back_ref[...] = back
    sum_ref[...] = jnp.sum(back.astype(F32), axis=0, keepdims=True)

    @pl.when(pl.program_id(0) == 0)
    def _():
        for at in range(4):
            all_ref[at * rows : (at + 1) * rows, :] = blocks[at][...]


def hidden_layer(blocks, weight, bias, dact):
    rows, width = blocks[0].shape
    cols = weight.shape[1]
    tile = min(256, cols)
    whole = pl.BlockSpec((rows, width), lambda n: (0, 0))
    column = pl.BlockSpec((4 * rows, tile), lambda n: (0, n))
    return pl.pallas_call(
        hidden_kernel,
        grid=(cols // tile,),
        in_specs=[whole] * 4
        + [
            pl.BlockSpec((width, tile), lambda n: (0, n)),
            pl.BlockSpec((1, tile), lambda n: (0, n)),
            column,
        ],
        out_specs=[
            column,
            column,
            pl.BlockSpec((1, tile), lambda n: (0, n)),
            pl.BlockSpec((4 * rows, width), lambda n: (0, 0)),
        ],
        out_shape=[
            jax.ShapeDtypeStruct((4 * rows, cols), BF16),
            jax.ShapeDtypeStruct((4 * rows, cols), BF16),
            jax.ShapeDtypeStruct((1, cols), F32),
            jax.ShapeDtypeStruct((4 * rows, width), BF16),
        ],
        compiler_params=pltpu.CompilerParams(vmem_limit_bytes=VMEM_GRANT),
        cost_estimate=pl.CostEstimate(
            flops=8 * rows * width * cols, bytes_accessed=12 * 10**6, transcendentals=0
        ),
    )(*blocks, weight, bias.reshape(1, -1), dact)


def mixed_kernel(*refs):
    blocks = refs[0:4]
    w_ref, out_ref, all_ref = refs[4:]
    rows = blocks[0].shape[0]
    for at in range(4):
        value = blocks[at][...]
        out_ref[at * rows : (at + 1) * rows, :] = mm(value, w_ref[...], NT).astype(BF16)
        all_ref[at * rows : (at + 1) * rows, :] = value


def back_mix(blocks, weight):
    rows, width = blocks[0].shape
    cols = weight.shape[0]
    return pl.pallas_call(
        mixed_kernel,
        in_specs=[pl.BlockSpec(memory_space=pltpu.VMEM)] * 5,
        out_specs=[pl.BlockSpec(memory_space=pltpu.VMEM)] * 2,
        out_shape=[
            jax.ShapeDtypeStruct((4 * rows, cols), BF16),
            jax.ShapeDtypeStruct((4 * rows, width), BF16),
        ],
        compiler_params=pltpu.CompilerParams(vmem_limit_bytes=VMEM_GRANT),
        cost_estimate=pl.CostEstimate(
            flops=8 * rows * width * cols, bytes_accessed=5 * 10**6, transcendentals=0
        ),
    )(*blocks, weight)


def muon_kernel(
    limit_ref,
    landed_ref,
    mom_hbm,
    master_hbm,
    grad_out,
    mom_out,
    master_out,
    grad_buf,
    mom_buf,
    master_buf,
    x_buf,
    gram,
    poly,
    sems,
    *,
    out_rows,
):
    count, share, size = landed_ref.shape
    tile = 512
    tiles = size // tile
    load_mom = pltpu.make_async_copy(mom_hbm, mom_buf, sems.at[0])
    load_master = pltpu.make_async_copy(master_hbm, master_buf, sems.at[1])
    store_grad = pltpu.make_async_copy(grad_buf, grad_out, sems.at[2])
    store_mom = pltpu.make_async_copy(mom_buf, mom_out, sems.at[3])
    store_master = pltpu.make_async_copy(master_buf, master_out, sems.at[4])
    load_mom.start()
    load_master.start()
    row_limit = limit_ref[0]
    col_limit = limit_ref[1]
    is_out = limit_ref[2] == 1

    @pl.when(is_out)
    def _():
        grad_buf[...] = jnp.zeros_like(grad_buf)
        for src in range(count):
            piece = landed_ref[src].astype(F32)
            grad_buf[src * out_rows : (src + 1) * out_rows, :] = piece[:out_rows]

    @pl.when(jnp.logical_not(is_out))
    def _():
        for src in range(count):
            grad_buf[src * share : (src + 1) * share, :] = landed_ref[src].astype(F32)

    store_grad.start()
    load_mom.wait()
    block = 128

    def valid(r):
        row = lax.broadcasted_iota(jnp.int32, (block, size), 0) + r * block
        col = lax.broadcasted_iota(jnp.int32, (block, size), 1)
        return (row < row_limit) & (col < col_limit)

    def at_rows(r, step):
        return pl.ds(pl.multiple_of(r * step, step), step)

    def momentum_rows(r, total):
        rows = at_rows(r, block)
        value = jnp.where(valid(r), mom_decay * mom_buf[rows, :] + grad_buf[rows, :], 0.0)
        mom_buf[rows, :] = value
        return total + value * value

    total = lax.fori_loop(0, size // block, momentum_rows, jnp.zeros((block, size), F32))
    store_mom.start()
    scale = 1.0 / (jnp.sqrt(jnp.sum(total)) + 1e-07)

    def first_rows(r, carry):
        rows = at_rows(r, block)
        x_buf[0, rows, :] = (mom_buf[rows, :] * scale).astype(BF16)
        return carry

    lax.fori_loop(0, size // block, first_rows, 0)

    def one_turn(turn, carry):
        now = lax.rem(turn, 2)
        later = 1 - now

        def gram_rows(r, c):
            rows = at_rows(r, tile)
            gram[rows, :] = mm(x_buf[now, rows, :], x_buf[now], NT).astype(BF16)
            return c

        lax.fori_loop(0, tiles, gram_rows, 0)

        def poly_rows(r, c):
            rows = at_rows(r, tile)
            mine = gram[rows, :]
            poly[rows, :] = (ns_b * mine.astype(F32) + ns_c * mm(mine, gram[...])).astype(BF16)
            return c

        lax.fori_loop(0, tiles, poly_rows, 0)

        def next_rows(r, c):
            rows = at_rows(r, tile)
            x_buf[later, rows, :] = (
                ns_a * x_buf[now, rows, :].astype(F32) + mm(poly[rows, :], x_buf[now])
            ).astype(BF16)
            return c

        lax.fori_loop(0, tiles, next_rows, 0)
        return carry

    lax.fori_loop(0, jnp.where(row_limit > 0, NS_STEPS, 0), one_turn, 0)
    load_master.wait()

    def master_rows(r, carry):
        rows = at_rows(r, block)
        ortho = x_buf[NS_STEPS % 2, rows, :].astype(F32)
        fresh = master_buf[rows, :] * (1.0 - muon_rate * muon_decay) - muon_rate * ortho
        master_buf[rows, :] = jnp.where(valid(r), fresh, 0.0)
        return carry

    lax.fori_loop(0, size // block, master_rows, 0)
    store_master.start()
    store_grad.wait()
    store_mom.wait()
    store_master.wait()


def muon_update(limits, landed, momentum, master, out_rows):
    size = momentum.shape[0]
    shape = jax.ShapeDtypeStruct((size, size), F32)
    anywhere = pl.BlockSpec(memory_space=pl.ANY)
    return pl.pallas_call(
        partial(muon_kernel, out_rows=out_rows),
        in_specs=[
            pl.BlockSpec(memory_space=pltpu.SMEM),
            pl.BlockSpec(memory_space=pltpu.VMEM),
            anywhere,
            anywhere,
        ],
        out_specs=[anywhere] * 3,
        out_shape=[shape] * 3,
        scratch_shapes=[
            pltpu.VMEM((size, size), F32),
            pltpu.VMEM((size, size), F32),
            pltpu.VMEM((size, size), F32),
            pltpu.VMEM((2, size, size), BF16),
            pltpu.VMEM((size, size), BF16),
            pltpu.VMEM((size, size), BF16),
            pltpu.SemaphoreType.DMA((5,)),
        ],
        compiler_params=pltpu.CompilerParams(vmem_limit_bytes=VMEM_GRANT),
        cost_estimate=pl.CostEstimate(
            flops=6 * NS_STEPS * size**3, bytes_accessed=22 * size * size, transcendentals=0
        ),
    )(limits, landed, momentum, master)


def swap(value, bit):
    count = lax.axis_size("tensor")
    return lax.ppermute(value, "tensor", [(i, i ^ bit) for i in range(count)])


def gather_four(value):
    core_block = swap(value, 1)
    far_block = swap(value, 2)
    return value, far_block, core_block, swap(far_block, 1)


def scatter_begin(values, weights, dims):
    size = values[0].shape[0] // 4

    def product(first, last):
        return sum(mm(v[first * size : last * size], w, dims) for v, w in zip(values, weights))

    arrived = swap(product(2, 4).astype(BF16), 1)
    return product(0, 2) + arrived.astype(F32)


def scatter_end(part):
    size = part.shape[0] // 2
    return part[:size] + swap(part[size:].astype(BF16), 2).astype(F32)


def data_swap(value, bit):
    count = lax.axis_size("dp")
    return lax.ppermute(value, "dp", [(i, i ^ bit) for i in range(count)])


def after(value, *others):
    return lax.optimization_barrier((value, *others))[0]


def last_bits(*bits):
    return [bit for bit in reversed(axis_bits("dp")) if bit not in bits] + list(bits)


def bit_axis(bit):
    return len(axis_bits("dp")) - bit.bit_length()


def spread(value):
    return value.reshape((2,) * len(axis_bits("dp")) + (-1, value.shape[-1]))


def double(piece, bit):
    upper = (lax.axis_index("dp") & bit) != 0
    other = data_swap(piece, bit)
    axis = bit_axis(bit)
    return jnp.where(
        upper,
        jnp.concatenate([other, piece], axis=axis),
        jnp.concatenate([piece, other], axis=axis),
    )


def open_piece(value):
    return value.reshape((1,) * len(axis_bits("dp")) + value.shape)


def gather_by(value, bits):
    piece = open_piece(value)
    for bit in bits:
        piece = double(piece, bit)
    return rows2(piece)


def halve(value, bit):
    upper = ((lax.axis_index("dp") & bit) != 0).astype(jnp.int32)
    axis = bit_axis(bit)
    give = lax.dynamic_slice_in_dim(value, 1 - upper, 1, axis)
    keep = lax.dynamic_slice_in_dim(value, upper, 1, axis)
    return (keep.astype(F32) + data_swap(give, bit).astype(F32)).astype(BF16)


def halve_by(value, bits):
    for bit in bits:
        value = halve(value, bit)
    return value


def axis_bits(name):
    count = lax.axis_size(name)
    bits = []
    bit = 1
    while bit < count:
        bits.append(bit)
        bit *= 2
    return bits


def small_gather(value):
    piece = value.reshape(1, -1)
    for name, axis in (("dp", 0), ("tensor", 1)):
        index = lax.axis_index(name)
        count = lax.axis_size(name)
        for bit in axis_bits(name):
            other = lax.ppermute(piece, name, [(i, i ^ bit) for i in range(count)])
            upper = (index & bit) != 0
            piece = jnp.where(
                upper,
                jnp.concatenate([other, piece], axis=axis),
                jnp.concatenate([piece, other], axis=axis),
            )
    return piece.reshape(-1)


def small_scatter(value):
    value = value.reshape(lax.axis_size("dp"), -1)
    for name, axis in (("tensor", 1), ("dp", 0)):
        index = lax.axis_index(name)
        count = lax.axis_size(name)
        for bit in reversed(axis_bits(name)):
            low, high = jnp.split(value, 2, axis=axis)
            upper = (index & bit) != 0
            give = jnp.where(upper, low, high)
            keep = jnp.where(upper, high, low)
            value = keep + lax.ppermute(give, name, [(i, i ^ bit) for i in range(count)])
    return value.reshape(-1)


def norm_parts(values):
    centred = values - jnp.mean(values, axis=-1, keepdims=True)
    spread = jnp.mean(centred * centred, axis=-1, keepdims=True)
    scale = lax.rsqrt(spread + ln_eps)
    return centred * scale, scale


def norm_back(unit, scale, gain_vec, grad):
    inner = grad * gain_vec
    return scale * (
        inner
        - jnp.mean(inner, axis=-1, keepdims=True)
        - unit * jnp.mean(inner * unit, axis=-1, keepdims=True)
    )


def per_device(
    inputs, out_grad, owners, master_slots, momentum_slots, small_master, small_first, small_second
):
    rows_dev, width = inputs.shape
    tensor_count = lax.axis_size("tensor")
    data_count = lax.axis_size("dp")
    tensor_idx = lax.axis_index("tensor")
    data_idx = lax.axis_index("dp")
    head_width = width // tensor_count
    ff_width = FF // tensor_count
    share = width // data_count
    share_out = head_width // data_count
    core = jnp.reshape(tensor_idx & 1, (1,)).astype(jnp.int32)
    owner_row = lax.dynamic_index_in_dim(owners, tensor_idx, 0, keepdims=False)
    owned = owner_row == data_idx
    slot_value = master_slots[0]

    slot_low = slot_value.astype(BF16)
    offer_out = jnp.pad(
        slot_low[:head_width].reshape(data_count, share_out, width),
        ((0, 0), (0, share - share_out), (0, 0)),
    )
    offer = jnp.where(owned[1], offer_out, slot_low.reshape(data_count, share, width))
    shares = lax.all_to_all(offer, "dp", 0, 0)

    def share_of(kind):
        return lax.dynamic_index_in_dim(shares, owner_row[kind], 0, keepdims=False)

    first = share_of(0)
    w_qk = gather_by(first[:, : 2 * head_width], last_bits(2, 1))
    w_v = gather_by(first[:, 2 * head_width : 3 * head_width], last_bits(2, 1)[::-1])
    w_out = gather_by(share_of(1)[:share_out], last_bits(1, 2))
    bits_proj = last_bits(1, 2)
    bits_fc = [2] + last_bits(2, 1)[:-2] + [1]
    w_proj = double(open_piece(after(share_of(3), w_v)), bits_proj[0])
    w_fc = double(open_piece(after(share_of(2), w_v)), bits_fc[0])

    params = small_gather(small_master)

    def own_slice(start, size):
        return lax.dynamic_slice_in_dim(params, start + tensor_idx * size, size, 0)

    gain_one = params[0:width]
    shift_one = params[width : 2 * width]
    bias_query = own_slice(2 * width, head_width)
    bias_value = own_slice(3 * width, head_width)
    bias_out = params[4 * width : 5 * width]
    gain_two = params[5 * width : 6 * width]
    shift_two = params[6 * width : 7 * width]
    bias_fc = own_slice(7 * width, ff_width)
    bias_proj = params[7 * width + FF :]

    part = rows_dev // CHUNKS
    rows_of = [slice(chunk * part, (chunk + 1) * part) for chunk in range(CHUNKS)]
    rows_in = inputs.astype(F32)
    unit_one, scale_one = norm_parts(rows_in)
    unit_all, _ = norm_parts(jnp.concatenate(gather_four(inputs)).astype(F32))
    normed_all = (unit_all * gain_one + shift_one).astype(BF16)
    dy_all = [jnp.concatenate(gather_four(out_grad[rows])) for rows in rows_of]
    bias_qk = jnp.concatenate([bias_query, jnp.zeros_like(bias_query)])
    scale_qk = jnp.where(jnp.arange(2 * head_width) < head_width, HEAD_DIM**-0.5, 1.0)
    qk = ((mm(normed_all, w_qk) + bias_qk) * scale_qk).astype(BF16)
    values = (mm(normed_all, w_v) + bias_value).astype(BF16)
    qk = qk.reshape(2, 2, rows_dev, 2 * head_width)
    values = values.reshape(2, 2, rows_dev, head_width)

    w_proj, w_fc = after((w_proj, w_fc), qk, values)
    for bit in bits_proj[1:-1]:
        w_proj = double(w_proj, bit)
    for bit in bits_fc[1:-1]:
        w_fc = double(w_fc, bit)

    mixed, log_sums, parts = [], [], []
    for chunk in range(CHUNKS):
        mixed_one, sums_one = attend(core, qk, values, chunk, CHUNKS)
        mixed.append(mixed_one)
        log_sums.append(sums_one)
        parts.append(scatter_begin([rows2(mixed_one)], [w_out], NN))
    w_proj = rows2(double(after(w_proj, mixed[-1]), bits_proj[-1]))
    w_fc = rows2(double(after(w_fc, parts[-1]), bits_fc[-1]))
    back_act = [mm(after(dy, parts[-1]), w_proj, NT).astype(BF16) for dy in dy_all]
    middles, mine_two, normed_two = [], [], []
    for chunk in range(CHUNKS):
        branch = scatter_end(parts[chunk])
        if chunk > 0:
            branch = after(branch, normed_two[-1])
        middle = rows_in[rows_of[chunk]] + branch + bias_out
        unit_two, scale_two = norm_parts(middle)
        normed_two.append((unit_two * gain_two + shift_two).astype(BF16))
        middles.append(middle)
        mine_two.append((unit_two, scale_two))

    blocks = [gather_four(value) for value in normed_two]
    acts, backs, wholes, parts = [], [], [], []
    fc_bias_grad = 0.0
    for chunk in range(CHUNKS):
        earlier = parts[-1] if chunk > 0 else normed_two[-1]
        block = after(blocks[chunk], earlier)
        act, back, sums, whole = hidden_layer(block, w_fc, bias_fc, back_act[chunk])
        parts.append(scatter_begin([back], [w_fc], NT))
        acts.append(act)
        backs.append(back)
        wholes.append(whole)
        fc_bias_grad = fc_bias_grad + sums[0]
    acts, backs = after((acts, backs), parts[-1])
    grad_proj = sum(mm(acts[i], dy_all[i], TN) for i in range(CHUNKS)).astype(BF16)
    grad_fc = sum(mm(wholes[i], backs[i], TN) for i in range(CHUNKS)).astype(BF16)
    half_proj = halve(spread(grad_proj), 1)
    half_fc = halve(spread(grad_fc), 2)

    back_middles, back_lows = [], []
    gain_two_grad, shift_two_grad, grad_out = 0.0, 0.0, 0.0
    for chunk in range(CHUNKS):
        unit_two, scale_two = mine_two[chunk]
        grad = scatter_end(parts[chunk])
        if chunk > 0:
            grad = after(grad, back_lows[-1])
        back_middle = out_grad[rows_of[chunk]].astype(F32) + norm_back(
            unit_two, scale_two, gain_two, grad
        )
        back_lows.append(back_middle.astype(BF16))
        gain_two_grad = gain_two_grad + jnp.sum(grad * unit_two, axis=0)
        shift_two_grad = shift_two_grad + jnp.sum(grad, axis=0)
        back_middles.append(back_middle)
    middle = jnp.concatenate(middles)
    back_middle = jnp.concatenate(back_middles)
    proj_bias_grad = jnp.sum(out_grad, axis=0, dtype=F32)
    out_bias_grad = jnp.sum(back_middle, axis=0)

    back_mixed = []
    for chunk in range(CHUNKS):
        block = after(gather_four(back_lows[chunk]), parts[-1])
        mixed_grad, mid = back_mix(block, w_out)
        back_mixed.append(mixed_grad.reshape(2, 2, part, head_width))
        grad_out = grad_out + mm(rows2(mixed[chunk]), mid, TN)
    share_out_grad = halve_by(spread(grad_out.astype(BF16)), last_bits(1, 2)[::-1])
    back_mixed, half_proj, half_fc = lax.optimization_barrier((back_mixed, half_proj, half_fc))
    back_qk, back_v = attend_back(core, qk, values, mixed, log_sums, back_mixed)
    share_proj = halve_by(half_proj, axis_bits("dp")[1:])
    share_fc = halve_by(half_fc, [1] + axis_bits("dp")[2:])
    grad_qk = mm(normed_all, rows2(back_qk), TN).astype(BF16)
    grad_v = mm(normed_all, rows2(back_v), TN).astype(BF16)
    half_qk = halve(spread(grad_qk), 1)
    share_qk = halve_by(half_qk, axis_bits("dp")[1:])
    share_v = halve_by(spread(grad_v), axis_bits("dp")[::-1])
    query_bias_grad = jnp.sum(back_qk[..., :head_width], axis=(0, 1, 2), dtype=F32)
    value_bias_grad = jnp.sum(back_v, axis=(0, 1, 2), dtype=F32)

    acts = after(acts, back_lows[-1])
    branches = [scatter_end(scatter_begin([act], [w_proj], NN)) for act in acts]
    block_out = (middle + jnp.concatenate(branches) + bias_proj).astype(BF16)
    back_qk, back_v = after((back_qk, back_v), half_qk, grad_v)
    back_normed = scatter_end(scatter_begin([rows2(back_qk), rows2(back_v)], [w_qk, w_v], NT))
    input_grad = back_middle + norm_back(unit_one, scale_one, gain_one, back_normed)
    gain_one_grad = jnp.sum(back_normed * unit_one, axis=0)
    shift_one_grad = jnp.sum(back_normed, axis=0)

    bundle = jnp.zeros((data_count, share, width), BF16)
    pieces = (
        jnp.concatenate(
            [rows2(share_qk), rows2(share_v), jnp.zeros((share, width - 3 * head_width), BF16)], axis=1
        ),
        jnp.pad(rows2(share_out_grad), ((0, share - share_out), (0, 0))),
        rows2(share_fc),
        rows2(share_proj),
    )
    for kind in range(4):
        bundle = lax.dynamic_update_index_in_dim(bundle, pieces[kind], owner_row[kind], 0)
    landed = lax.all_to_all(bundle, "dp", 0, 0)
    full_grad = jnp.concatenate(
        [
            gain_one_grad,
            shift_one_grad,
            jnp.zeros((2 * width,), F32),
            out_bias_grad,
            gain_two_grad,
            shift_two_grad,
            jnp.zeros((FF,), F32),
            proj_bias_grad,
        ]
    )
    for grad, start, size in (
        (query_bias_grad, 2 * width, head_width),
        (value_bias_grad, 3 * width, head_width),
        (fc_bias_grad, 7 * width, ff_width),
    ):
        full_grad = lax.dynamic_update_slice_in_dim(full_grad, grad, start + tensor_idx * size, 0)
    small_grad = small_scatter(full_grad)
    first_new = beta_one * small_first + (1.0 - beta_one) * small_grad
    second_new = beta_two * small_second + (1.0 - beta_two) * small_grad * small_grad
    first_hat = first_new / (1.0 - beta_one**STEP)
    second_hat = second_new / (1.0 - beta_two**STEP)
    small_new = small_master - adam_rate * first_hat / (jnp.sqrt(second_hat) + adam_eps)

    row_limit = jnp.where(owned[1], head_width, jnp.where(jnp.any(owned), width, 0))
    col_limit = jnp.where(owned[0], 3 * head_width, width)
    limits = jnp.stack([row_limit, col_limit, owned[1].astype(jnp.int32)]).astype(jnp.int32)
    grad_slot, mom_slot, fresh_slot = muon_update(
        limits, landed, momentum_slots[0], slot_value, share_out
    )
    return (
        block_out,
        input_grad,
        grad_slot[None],
        mom_slot[None],
        fresh_slot[None],
        small_grad,
        second_new,
        small_new,
    )


def solution(mesh):
    return jax.shard_map(
        per_device,
        mesh=mesh,
        in_specs=(
            P(("dp", "tensor"), None),
            P(("dp", "tensor"), None),
            P(),
            P("dp", "tensor", None),
            P("dp", "tensor", None),
            P(("dp", "tensor")),
            P(("dp", "tensor")),
            P(("dp", "tensor")),
        ),
        out_specs=(
            P(("dp", "tensor"), None),
            P(("dp", "tensor"), None),
            P("dp", "tensor", None),
            P("dp", "tensor", None),
            P("dp", "tensor", None),
            P(("dp", "tensor")),
            P(("dp", "tensor")),
            P(("dp", "tensor")),
        ),
        check_vma=False,
    )
```

```python
from functools import partial

import jax
import jax.numpy as jnp
from jax import lax
from jax.experimental import pallas as pl
from jax.experimental.pallas import tpu as pltpu
from jax.sharding import PartitionSpec as P

HEADS = 16
FF = 4096
SEQ = 1024
NS_STEPS = 5
STEP = 10
HEAD_DIM = 64

ln_eps = 1e-05
mom_decay = 0.95
ns_a = 3.4445
ns_b = -4.775
ns_c = 2.0315
muon_rate = 0.5
muon_decay = 0.01
beta_one = 0.9
beta_two = 0.95
adam_rate = 0.2
adam_eps = 1e-08
masked_score = -1e30
gelu_in = 0.7978845608028654
gelu_cube = 0.044715

CHUNKS = 2
TILE = 256
VMEM_GRANT = 48 * 1024 * 1024
BF16 = jnp.bfloat16
F32 = jnp.float32

NN = (((1,), (0,)), ((), ()))
NT = (((1,), (1,)), ((), ()))
TN = (((0,), (0,)), ((), ()))


def mm(left, right, dims=NN):
    return lax.dot_general(left, right, dims, preferred_element_type=F32)


def rows2(value):
    return value.reshape(-1, value.shape[-1])


def head_ids(shape):
    return lax.broadcasted_iota(jnp.int32, shape, 1) // HEAD_DIM


def causal_tile(tile):
    row = lax.broadcasted_iota(jnp.int32, (tile, tile), 0)
    col = lax.broadcasted_iota(jnp.int32, (tile, tile), 1)
    return row >= col


def attend_kernel(core_ref, q_ref, k_ref, v_ref, o_ref, lse_ref, *, subs, heads):
    core = core_ref[0]
    place = (core, 1 - core)
    width = q_ref.shape[-1]
    col_head = head_ids((TILE, width))
    lane = lax.broadcasted_iota(jnp.int32, (TILE, 128), 1)
    causal = causal_tile(TILE)
    per_half = k_ref.shape[2] // TILE
    for half in range(2):
        for at, sub in enumerate(subs):
            blk = per_half * half + sub
            rows = slice(at * TILE, (at + 1) * TILE)
            q_blk = q_ref[place[half], 0, rows, :]
            acc = jnp.zeros((TILE, width), F32)
            lse = jnp.zeros((TILE, 128), F32)
            for head in range(heads):
                q_one = jnp.where(col_head == head, q_blk, jnp.zeros_like(q_blk))
                scores = []
                for j in range(blk + 1):
                    cols = slice((j % per_half) * TILE, (j % per_half + 1) * TILE)
                    s = mm(q_one, k_ref[place[j // per_half], 0, cols, :], NT)
                    if j == blk:
                        s = jnp.where(causal, s, masked_score)
                    scores.append(s)
                top = scores[0]
                for s in scores[1:]:
                    top = jnp.maximum(top, s)
                top = jnp.max(top, axis=1, keepdims=True)
                total = jnp.zeros((TILE, TILE), F32)
                out = jnp.zeros((TILE, width), F32)
                for j in range(blk + 1):
                    cols = slice((j % per_half) * TILE, (j % per_half + 1) * TILE)
                    p = jnp.exp(scores[j] - top)
                    total = total + p
                    out = out + mm(p.astype(BF16), v_ref[place[j // per_half], 0, cols, :])
                total = jnp.sum(total, axis=1, keepdims=True)
                acc = jnp.where(col_head == head, out * (1.0 / total), acc)
                lse = jnp.where(lane == head, top + jnp.log(total), lse)
            o_ref[place[half], 0, rows, :] = acc.astype(BF16)
            lse_ref[place[half], 0, rows, :] = lse


def attend(core, qk, v, chunk, chunks):
    _, seqs, rows, width = v.shape
    part = rows // chunks
    per = part // TILE
    subs = tuple(range(chunk * per, (chunk + 1) * per))
    return pl.pallas_call(
        partial(attend_kernel, subs=subs, heads=width // HEAD_DIM),
        grid_spec=pltpu.PrefetchScalarGridSpec(
            num_scalar_prefetch=1,
            grid=(seqs,),
            in_specs=[
                pl.BlockSpec((2, 1, part, width), lambda s, c: (0, s, chunk, 0)),
                pl.BlockSpec((2, 1, rows, width), lambda s, c: (0, s, 0, 1)),
                pl.BlockSpec((2, 1, rows, width), lambda s, c: (0, s, 0, 0)),
            ],
            out_specs=[
                pl.BlockSpec((2, 1, part, width), lambda s, c: (0, s, 0, 0)),
                pl.BlockSpec((2, 1, part, 128), lambda s, c: (0, s, 0, 0)),
            ],
        ),
        out_shape=[
            jax.ShapeDtypeStruct((2, seqs, part, width), BF16),
            jax.ShapeDtypeStruct((2, seqs, part, 128), F32),
        ],
        compiler_params=pltpu.CompilerParams(vmem_limit_bytes=VMEM_GRANT),
        cost_estimate=pl.CostEstimate(
            flops=10 * 10**9 // chunks, bytes_accessed=6 * 10**6, transcendentals=0
        ),
    )(core, qk, qk, v)


def attend_back_kernel(
    core_ref, q_ref, k_ref, v_ref, *refs, heads, chunks
):
    o_refs = refs[0:chunks]
    lse_refs = refs[chunks : 2 * chunks]
    do_refs = refs[2 * chunks : 3 * chunks]
    out_ref, v_out_ref, dk_acc, dv_acc = refs[-4:]
    core = core_ref[0]
    place = (core, 1 - core)
    width = q_ref.shape[-1]
    col_head = head_ids((TILE, width))
    causal = causal_tile(TILE)
    per_half = k_ref.shape[2] // TILE
    per_chunk = per_half // chunks
    dk_acc[...] = jnp.zeros_like(dk_acc)
    dv_acc[...] = jnp.zeros_like(dv_acc)
    for half in range(2):
        for sub in range(per_half):
            blk = per_half * half + sub
            rows = slice(sub * TILE, (sub + 1) * TILE)
            inner = slice((sub % per_chunk) * TILE, (sub % per_chunk + 1) * TILE)
            q_blk = q_ref[place[half], 0, rows, :]
            do_blk = do_refs[sub // per_chunk][place[half], 0, inner, :]
            o_blk = o_refs[sub // per_chunk][place[half], 0, inner, :]
            lse_blk = lse_refs[sub // per_chunk][place[half], 0, inner, :]
            overlap = do_blk.astype(F32) * o_blk.astype(F32)
            q_all, do_all, lse_all, delta_all = [], [], [], []
            for head in range(heads):
                mine = col_head == head
                q_all.append(jnp.where(mine, q_blk, jnp.zeros_like(q_blk)))
                do_all.append(jnp.where(mine, do_blk, jnp.zeros_like(do_blk)))
                lse_all.append(lse_blk[:, head : head + 1])
                delta_all.append(jnp.sum(jnp.where(mine, overlap, 0.0), axis=1, keepdims=True))
            q_cat = jnp.concatenate(q_all, axis=0)
            do_cat = jnp.concatenate(do_all, axis=0)
            dq = [jnp.zeros((TILE, width), F32) for _ in range(heads)]
            for j in range(blk + 1):
                cols = slice((j % per_half) * TILE, (j % per_half + 1) * TILE)
                k_blk = k_ref[place[j // per_half], 0, cols, :]
                v_blk = v_ref[place[j // per_half], 0, cols, :]
                p_all, ds_all = [], []
                for head in range(heads):
                    p = jnp.exp(mm(q_all[head], k_blk, NT) - lse_all[head])
                    if j == blk:
                        p = jnp.where(causal, p, 0.0)
                    dp = mm(do_all[head], v_blk, NT)
                    ds = (p * (dp - delta_all[head])).astype(BF16)
                    dq[head] = dq[head] + mm(ds, k_blk)
                    p_all.append(p.astype(BF16))
                    ds_all.append(ds)
                dk_acc[j] += mm(jnp.concatenate(ds_all, axis=0), q_cat, TN)
                dv_acc[j] += mm(jnp.concatenate(p_all, axis=0), do_cat, TN)
            total = dq[0]
            for head in range(1, heads):
                total = jnp.where(col_head == head, dq[head], total)
            out_ref[place[half], 0, rows, 0:width] = (total * HEAD_DIM**-0.5).astype(BF16)
    for j in range(2 * per_half):
        rows = slice((j % per_half) * TILE, (j % per_half + 1) * TILE)
        out_ref[place[j // per_half], 0, rows, width : 2 * width] = dk_acc[j].astype(BF16)
        v_out_ref[place[j // per_half], 0, rows, :] = dv_acc[j].astype(BF16)


def attend_back(core, qk, v, outs, lses, back, seq, before=()):
    _, _, rows, width = v.shape
    chunks = len(outs)
    part = rows // chunks

    def block(size, cols, at):
        return pl.BlockSpec((2, 1, size, cols), lambda s, c: (0, seq, 0, at))

    operands = (core, qk, qk, v, *outs, *lses, *back)
    return pl.pallas_call(
        partial(attend_back_kernel, heads=width // HEAD_DIM, chunks=chunks),
        grid_spec=pltpu.PrefetchScalarGridSpec(
            num_scalar_prefetch=1,
            grid=(1,),
            in_specs=[block(rows, width, 0), block(rows, width, 1), block(rows, width, 0)]
            + [block(part, width, 0)] * chunks
            + [block(part, 128, 0)] * chunks
            + [block(part, width, 0)] * chunks
            + [pl.BlockSpec(memory_space=pl.ANY)] * len(before),
            out_specs=[block(rows, 2 * width, 0), block(rows, width, 0)],
            scratch_shapes=[pltpu.VMEM((2 * rows // TILE, TILE, width), F32)] * 2,
        ),
        out_shape=[jax.ShapeDtypeStruct(qk.shape, BF16), jax.ShapeDtypeStruct(v.shape, BF16)],
        input_output_aliases={len(operands) + i: i for i in range(len(before))},
        compiler_params=pltpu.CompilerParams(vmem_limit_bytes=VMEM_GRANT),
        cost_estimate=pl.CostEstimate(
            flops=12 * 10**9, bytes_accessed=6 * 10**6, transcendentals=0
        ),
    )(*operands, *before)


def hidden_kernel(*refs):
    blocks = refs[:-7]
    w_ref, bias_ref, dact_ref, act_ref, back_ref, sum_ref, all_ref = refs[-7:]
    rows = blocks[0].shape[0]
    value = jnp.concatenate([block[...] for block in blocks], axis=0)
    hidden = mm(value, w_ref[...]) + bias_ref[...]
    square = hidden * hidden
    bent = jnp.tanh(gelu_in * hidden * (1.0 + gelu_cube * square))
    half = 0.5 * (1.0 + bent)
    act_ref[...] = (hidden * half).astype(BF16)
    slope = half + 0.5 * hidden * (1.0 - bent * bent) * (
        gelu_in * (1.0 + 3.0 * gelu_cube * square)
    )
    back = (dact_ref[...].astype(F32) * slope).astype(BF16)
    back_ref[...] = back
    sum_ref[...] = jnp.sum(back.astype(F32), axis=0, keepdims=True)

    @pl.when(pl.program_id(0) == 0)
    def _():
        for at in range(len(blocks)):
            all_ref[at * rows : (at + 1) * rows, :] = blocks[at][...]


def hidden_layer(blocks, weight, bias, dact):
    rows, width = blocks[0].shape
    cols = weight.shape[1]
    total = len(blocks) * rows
    tile = min(256, cols)
    whole = pl.BlockSpec((rows, width), lambda n: (0, 0))
    column = pl.BlockSpec((total, tile), lambda n: (0, n))
    return pl.pallas_call(
        hidden_kernel,
        grid=(cols // tile,),
        in_specs=[whole] * len(blocks)
        + [
            pl.BlockSpec((width, tile), lambda n: (0, n)),
            pl.BlockSpec((1, tile), lambda n: (0, n)),
            column,
        ],
        out_specs=[
            column,
            column,
            pl.BlockSpec((1, tile), lambda n: (0, n)),
            pl.BlockSpec((total, width), lambda n: (0, 0)),
        ],
        out_shape=[
            jax.ShapeDtypeStruct((total, cols), BF16),
            jax.ShapeDtypeStruct((total, cols), BF16),
            jax.ShapeDtypeStruct((1, cols), F32),
            jax.ShapeDtypeStruct((total, width), BF16),
        ],
        compiler_params=pltpu.CompilerParams(vmem_limit_bytes=VMEM_GRANT),
        cost_estimate=pl.CostEstimate(
            flops=2 * total * width * cols, bytes_accessed=12 * 10**6, transcendentals=0
        ),
    )(*blocks, weight, bias.reshape(1, -1), dact)


def mixed_kernel(*refs):
    blocks = refs[:-3]
    w_ref, out_ref, all_ref = refs[-3:]
    rows = blocks[0].shape[0]
    for at in range(len(blocks)):
        value = blocks[at][...]
        out_ref[at * rows : (at + 1) * rows, :] = mm(value, w_ref[...], NT).astype(BF16)
        all_ref[at * rows : (at + 1) * rows, :] = value


def back_mix(blocks, weight):
    rows, width = blocks[0].shape
    cols = weight.shape[0]
    total = len(blocks) * rows
    return pl.pallas_call(
        mixed_kernel,
        in_specs=[pl.BlockSpec(memory_space=pltpu.VMEM)] * (len(blocks) + 1),
        out_specs=[pl.BlockSpec(memory_space=pltpu.VMEM)] * 2,
        out_shape=[
            jax.ShapeDtypeStruct((total, cols), BF16),
            jax.ShapeDtypeStruct((total, width), BF16),
        ],
        compiler_params=pltpu.CompilerParams(vmem_limit_bytes=VMEM_GRANT),
        cost_estimate=pl.CostEstimate(
            flops=2 * total * width * cols, bytes_accessed=5 * 10**6, transcendentals=0
        ),
    )(*blocks, weight)


def muon_kernel(
    limit_ref,
    landed_ref,
    mom_hbm,
    master_hbm,
    grad_out,
    mom_out,
    master_out,
    grad_buf,
    mom_buf,
    master_buf,
    x_buf,
    gram,
    poly,
    sems,
    *,
    out_rows,
):
    count, share, size = landed_ref.shape
    tile = 512
    tiles = size // tile
    load_mom = pltpu.make_async_copy(mom_hbm, mom_buf, sems.at[0])
    load_master = pltpu.make_async_copy(master_hbm, master_buf, sems.at[1])
    store_grad = pltpu.make_async_copy(grad_buf, grad_out, sems.at[2])
    store_mom = pltpu.make_async_copy(mom_buf, mom_out, sems.at[3])
    store_master = pltpu.make_async_copy(master_buf, master_out, sems.at[4])
    load_mom.start()
    load_master.start()
    row_limit = limit_ref[0]
    col_limit = limit_ref[1]
    is_out = limit_ref[2] == 1

    @pl.when(is_out)
    def _():
        grad_buf[...] = jnp.zeros_like(grad_buf)
        for src in range(count):
            cols = size * out_rows // share
            piece = landed_ref[src].astype(F32)[:, size - cols :]
            for at in range(share // out_rows):
                grad_buf[
                    src * out_rows : (src + 1) * out_rows, at * cols : (at + 1) * cols
                ] = piece[at * out_rows : (at + 1) * out_rows]

    @pl.when(jnp.logical_not(is_out))
    def _():
        for src in range(count):
            grad_buf[src * share : (src + 1) * share, :] = landed_ref[src].astype(F32)

    store_grad.start()
    load_mom.wait()
    block = 128

    def valid(r):
        row = lax.broadcasted_iota(jnp.int32, (block, size), 0) + r * block
        col = lax.broadcasted_iota(jnp.int32, (block, size), 1)
        return (row < row_limit) & (col < col_limit)

    def at_rows(r, step):
        return pl.ds(pl.multiple_of(r * step, step), step)

    def momentum_rows(r, total):
        rows = at_rows(r, block)
        value = jnp.where(valid(r), mom_decay * mom_buf[rows, :] + grad_buf[rows, :], 0.0)
        mom_buf[rows, :] = value
        return total + value * value

    total = lax.fori_loop(0, size // block, momentum_rows, jnp.zeros((block, size), F32))
    store_mom.start()
    scale = 1.0 / (jnp.sqrt(jnp.sum(total)) + 1e-07)

    def first_rows(r, carry):
        rows = at_rows(r, block)
        x_buf[0, rows, :] = (mom_buf[rows, :] * scale).astype(BF16)
        return carry

    lax.fori_loop(0, size // block, first_rows, 0)

    def one_turn(turn, carry):
        now = lax.rem(turn, 2)
        later = 1 - now

        def gram_rows(r, c):
            rows = at_rows(r, tile)
            gram[rows, :] = mm(x_buf[now, rows, :], x_buf[now], NT).astype(BF16)
            return c

        lax.fori_loop(0, tiles, gram_rows, 0)

        def poly_rows(r, c):
            rows = at_rows(r, tile)
            mine = gram[rows, :]
            poly[rows, :] = (ns_b * mine.astype(F32) + ns_c * mm(mine, gram[...])).astype(BF16)
            return c

        lax.fori_loop(0, tiles, poly_rows, 0)

        def next_rows(r, c):
            rows = at_rows(r, tile)
            x_buf[later, rows, :] = (
                ns_a * x_buf[now, rows, :].astype(F32) + mm(poly[rows, :], x_buf[now])
            ).astype(BF16)
            return c

        lax.fori_loop(0, tiles, next_rows, 0)
        return carry

    lax.fori_loop(0, jnp.where(row_limit > 0, NS_STEPS, 0), one_turn, 0)
    load_master.wait()

    def master_rows(r, carry):
        rows = at_rows(r, block)
        ortho = x_buf[NS_STEPS % 2, rows, :].astype(F32)
        fresh = master_buf[rows, :] * (1.0 - muon_rate * muon_decay) - muon_rate * ortho
        master_buf[rows, :] = jnp.where(valid(r), fresh, 0.0)
        return carry

    lax.fori_loop(0, size // block, master_rows, 0)
    store_master.start()
    store_grad.wait()
    store_mom.wait()
    store_master.wait()


def muon_update(limits, landed, momentum, master, out_rows):
    size = momentum.shape[0]
    shape = jax.ShapeDtypeStruct((size, size), F32)
    anywhere = pl.BlockSpec(memory_space=pl.ANY)
    return pl.pallas_call(
        partial(muon_kernel, out_rows=out_rows),
        in_specs=[
            pl.BlockSpec(memory_space=pltpu.SMEM),
            pl.BlockSpec(memory_space=pltpu.VMEM),
            anywhere,
            anywhere,
        ],
        out_specs=[anywhere] * 3,
        out_shape=[shape] * 3,
        scratch_shapes=[
            pltpu.VMEM((size, size), F32),
            pltpu.VMEM((size, size), F32),
            pltpu.VMEM((size, size), F32),
            pltpu.VMEM((2, size, size), BF16),
            pltpu.VMEM((size, size), BF16),
            pltpu.VMEM((size, size), BF16),
            pltpu.SemaphoreType.DMA((5,)),
        ],
        compiler_params=pltpu.CompilerParams(vmem_limit_bytes=VMEM_GRANT),
        cost_estimate=pl.CostEstimate(
            flops=6 * NS_STEPS * size**3, bytes_accessed=22 * size * size, transcendentals=0
        ),
    )(limits, landed, momentum, master)


def swap(value, bit):
    count = lax.axis_size("tensor")
    return lax.ppermute(value, "tensor", [(i, i ^ bit) for i in range(count)])


def gather_four(value):
    core_block = swap(value, 1)
    far_block = swap(value, 2)
    return value, far_block, core_block, swap(far_block, 1)


def scatter_begin(values, weights, dims):
    size = values[0].shape[0] // 4

    def product(first, last):
        return sum(mm(v[first * size : last * size], w, dims) for v, w in zip(values, weights))

    arrived = swap(product(2, 4).astype(BF16), 1)
    return product(0, 2) + arrived.astype(F32)


def scatter_end(part):
    size = part.shape[0] // 2
    return part[:size] + swap(part[size:].astype(BF16), 2).astype(F32)


def exchange(part):
    size = part.shape[0] // 2
    given = part.astype(BF16)
    given = jnp.concatenate([given[size:], given[:size]])
    return part + swap(given, 2).astype(F32)


def data_swap(value, bit):
    count = lax.axis_size("dp")
    return lax.ppermute(value, "dp", [(i, i ^ bit) for i in range(count)])


def after(value, *others):
    return lax.optimization_barrier((value, *others))[0]


def last_bits(*bits):
    return [bit for bit in reversed(axis_bits("dp")) if bit not in bits] + list(bits)


def bit_axis(bit):
    return len(axis_bits("dp")) - bit.bit_length()


def spread(value):
    return value.reshape((2,) * len(axis_bits("dp")) + (-1, value.shape[-1]))


def double(piece, bit):
    upper = (lax.axis_index("dp") & bit) != 0
    other = data_swap(piece, bit)
    axis = bit_axis(bit)
    return jnp.where(
        upper,
        jnp.concatenate([other, piece], axis=axis),
        jnp.concatenate([piece, other], axis=axis),
    )


def open_piece(value):
    return value.reshape((1,) * len(axis_bits("dp")) + value.shape)


def gather_by(value, bits):
    piece = open_piece(value)
    for bit in bits:
        piece = double(piece, bit)
    return rows2(piece)


def halve(value, bit):
    upper = ((lax.axis_index("dp") & bit) != 0).astype(jnp.int32)
    axis = bit_axis(bit)
    give = lax.dynamic_slice_in_dim(value, 1 - upper, 1, axis)
    keep = lax.dynamic_slice_in_dim(value, upper, 1, axis)
    return (keep.astype(F32) + data_swap(give, bit).astype(F32)).astype(BF16)


def halve_by(value, bits):
    for bit in bits:
        value = halve(value, bit)
    return value


def axis_bits(name):
    count = lax.axis_size(name)
    bits = []
    bit = 1
    while bit < count:
        bits.append(bit)
        bit *= 2
    return bits


def small_gather(piece, name, axis):
    index = lax.axis_index(name)
    count = lax.axis_size(name)
    for bit in axis_bits(name):
        other = lax.ppermute(piece, name, [(i, i ^ bit) for i in range(count)])
        upper = (index & bit) != 0
        piece = jnp.where(
            upper,
            jnp.concatenate([other, piece], axis=axis),
            jnp.concatenate([piece, other], axis=axis),
        )
    return piece


def small_scatter(value):
    value = value.reshape(lax.axis_size("dp"), -1)
    for name, axis in (("tensor", 1), ("dp", 0)):
        index = lax.axis_index(name)
        count = lax.axis_size(name)
        for bit in reversed(axis_bits(name)):
            low, high = jnp.split(value, 2, axis=axis)
            upper = (index & bit) != 0
            give = jnp.where(upper, low, high)
            keep = jnp.where(upper, high, low)
            value = keep + lax.ppermute(give, name, [(i, i ^ bit) for i in range(count)])
    return value.reshape(-1)


def norm_parts(values):
    centred = values - jnp.mean(values, axis=-1, keepdims=True)
    spread = jnp.mean(centred * centred, axis=-1, keepdims=True)
    scale = lax.rsqrt(spread + ln_eps)
    return centred * scale, scale


def norm_back(unit, scale, gain_vec, grad):
    inner = grad * gain_vec
    return scale * (
        inner
        - jnp.mean(inner, axis=-1, keepdims=True)
        - unit * jnp.mean(inner * unit, axis=-1, keepdims=True)
    )


def per_device(
    inputs, out_grad, owners, master_slots, momentum_slots, small_master, small_first, small_second
):
    rows_dev, width = inputs.shape
    tensor_count = lax.axis_size("tensor")
    data_count = lax.axis_size("dp")
    tensor_idx = lax.axis_index("tensor")
    data_idx = lax.axis_index("dp")
    head_width = width // tensor_count
    ff_width = FF // tensor_count
    share = width // data_count
    share_out = head_width // data_count
    core = jnp.reshape(tensor_idx & 1, (1,)).astype(jnp.int32)
    owner_row = lax.dynamic_index_in_dim(owners, tensor_idx, 0, keepdims=False)
    owned = owner_row == data_idx
    slot_value = master_slots[0]

    params = small_gather(small_master.reshape(1, -1), "dp", 0)
    slot_low = slot_value.astype(BF16)
    offer_out = slot_low[:head_width].reshape(data_count, share_out, tensor_count, head_width)
    offer_out = jnp.swapaxes(offer_out, 1, 2).reshape(data_count, share, head_width)
    offer_out = jnp.pad(offer_out, ((0, 0), (0, 0), (width - head_width, 0)))
    offer = jnp.where(owned[1], offer_out, slot_low.reshape(data_count, share, width))
    shares = lax.all_to_all(after(offer, params), "dp", 0, 0)
    params = small_gather(params, "tensor", 1).reshape(-1)

    def own_slice(start, size):
        return lax.dynamic_slice_in_dim(params, start + tensor_idx * size, size, 0)

    gain_one = params[0:width]
    shift_one = params[width : 2 * width]
    bias_query = own_slice(2 * width, head_width)
    bias_value = own_slice(3 * width, head_width)
    bias_out = params[4 * width : 5 * width]
    gain_two = params[5 * width : 6 * width]
    shift_two = params[6 * width : 7 * width]
    bias_fc = own_slice(7 * width, ff_width)
    bias_proj = params[7 * width + FF :]

    part = rows_dev // CHUNKS
    rows_of = [slice(chunk * part, (chunk + 1) * part) for chunk in range(CHUNKS)]
    rows_in = inputs.astype(F32)
    unit_one, scale_one = norm_parts(rows_in)
    inputs_four = gather_four(inputs)
    unit_all, _ = norm_parts(jnp.concatenate(inputs_four).astype(F32))
    normed_all = (unit_all * gain_one + shift_one).astype(BF16)
    dy_four = [gather_four(out_grad[rows]) for rows in rows_of]
    dy_all = [jnp.concatenate(four) for four in dy_four]

    shares = after(shares, normed_all, *dy_all)

    def share_of(kind):
        return lax.dynamic_index_in_dim(shares, owner_row[kind], 0, keepdims=False)

    split = 2 * head_width
    first = share_of(0)
    piece_vo = jnp.concatenate(
        [first[:, split : split + head_width], share_of(1)[:, width - head_width :]], axis=1
    )
    w_qk = gather_by(first[:, :split], last_bits(2, 1))
    w_vo = gather_by(piece_vo, last_bits(1, 2))
    w_v = w_vo[:, :head_width]
    w_out = w_vo[:, head_width:].reshape(data_count, tensor_count, share_out, head_width)
    w_out = jnp.swapaxes(w_out, 1, 2).reshape(head_width, width)
    bits_proj = last_bits(1, 2)
    bits_fc = last_bits(2, 1)
    w_proj = double(open_piece(share_of(3)), bits_proj[0])
    w_fc = double(open_piece(after(share_of(2), w_proj)), bits_fc[0])
    bias_qk = jnp.concatenate([bias_query, jnp.zeros_like(bias_query)])
    scale_qk = jnp.where(jnp.arange(split) < head_width, HEAD_DIM**-0.5, 1.0)
    qk = ((mm(normed_all, w_qk) + bias_qk) * scale_qk).astype(BF16)
    values = (mm(normed_all, w_v) + bias_value).astype(BF16)
    qk, values = after((qk, values), w_proj, w_fc)
    qk = qk.reshape(2, 2, rows_dev, split)
    values = values.reshape(2, 2, rows_dev, head_width)

    for bit in bits_proj[1:-1]:
        w_proj = double(w_proj, bit)
    for bit in bits_fc[1:-1]:
        w_fc = double(w_fc, bit)
    mixed, log_sums, parts = [], [], []
    for chunk in range(CHUNKS):
        mixed_one, sums_one = attend(core, qk, values, chunk, CHUNKS)
        if chunk > 0:
            mixed_one = after(mixed_one, w_proj, w_fc)
        mixed.append(mixed_one)
        log_sums.append(sums_one)
        parts.append(scatter_begin([rows2(mixed_one)], [w_out], NN))
    w_proj = rows2(double(after(w_proj, mixed[-1]), bits_proj[-1]))
    w_fc = rows2(double(after(w_fc, mixed[-1]), bits_fc[-1]))
    back_act = [mm(after(dy, parts[-1]), w_proj, NT).astype(BF16) for dy in dy_all]
    middles, mine_two, normed_two = [], [], []
    branches = [exchange(value) for value in parts]
    for chunk in range(CHUNKS):
        rows = rows_of[chunk]
        branch = branches[chunk]
        if chunk > 0:
            branch = after(branch, normed_two[-1])
        residual = jnp.concatenate([inputs[rows], inputs_four[1][rows]]).astype(F32)
        middle = residual + branch + bias_out
        unit_two, scale_two = norm_parts(middle)
        normed_two.append((unit_two * gain_two + shift_two).astype(BF16))
        middles.append(middle[:part])
        mine_two.append((unit_two, scale_two))

    acts, backs, wholes, parts = [], [], [], []
    grad_proj, grad_fc, fc_bias_grad = 0.0, 0.0, 0.0
    for chunk in range(CHUNKS):
        block = (normed_two[chunk], swap(normed_two[chunk], 1))
        if chunk > 0:
            block = after(block, parts[-1])
        act, back, sums, whole = hidden_layer(block, w_fc, bias_fc, back_act[chunk])
        parts.append(scatter_begin([after(back, branches[-1])], [w_fc], NT))
        act, back, whole = after((act, back, whole), parts[-1])
        grad_proj = grad_proj + mm(act, dy_all[chunk], TN)
        grad_fc = grad_fc + mm(whole, back, TN)
        acts.append(act)
        fc_bias_grad = fc_bias_grad + sums[0]
    half_proj = halve(spread(grad_proj.astype(BF16)), 1)
    half_fc = halve(spread(grad_fc.astype(BF16)), 2)

    back_middles, back_lows, back_mixed, mids = [], [], [], []
    gain_two_grad, shift_two_grad = 0.0, 0.0
    for chunk in range(CHUNKS):
        unit_two, scale_two = mine_two[chunk]
        grad = exchange(parts[chunk])
        if chunk > 0:
            grad = after(grad, back_lows[-1])
        dy = jnp.concatenate(dy_four[chunk][:2]).astype(F32)
        back_middle = dy + norm_back(unit_two, scale_two, gain_two, grad)
        back_lows.append(back_middle.astype(BF16))
        gain_two_grad = gain_two_grad + jnp.sum(grad[:part] * unit_two[:part], axis=0)
        shift_two_grad = shift_two_grad + jnp.sum(grad[:part], axis=0)
        back_middles.append(back_middle[:part])
        block = after((back_lows[-1], swap(back_lows[-1], 1)), parts[-1])
        mixed_grad, mid = back_mix(block, w_out)
        back_mixed.append(mixed_grad.reshape(2, 2, part, head_width))
        mids.append(mid)
    middle = jnp.concatenate(middles)
    back_middle = jnp.concatenate(back_middles)
    proj_bias_grad = jnp.sum(out_grad, axis=0, dtype=F32)
    out_bias_grad = jnp.sum(back_middle, axis=0)

    back_mixed, half_proj, half_fc = lax.optimization_barrier((back_mixed, half_proj, half_fc))
    steps = axis_bits("dp")
    rest_proj, rest_fc = steps[1:], steps[2:] + [1]
    half_proj = halve(half_proj, rest_proj[0])
    half_fc = halve(half_fc, rest_fc[0])
    attend_grad = attend_back(core, qk, values, mixed, log_sums, back_mixed, 0)
    back_mixed = after(back_mixed, half_proj, half_fc)
    back_qk, back_v = attend_back(core, qk, values, mixed, log_sums, back_mixed, 1, attend_grad)
    share_proj = halve_by(half_proj, rest_proj[1:])
    share_fc = halve_by(half_fc, rest_fc[1:])
    grad_out = sum(mm(rows2(mixed[i]), mids[i], TN) for i in range(CHUNKS)).astype(BF16)
    grad_out = grad_out.reshape(data_count, share_out, tensor_count, head_width)
    grad_out = jnp.swapaxes(grad_out, 1, 2).reshape(width, head_width)
    grad_qk = mm(normed_all, rows2(back_qk), TN).astype(BF16)
    grad_v = mm(normed_all, rows2(back_v), TN).astype(BF16)
    grad_vo = jnp.concatenate([grad_v, grad_out], axis=1)
    half_qk = halve(spread(grad_qk), 1)
    half_vo = halve(spread(grad_vo), 2)
    share_qk = halve_by(half_qk, steps[1:])
    share_vo = halve_by(half_vo, [1] + steps[2:])

    acts = after(acts, back_lows[-1])
    branches = [scatter_end(scatter_begin([act], [w_proj], NN)) for act in acts]
    block_out = (middle + jnp.concatenate(branches) + bias_proj).astype(BF16)
    late_qk, late_v = after((back_qk, back_v), grad_qk, grad_vo)
    back_normed = scatter_end(scatter_begin([rows2(late_qk), rows2(late_v)], [w_qk, w_v], NT))
    input_grad = back_middle + norm_back(unit_one, scale_one, gain_one, back_normed)
    gain_one_grad = jnp.sum(back_normed * unit_one, axis=0)
    shift_one_grad = jnp.sum(back_normed, axis=0)
    query_bias_grad = jnp.sum(late_qk[..., :head_width], axis=(0, 1, 2), dtype=F32)
    value_bias_grad = jnp.sum(late_v, axis=(0, 1, 2), dtype=F32)

    bundle = jnp.zeros((data_count, share, width), BF16)
    pieces = (
        jnp.concatenate(
            [
                rows2(share_qk),
                rows2(share_vo)[:, :head_width],
                jnp.zeros((share, width - 3 * head_width), BF16),
            ],
            axis=1,
        ),
        jnp.pad(rows2(share_vo)[:, head_width:], ((0, 0), (width - head_width, 0))),
        rows2(share_fc),
        rows2(share_proj),
    )
    for kind in range(4):
        bundle = lax.dynamic_update_index_in_dim(bundle, pieces[kind], owner_row[kind], 0)
    landed = lax.all_to_all(bundle, "dp", 0, 0)
    full_grad = jnp.concatenate(
        [
            gain_one_grad,
            shift_one_grad,
            jnp.zeros((2 * width,), F32),
            out_bias_grad,
            gain_two_grad,
            shift_two_grad,
            jnp.zeros((FF,), F32),
            proj_bias_grad,
        ]
    )
    for grad, start, size in (
        (query_bias_grad, 2 * width, head_width),
        (value_bias_grad, 3 * width, head_width),
        (fc_bias_grad, 7 * width, ff_width),
    ):
        full_grad = lax.dynamic_update_slice_in_dim(full_grad, grad, start + tensor_idx * size, 0)
    small_grad = small_scatter(full_grad)
    first_new = beta_one * small_first + (1.0 - beta_one) * small_grad
    second_new = beta_two * small_second + (1.0 - beta_two) * small_grad * small_grad
    first_hat = first_new / (1.0 - beta_one**STEP)
    second_hat = second_new / (1.0 - beta_two**STEP)
    small_new = small_master - adam_rate * first_hat / (jnp.sqrt(second_hat) + adam_eps)

    row_limit = jnp.where(owned[1], head_width, jnp.where(jnp.any(owned), width, 0))
    col_limit = jnp.where(owned[0], 3 * head_width, width)
    limits = jnp.stack([row_limit, col_limit, owned[1].astype(jnp.int32)]).astype(jnp.int32)
    grad_slot, mom_slot, fresh_slot = muon_update(
        limits, landed, momentum_slots[0], slot_value, share_out
    )
    return (
        block_out,
        input_grad,
        grad_slot[None],
        mom_slot[None],
        fresh_slot[None],
        small_grad,
        second_new,
        small_new,
    )


def solution(mesh):
    return jax.shard_map(
        per_device,
        mesh=mesh,
        in_specs=(
            P(("dp", "tensor"), None),
            P(("dp", "tensor"), None),
            P(),
            P("dp", "tensor", None),
            P("dp", "tensor", None),
            P(("dp", "tensor")),
            P(("dp", "tensor")),
            P(("dp", "tensor")),
        ),
        out_specs=(
            P(("dp", "tensor"), None),
            P(("dp", "tensor"), None),
            P("dp", "tensor", None),
            P("dp", "tensor", None),
            P("dp", "tensor", None),
            P(("dp", "tensor")),
            P(("dp", "tensor")),
            P(("dp", "tensor")),
        ),
        check_vma=False,
    )
```

```python
from functools import partial

import jax
import jax.numpy as jnp
from jax import lax
from jax.experimental import pallas as pl
from jax.experimental.pallas import tpu as pltpu
from jax.sharding import PartitionSpec as P

HEADS = 16
FF = 4096
SEQ = 1024
NS_STEPS = 5
STEP = 10
HEAD_DIM = 64

ln_eps = 1e-05
mom_decay = 0.95
ns_a = 3.4445
ns_b = -4.775
ns_c = 2.0315
muon_rate = 0.5
muon_decay = 0.01
beta_one = 0.9
beta_two = 0.95
adam_rate = 0.2
adam_eps = 1e-08
masked_score = -1e30
gelu_in = 0.7978845608028654
gelu_cube = 0.044715

CHUNKS = 2
TILE = 256
VMEM_GRANT = 48 * 1024 * 1024
BF16 = jnp.bfloat16
F32 = jnp.float32

NN = (((1,), (0,)), ((), ()))
NT = (((1,), (1,)), ((), ()))
TN = (((0,), (0,)), ((), ()))


def mm(left, right, dims=NN):
    return lax.dot_general(left, right, dims, preferred_element_type=F32)


def rows2(value):
    return value.reshape(-1, value.shape[-1])


def head_ids(shape):
    return lax.broadcasted_iota(jnp.int32, shape, 1) // HEAD_DIM


def causal_tile(tile):
    row = lax.broadcasted_iota(jnp.int32, (tile, tile), 0)
    col = lax.broadcasted_iota(jnp.int32, (tile, tile), 1)
    return row >= col


def attend_kernel(core_ref, q_ref, k_ref, v_ref, o_ref, lse_ref, *, subs, heads):
    core = core_ref[0]
    place = (core, 1 - core)
    width = q_ref.shape[-1]
    col_head = head_ids((TILE, width))
    lane = lax.broadcasted_iota(jnp.int32, (TILE, 128), 1)
    causal = causal_tile(TILE)
    per_half = k_ref.shape[2] // TILE
    for half in range(2):
        for at, sub in enumerate(subs):
            blk = per_half * half + sub
            rows = slice(at * TILE, (at + 1) * TILE)
            q_blk = q_ref[place[half], 0, rows, :]
            acc = jnp.zeros((TILE, width), F32)
            lse = jnp.zeros((TILE, 128), F32)
            for head in range(heads):
                q_one = jnp.where(col_head == head, q_blk, jnp.zeros_like(q_blk))
                scores = []
                for j in range(blk + 1):
                    cols = slice((j % per_half) * TILE, (j % per_half + 1) * TILE)
                    s = mm(q_one, k_ref[place[j // per_half], 0, cols, :], NT)
                    if j == blk:
                        s = jnp.where(causal, s, masked_score)
                    scores.append(s)
                top = scores[0]
                for s in scores[1:]:
                    top = jnp.maximum(top, s)
                top = jnp.max(top, axis=1, keepdims=True)
                total = jnp.zeros((TILE, TILE), F32)
                out = jnp.zeros((TILE, width), F32)
                for j in range(blk + 1):
                    cols = slice((j % per_half) * TILE, (j % per_half + 1) * TILE)
                    p = jnp.exp(scores[j] - top)
                    total = total + p
                    out = out + mm(p.astype(BF16), v_ref[place[j // per_half], 0, cols, :])
                total = jnp.sum(total, axis=1, keepdims=True)
                acc = jnp.where(col_head == head, out * (1.0 / total), acc)
                lse = jnp.where(lane == head, top + jnp.log(total), lse)
            o_ref[place[half], 0, rows, :] = acc.astype(BF16)
            lse_ref[place[half], 0, rows, :] = lse


def attend(core, qk, v, chunk, chunks):
    _, seqs, rows, width = v.shape
    part = rows // chunks
    per = part // TILE
    subs = tuple(range(chunk * per, (chunk + 1) * per))
    return pl.pallas_call(
        partial(attend_kernel, subs=subs, heads=width // HEAD_DIM),
        grid_spec=pltpu.PrefetchScalarGridSpec(
            num_scalar_prefetch=1,
            grid=(seqs,),
            in_specs=[
                pl.BlockSpec((2, 1, part, width), lambda s, c: (0, s, chunk, 0)),
                pl.BlockSpec((2, 1, rows, width), lambda s, c: (0, s, 0, 1)),
                pl.BlockSpec((2, 1, rows, width), lambda s, c: (0, s, 0, 0)),
            ],
            out_specs=[
                pl.BlockSpec((2, 1, part, width), lambda s, c: (0, s, 0, 0)),
                pl.BlockSpec((2, 1, part, 128), lambda s, c: (0, s, 0, 0)),
            ],
        ),
        out_shape=[
            jax.ShapeDtypeStruct((2, seqs, part, width), BF16),
            jax.ShapeDtypeStruct((2, seqs, part, 128), F32),
        ],
        compiler_params=pltpu.CompilerParams(vmem_limit_bytes=VMEM_GRANT),
        cost_estimate=pl.CostEstimate(
            flops=10 * 10**9 // chunks, bytes_accessed=6 * 10**6, transcendentals=0
        ),
    )(core, qk, qk, v)


def attend_back_kernel(
    core_ref, q_ref, k_ref, v_ref, *refs, heads, chunks
):
    o_refs = refs[0:chunks]
    lse_refs = refs[chunks : 2 * chunks]
    do_refs = refs[2 * chunks : 3 * chunks]
    out_ref, v_out_ref, dk_acc, dv_acc = refs[-4:]
    core = core_ref[0]
    place = (core, 1 - core)
    width = q_ref.shape[-1]
    col_head = head_ids((TILE, width))
    causal = causal_tile(TILE)
    per_half = k_ref.shape[2] // TILE
    per_chunk = per_half // chunks
    dk_acc[...] = jnp.zeros_like(dk_acc)
    dv_acc[...] = jnp.zeros_like(dv_acc)
    for half in range(2):
        for sub in range(per_half):
            blk = per_half * half + sub
            rows = slice(sub * TILE, (sub + 1) * TILE)
            inner = slice((sub % per_chunk) * TILE, (sub % per_chunk + 1) * TILE)
            q_blk = q_ref[place[half], 0, rows, :]
            do_blk = do_refs[sub // per_chunk][place[half], 0, inner, :]
            o_blk = o_refs[sub // per_chunk][place[half], 0, inner, :]
            lse_blk = lse_refs[sub // per_chunk][place[half], 0, inner, :]
            overlap = do_blk.astype(F32) * o_blk.astype(F32)
            q_all, do_all, lse_all, delta_all = [], [], [], []
            for head in range(heads):
                mine = col_head == head
                q_all.append(jnp.where(mine, q_blk, jnp.zeros_like(q_blk)))
                do_all.append(jnp.where(mine, do_blk, jnp.zeros_like(do_blk)))
                lse_all.append(lse_blk[:, head : head + 1])
                delta_all.append(jnp.sum(jnp.where(mine, overlap, 0.0), axis=1, keepdims=True))
            q_cat = jnp.concatenate(q_all, axis=0)
            do_cat = jnp.concatenate(do_all, axis=0)
            dq = [jnp.zeros((TILE, width), F32) for _ in range(heads)]
            for j in range(blk + 1):
                cols = slice((j % per_half) * TILE, (j % per_half + 1) * TILE)
                k_blk = k_ref[place[j // per_half], 0, cols, :]
                v_blk = v_ref[place[j // per_half], 0, cols, :]
                p_all, ds_all = [], []
                for head in range(heads):
                    p = jnp.exp(mm(q_all[head], k_blk, NT) - lse_all[head])
                    if j == blk:
                        p = jnp.where(causal, p, 0.0)
                    dp = mm(do_all[head], v_blk, NT)
                    ds = (p * (dp - delta_all[head])).astype(BF16)
                    dq[head] = dq[head] + mm(ds, k_blk)
                    p_all.append(p.astype(BF16))
                    ds_all.append(ds)
                dk_acc[j] += mm(jnp.concatenate(ds_all, axis=0), q_cat, TN)
                dv_acc[j] += mm(jnp.concatenate(p_all, axis=0), do_cat, TN)
            total = dq[0]
            for head in range(1, heads):
                total = jnp.where(col_head == head, dq[head], total)
            out_ref[place[half], 0, rows, 0:width] = (total * HEAD_DIM**-0.5).astype(BF16)
    for j in range(2 * per_half):
        rows = slice((j % per_half) * TILE, (j % per_half + 1) * TILE)
        out_ref[place[j // per_half], 0, rows, width : 2 * width] = dk_acc[j].astype(BF16)
        v_out_ref[place[j // per_half], 0, rows, :] = dv_acc[j].astype(BF16)


def attend_back(core, qk, v, outs, lses, back, seq, before=()):
    _, _, rows, width = v.shape
    chunks = len(outs)
    part = rows // chunks

    def block(size, cols, at):
        return pl.BlockSpec((2, 1, size, cols), lambda s, c: (0, seq, 0, at))

    operands = (core, qk, qk, v, *outs, *lses, *back)
    return pl.pallas_call(
        partial(attend_back_kernel, heads=width // HEAD_DIM, chunks=chunks),
        grid_spec=pltpu.PrefetchScalarGridSpec(
            num_scalar_prefetch=1,
            grid=(1,),
            in_specs=[block(rows, width, 0), block(rows, width, 1), block(rows, width, 0)]
            + [block(part, width, 0)] * chunks
            + [block(part, 128, 0)] * chunks
            + [block(part, width, 0)] * chunks
            + [pl.BlockSpec(memory_space=pl.ANY)] * len(before),
            out_specs=[block(rows, 2 * width, 0), block(rows, width, 0)],
            scratch_shapes=[pltpu.VMEM((2 * rows // TILE, TILE, width), F32)] * 2,
        ),
        out_shape=[jax.ShapeDtypeStruct(qk.shape, BF16), jax.ShapeDtypeStruct(v.shape, BF16)],
        input_output_aliases={len(operands) + i: i for i in range(len(before))},
        compiler_params=pltpu.CompilerParams(vmem_limit_bytes=VMEM_GRANT),
        cost_estimate=pl.CostEstimate(
            flops=12 * 10**9, bytes_accessed=6 * 10**6, transcendentals=0
        ),
    )(*operands, *before)


def hidden_kernel(*refs):
    blocks = refs[:-7]
    w_ref, bias_ref, dact_ref, act_ref, back_ref, sum_ref, all_ref = refs[-7:]
    rows = blocks[0].shape[0]
    value = jnp.concatenate([block[...] for block in blocks], axis=0)
    hidden = mm(value, w_ref[...]) + bias_ref[...]
    square = hidden * hidden
    bent = jnp.tanh(gelu_in * hidden * (1.0 + gelu_cube * square))
    half = 0.5 * (1.0 + bent)
    act_ref[...] = (hidden * half).astype(BF16)
    slope = half + 0.5 * hidden * (1.0 - bent * bent) * (
        gelu_in * (1.0 + 3.0 * gelu_cube * square)
    )
    back = (dact_ref[...].astype(F32) * slope).astype(BF16)
    back_ref[...] = back
    sum_ref[...] = jnp.sum(back.astype(F32), axis=0, keepdims=True)

    @pl.when(pl.program_id(0) == 0)
    def _():
        for at in range(len(blocks)):
            all_ref[at * rows : (at + 1) * rows, :] = blocks[at][...]


def hidden_layer(blocks, weight, bias, dact):
    rows, width = blocks[0].shape
    cols = weight.shape[1]
    total = len(blocks) * rows
    tile = min(256, cols)
    whole = pl.BlockSpec((rows, width), lambda n: (0, 0))
    column = pl.BlockSpec((total, tile), lambda n: (0, n))
    return pl.pallas_call(
        hidden_kernel,
        grid=(cols // tile,),
        in_specs=[whole] * len(blocks)
        + [
            pl.BlockSpec((width, tile), lambda n: (0, n)),
            pl.BlockSpec((1, tile), lambda n: (0, n)),
            column,
        ],
        out_specs=[
            column,
            column,
            pl.BlockSpec((1, tile), lambda n: (0, n)),
            pl.BlockSpec((total, width), lambda n: (0, 0)),
        ],
        out_shape=[
            jax.ShapeDtypeStruct((total, cols), BF16),
            jax.ShapeDtypeStruct((total, cols), BF16),
            jax.ShapeDtypeStruct((1, cols), F32),
            jax.ShapeDtypeStruct((total, width), BF16),
        ],
        compiler_params=pltpu.CompilerParams(vmem_limit_bytes=VMEM_GRANT),
        cost_estimate=pl.CostEstimate(
            flops=2 * total * width * cols, bytes_accessed=12 * 10**6, transcendentals=0
        ),
    )(*blocks, weight, bias.reshape(1, -1), dact)


def mixed_kernel(*refs):
    blocks = refs[:-3]
    w_ref, out_ref, all_ref = refs[-3:]
    rows = blocks[0].shape[0]
    for at in range(len(blocks)):
        value = blocks[at][...]
        out_ref[at * rows : (at + 1) * rows, :] = mm(value, w_ref[...], NT).astype(BF16)
        all_ref[at * rows : (at + 1) * rows, :] = value


def back_mix(blocks, weight):
    rows, width = blocks[0].shape
    cols = weight.shape[0]
    total = len(blocks) * rows
    return pl.pallas_call(
        mixed_kernel,
        in_specs=[pl.BlockSpec(memory_space=pltpu.VMEM)] * (len(blocks) + 1),
        out_specs=[pl.BlockSpec(memory_space=pltpu.VMEM)] * 2,
        out_shape=[
            jax.ShapeDtypeStruct((total, cols), BF16),
            jax.ShapeDtypeStruct((total, width), BF16),
        ],
        compiler_params=pltpu.CompilerParams(vmem_limit_bytes=VMEM_GRANT),
        cost_estimate=pl.CostEstimate(
            flops=2 * total * width * cols, bytes_accessed=5 * 10**6, transcendentals=0
        ),
    )(*blocks, weight)


def muon_kernel(
    limit_ref,
    landed_ref,
    mom_hbm,
    master_hbm,
    grad_out,
    mom_out,
    master_out,
    grad_buf,
    mom_buf,
    master_buf,
    x_buf,
    gram,
    poly,
    sems,
    *,
    out_rows,
):
    count, share, size = landed_ref.shape
    tile = 512
    tiles = size // tile
    load_mom = pltpu.make_async_copy(mom_hbm, mom_buf, sems.at[0])
    load_master = pltpu.make_async_copy(master_hbm, master_buf, sems.at[1])
    store_grad = pltpu.make_async_copy(grad_buf, grad_out, sems.at[2])
    store_mom = pltpu.make_async_copy(mom_buf, mom_out, sems.at[3])
    store_master = pltpu.make_async_copy(master_buf, master_out, sems.at[4])
    load_mom.start()
    load_master.start()
    row_limit = limit_ref[0]
    col_limit = limit_ref[1]
    is_out = limit_ref[2] == 1

    @pl.when(is_out)
    def _():
        grad_buf[...] = jnp.zeros_like(grad_buf)
        for src in range(count):
            cols = size * out_rows // share
            piece = landed_ref[src].astype(F32)[:, size - cols :]
            for at in range(share // out_rows):
                grad_buf[
                    src * out_rows : (src + 1) * out_rows, at * cols : (at + 1) * cols
                ] = piece[at * out_rows : (at + 1) * out_rows]

    @pl.when(jnp.logical_not(is_out))
    def _():
        for src in range(count):
            grad_buf[src * share : (src + 1) * share, :] = landed_ref[src].astype(F32)

    store_grad.start()
    load_mom.wait()
    block = 128

    def valid(r):
        row = lax.broadcasted_iota(jnp.int32, (block, size), 0) + r * block
        col = lax.broadcasted_iota(jnp.int32, (block, size), 1)
        return (row < row_limit) & (col < col_limit)

    def at_rows(r, step):
        return pl.ds(pl.multiple_of(r * step, step), step)

    def momentum_rows(r, total):
        rows = at_rows(r, block)
        value = jnp.where(valid(r), mom_decay * mom_buf[rows, :] + grad_buf[rows, :], 0.0)
        mom_buf[rows, :] = value
        return total + value * value

    total = lax.fori_loop(0, size // block, momentum_rows, jnp.zeros((block, size), F32))
    store_mom.start()
    scale = 1.0 / (jnp.sqrt(jnp.sum(total)) + 1e-07)

    def first_rows(r, carry):
        rows = at_rows(r, block)
        x_buf[0, rows, :] = (mom_buf[rows, :] * scale).astype(BF16)
        return carry

    lax.fori_loop(0, size // block, first_rows, 0)

    def one_turn(turn, carry):
        now = lax.rem(turn, 2)
        later = 1 - now

        for r in range(size // TILE):
            rows, rest = slice(r * TILE, (r + 1) * TILE), slice(r * TILE, size)
            value = mm(x_buf[now, rows, :], x_buf[now, rest, :], NT).astype(BF16)
            gram[rows, rest] = value
            for c in range(r + 1, size // TILE):
                block_rows = slice(c * TILE, (c + 1) * TILE)
                gram[block_rows, rows] = value[:, (c - r) * TILE : (c - r + 1) * TILE].T

        for r in range(size // TILE):
            rows, rest = slice(r * TILE, (r + 1) * TILE), slice(r * TILE, size)
            square = mm(gram[rows, :], gram[:, rest])
            value = (ns_b * gram[rows, rest].astype(F32) + ns_c * square).astype(BF16)
            poly[rows, rest] = value
            for c in range(r + 1, size // TILE):
                block_rows = slice(c * TILE, (c + 1) * TILE)
                poly[block_rows, rows] = value[:, (c - r) * TILE : (c - r + 1) * TILE].T

        def next_rows(r, c):
            rows = at_rows(r, tile)
            x_buf[later, rows, :] = (
                ns_a * x_buf[now, rows, :].astype(F32) + mm(poly[rows, :], x_buf[now])
            ).astype(BF16)
            return c

        lax.fori_loop(0, tiles, next_rows, 0)
        return carry

    lax.fori_loop(0, jnp.where(row_limit > 0, NS_STEPS, 0), one_turn, 0)
    load_master.wait()

    def master_rows(r, carry):
        rows = at_rows(r, block)
        ortho = x_buf[NS_STEPS % 2, rows, :].astype(F32)
        fresh = master_buf[rows, :] * (1.0 - muon_rate * muon_decay) - muon_rate * ortho
        master_buf[rows, :] = jnp.where(valid(r), fresh, 0.0)
        return carry

    lax.fori_loop(0, size // block, master_rows, 0)
    store_master.start()
    store_grad.wait()
    store_mom.wait()
    store_master.wait()


def muon_update(limits, landed, momentum, master, out_rows):
    size = momentum.shape[0]
    shape = jax.ShapeDtypeStruct((size, size), F32)
    anywhere = pl.BlockSpec(memory_space=pl.ANY)
    return pl.pallas_call(
        partial(muon_kernel, out_rows=out_rows),
        in_specs=[
            pl.BlockSpec(memory_space=pltpu.SMEM),
            pl.BlockSpec(memory_space=pltpu.VMEM),
            anywhere,
            anywhere,
        ],
        out_specs=[anywhere] * 3,
        out_shape=[shape] * 3,
        scratch_shapes=[
            pltpu.VMEM((size, size), F32),
            pltpu.VMEM((size, size), F32),
            pltpu.VMEM((size, size), F32),
            pltpu.VMEM((2, size, size), BF16),
            pltpu.VMEM((size, size), BF16),
            pltpu.VMEM((size, size), BF16),
            pltpu.SemaphoreType.DMA((5,)),
        ],
        compiler_params=pltpu.CompilerParams(vmem_limit_bytes=VMEM_GRANT),
        cost_estimate=pl.CostEstimate(
            flops=6 * NS_STEPS * size**3, bytes_accessed=22 * size * size, transcendentals=0
        ),
    )(limits, landed, momentum, master)


def swap(value, bit):
    count = lax.axis_size("tensor")
    return lax.ppermute(value, "tensor", [(i, i ^ bit) for i in range(count)])


def gather_four(value):
    core_block = swap(value, 1)
    far_block = swap(value, 2)
    return value, far_block, core_block, swap(far_block, 1)


def scatter_begin(values, weights, dims):
    size = values[0].shape[0] // 4

    def product(first, last):
        return sum(mm(v[first * size : last * size], w, dims) for v, w in zip(values, weights))

    arrived = swap(product(2, 4).astype(BF16), 1)
    return product(0, 2) + arrived.astype(F32)


def scatter_end(part):
    size = part.shape[0] // 2
    return part[:size] + swap(part[size:].astype(BF16), 2).astype(F32)


def exchange(part):
    size = part.shape[0] // 2
    given = part.astype(BF16)
    given = jnp.concatenate([given[size:], given[:size]])
    return part + swap(given, 2).astype(F32)


def data_swap(value, bit):
    count = lax.axis_size("dp")
    return lax.ppermute(value, "dp", [(i, i ^ bit) for i in range(count)])


def after(value, *others):
    return lax.optimization_barrier((value, *others))[0]


def last_bits(*bits):
    return [bit for bit in reversed(axis_bits("dp")) if bit not in bits] + list(bits)


def bit_axis(bit):
    return len(axis_bits("dp")) - bit.bit_length()


def spread(value):
    return value.reshape((2,) * len(axis_bits("dp")) + (-1, value.shape[-1]))


def double(piece, bit):
    upper = (lax.axis_index("dp") & bit) != 0
    other = data_swap(piece, bit)
    axis = bit_axis(bit)
    return jnp.where(
        upper,
        jnp.concatenate([other, piece], axis=axis),
        jnp.concatenate([piece, other], axis=axis),
    )


def open_piece(value):
    return value.reshape((1,) * len(axis_bits("dp")) + value.shape)


def gather_by(value, bits):
    piece = open_piece(value)
    for bit in bits:
        piece = double(piece, bit)
    return rows2(piece)


def halve(value, bit):
    upper = ((lax.axis_index("dp") & bit) != 0).astype(jnp.int32)
    axis = bit_axis(bit)
    give = lax.dynamic_slice_in_dim(value, 1 - upper, 1, axis)
    keep = lax.dynamic_slice_in_dim(value, upper, 1, axis)
    return (keep.astype(F32) + data_swap(give, bit).astype(F32)).astype(BF16)


def halve_by(value, bits):
    for bit in bits:
        value = halve(value, bit)
    return value


def axis_bits(name):
    count = lax.axis_size(name)
    bits = []
    bit = 1
    while bit < count:
        bits.append(bit)
        bit *= 2
    return bits


def small_gather(piece, name, axis):
    index = lax.axis_index(name)
    count = lax.axis_size(name)
    for bit in axis_bits(name):
        other = lax.ppermute(piece, name, [(i, i ^ bit) for i in range(count)])
        upper = (index & bit) != 0
        piece = jnp.where(
            upper,
            jnp.concatenate([other, piece], axis=axis),
            jnp.concatenate([piece, other], axis=axis),
        )
    return piece


def small_scatter(value):
    value = value.reshape(lax.axis_size("dp"), -1)
    for name, axis in (("tensor", 1), ("dp", 0)):
        index = lax.axis_index(name)
        count = lax.axis_size(name)
        for bit in reversed(axis_bits(name)):
            low, high = jnp.split(value, 2, axis=axis)
            upper = (index & bit) != 0
            give = jnp.where(upper, low, high)
            keep = jnp.where(upper, high, low)
            value = keep + lax.ppermute(give, name, [(i, i ^ bit) for i in range(count)])
    return value.reshape(-1)


def norm_parts(values):
    centred = values - jnp.mean(values, axis=-1, keepdims=True)
    spread = jnp.mean(centred * centred, axis=-1, keepdims=True)
    scale = lax.rsqrt(spread + ln_eps)
    return centred * scale, scale


def norm_back(unit, scale, gain_vec, grad):
    inner = grad * gain_vec
    return scale * (
        inner
        - jnp.mean(inner, axis=-1, keepdims=True)
        - unit * jnp.mean(inner * unit, axis=-1, keepdims=True)
    )


def per_device(
    inputs, out_grad, owners, master_slots, momentum_slots, small_master, small_first, small_second
):
    rows_dev, width = inputs.shape
    tensor_count = lax.axis_size("tensor")
    data_count = lax.axis_size("dp")
    tensor_idx = lax.axis_index("tensor")
    data_idx = lax.axis_index("dp")
    head_width = width // tensor_count
    ff_width = FF // tensor_count
    share = width // data_count
    share_out = head_width // data_count
    core = jnp.reshape(tensor_idx & 1, (1,)).astype(jnp.int32)
    owner_row = lax.dynamic_index_in_dim(owners, tensor_idx, 0, keepdims=False)
    owned = owner_row == data_idx
    slot_value = master_slots[0]

    group_params = small_gather(small_master.reshape(1, -1), "tensor", 1)
    params = small_gather(group_params, "dp", 0)
    slot_low = slot_value.astype(BF16)
    offer_out = slot_low[:head_width].reshape(data_count, share_out, tensor_count, head_width)
    offer_out = jnp.swapaxes(offer_out, 1, 2).reshape(data_count, share, head_width)
    offer_out = jnp.pad(offer_out, ((0, 0), (0, 0), (width - head_width, 0)))
    offer = jnp.where(owned[1], offer_out, slot_low.reshape(data_count, share, width))
    shares = lax.all_to_all(after(offer, params), "dp", 0, 0)
    params = params.reshape(-1)

    def own_slice(start, size):
        return lax.dynamic_slice_in_dim(params, start + tensor_idx * size, size, 0)

    gain_one = params[0:width]
    shift_one = params[width : 2 * width]
    bias_query = own_slice(2 * width, head_width)
    bias_value = own_slice(3 * width, head_width)
    bias_out = params[4 * width : 5 * width]
    gain_two = params[5 * width : 6 * width]
    shift_two = params[6 * width : 7 * width]
    bias_fc = own_slice(7 * width, ff_width)
    bias_proj = params[7 * width + FF :]

    part = rows_dev // CHUNKS
    rows_of = [slice(chunk * part, (chunk + 1) * part) for chunk in range(CHUNKS)]
    rows_in = inputs.astype(F32)
    unit_one, scale_one = norm_parts(rows_in)
    inputs_four = gather_four(after(inputs, group_params))
    unit_all, _ = norm_parts(jnp.concatenate(inputs_four).astype(F32))
    normed_all = (unit_all * gain_one + shift_one).astype(BF16)
    dy_four = [gather_four(after(out_grad[rows], inputs_four[1])) for rows in rows_of]
    dy_all = [jnp.concatenate(four) for four in dy_four]

    shares = after(shares, normed_all, *dy_all)

    def share_of(kind):
        return lax.dynamic_index_in_dim(shares, owner_row[kind], 0, keepdims=False)

    split = 2 * head_width
    first = share_of(0)
    piece_vo = jnp.concatenate(
        [first[:, split : split + head_width], share_of(1)[:, width - head_width :]], axis=1
    )
    bits_qk, bits_vo = last_bits(2, 1), last_bits(1, 2)
    one_qk = double(open_piece(first[:, :split]), bits_qk[0])
    one_vo = double(open_piece(piece_vo), bits_vo[0])
    w_qk, w_vo = one_qk, one_vo
    for bit in bits_qk[1:]:
        w_qk = double(w_qk, bit)
    for bit in bits_vo[1:]:
        w_vo = double(w_vo, bit)
    w_qk, w_vo = rows2(w_qk), rows2(w_vo)
    w_v = w_vo[:, :head_width]
    w_out = w_vo[:, head_width:].reshape(data_count, tensor_count, share_out, head_width)
    w_out = jnp.swapaxes(w_out, 1, 2).reshape(head_width, width)
    bits_proj = last_bits(1, 2)
    bits_fc = last_bits(2, 1)
    w_proj = double(open_piece(after(share_of(3), one_qk, one_vo)), bits_proj[0])
    w_fc = double(open_piece(after(share_of(2), w_proj)), bits_fc[0])
    bias_qk = jnp.concatenate([bias_query, jnp.zeros_like(bias_query)])
    scale_qk = jnp.where(jnp.arange(split) < head_width, HEAD_DIM**-0.5, 1.0)
    qk = ((mm(normed_all, w_qk) + bias_qk) * scale_qk).astype(BF16)
    values = (mm(normed_all, w_v) + bias_value).astype(BF16)
    qk = qk.reshape(2, 2, rows_dev, split)
    values = values.reshape(2, 2, rows_dev, head_width)

    first_steps = (w_proj, w_fc)
    for bit in bits_proj[1:-1]:
        w_proj = double(w_proj, bit)
    for bit in bits_fc[1:-1]:
        w_fc = double(w_fc, bit)
    mixed, log_sums, parts = [], [], []
    for chunk in range(CHUNKS):
        late = (qk, values) if chunk == 0 else after((qk, values), *first_steps)
        mixed_one, sums_one = attend(core, *late, chunk, CHUNKS)
        if chunk > 0:
            mixed_one = after(mixed_one, w_proj, w_fc)
        mixed.append(mixed_one)
        log_sums.append(sums_one)
        parts.append(scatter_begin([rows2(mixed_one)], [w_out], NN))
    w_proj = rows2(double(after(w_proj, mixed[-1]), bits_proj[-1]))
    w_fc = rows2(double(after(w_fc, mixed[-1]), bits_fc[-1]))
    back_act = [mm(after(dy, parts[-1]), w_proj, NT).astype(BF16) for dy in dy_all]
    middles, mine_two, normed_two = [], [], []
    branches = [exchange(value) for value in parts]
    for chunk in range(CHUNKS):
        rows = rows_of[chunk]
        branch = branches[chunk]
        if chunk > 0:
            branch = after(branch, normed_two[-1])
        residual = jnp.concatenate([inputs[rows], inputs_four[1][rows]]).astype(F32)
        middle = residual + branch + bias_out
        unit_two, scale_two = norm_parts(middle)
        normed_two.append((unit_two * gain_two + shift_two).astype(BF16))
        middles.append(middle[:part])
        mine_two.append((unit_two, scale_two))

    acts, backs, wholes, parts, sums_two = [], [], [], [], []
    grad_proj, grad_fc, fc_bias_grad = 0.0, 0.0, 0.0
    for chunk in range(CHUNKS):
        block = (normed_two[chunk], swap(normed_two[chunk], 1))
        if chunk > 0:
            block = after(block, parts[-1])
        act, back, sums, whole = hidden_layer(block, w_fc, bias_fc, back_act[chunk])
        parts.append(scatter_begin([after(back, *sums_two)], [w_fc], NT))
        sums_two.append(exchange(parts[-1]))
        acts.append(act)
        backs.append(back)
        wholes.append(whole)
        fc_bias_grad = fc_bias_grad + sums[0]
    back_middles, back_lows, back_mixed, mids = [], [], [], []
    gain_two_grad, shift_two_grad = 0.0, 0.0
    for chunk in range(CHUNKS):
        unit_two, scale_two = mine_two[chunk]
        grad = after(sums_two[chunk], parts[-1], *back_lows[-1:])
        dy = jnp.concatenate(dy_four[chunk][:2]).astype(F32)
        back_middle = dy + norm_back(unit_two, scale_two, gain_two, grad)
        back_lows.append(back_middle.astype(BF16))
        gain_two_grad = gain_two_grad + jnp.sum(grad[:part] * unit_two[:part], axis=0)
        shift_two_grad = shift_two_grad + jnp.sum(grad[:part], axis=0)
        back_middles.append(back_middle[:part])
        block = after((back_lows[-1], swap(back_lows[-1], 1)), parts[-1])
        grad_rows = (acts[chunk], wholes[chunk], backs[chunk])
        act, whole, back = after(grad_rows, parts[0] if chunk == 0 else back_lows[0])
        grad_proj = grad_proj + mm(act, dy_all[chunk], TN)
        grad_fc = grad_fc + mm(whole, back, TN)
        mixed_grad, mid = back_mix(block, w_out)
        back_mixed.append(mixed_grad.reshape(2, 2, part, head_width))
        mids.append(mid)
    middle = jnp.concatenate(middles)
    back_middle = jnp.concatenate(back_middles)
    proj_bias_grad = jnp.sum(out_grad, axis=0, dtype=F32)
    out_bias_grad = jnp.sum(back_middle, axis=0)

    grad_proj, grad_fc = grad_proj.astype(BF16), grad_fc.astype(BF16)
    half_proj = halve(spread(grad_proj), 1)
    half_fc = halve(spread(grad_fc), 2)
    back_mixed, half_proj, half_fc = lax.optimization_barrier((back_mixed, half_proj, half_fc))
    steps = axis_bits("dp")
    rest_proj, rest_fc = steps[1:], steps[2:] + [1]
    half_proj = halve(half_proj, rest_proj[0])
    half_fc = halve(half_fc, rest_fc[0])
    attend_grad = attend_back(core, qk, values, mixed, log_sums, back_mixed, 0)
    back_mixed = after(back_mixed, half_proj, half_fc)
    back_qk, back_v = attend_back(core, qk, values, mixed, log_sums, back_mixed, 1, attend_grad)
    share_proj = halve_by(half_proj, rest_proj[1:])
    share_fc = halve_by(half_fc, rest_fc[1:])
    grad_out = sum(mm(rows2(mixed[i]), mids[i], TN) for i in range(CHUNKS)).astype(BF16)
    grad_out = grad_out.reshape(data_count, share_out, tensor_count, head_width)
    grad_out = jnp.swapaxes(grad_out, 1, 2).reshape(width, head_width)
    grad_qk = mm(normed_all, rows2(back_qk), TN).astype(BF16)
    grad_v = mm(normed_all, rows2(back_v), TN).astype(BF16)
    grad_vo = jnp.concatenate([grad_v, grad_out], axis=1)
    half_qk = halve(spread(grad_qk), 1)
    half_vo = halve(spread(grad_vo), 2)
    share_qk = halve_by(half_qk, steps[1:])
    share_vo = halve_by(half_vo, [1] + steps[2:])

    acts = after(acts, grad_qk)
    branches = [scatter_end(scatter_begin([act], [w_proj], NN)) for act in acts]
    block_out = (middle + jnp.concatenate(branches) + bias_proj).astype(BF16)
    late_qk, late_v = after((back_qk, back_v), grad_qk, grad_vo)
    back_normed = scatter_end(scatter_begin([rows2(late_qk), rows2(late_v)], [w_qk, w_v], NT))
    input_grad = back_middle + norm_back(unit_one, scale_one, gain_one, back_normed)
    gain_one_grad = jnp.sum(back_normed * unit_one, axis=0)
    shift_one_grad = jnp.sum(back_normed, axis=0)
    query_bias_grad = jnp.sum(late_qk[..., :head_width], axis=(0, 1, 2), dtype=F32)
    value_bias_grad = jnp.sum(late_v, axis=(0, 1, 2), dtype=F32)

    bundle = jnp.zeros((data_count, share, width), BF16)
    pieces = (
        jnp.concatenate(
            [
                rows2(share_qk),
                rows2(share_vo)[:, :head_width],
                jnp.zeros((share, width - 3 * head_width), BF16),
            ],
            axis=1,
        ),
        jnp.pad(rows2(share_vo)[:, head_width:], ((0, 0), (width - head_width, 0))),
        rows2(share_fc),
        rows2(share_proj),
    )
    for kind in range(4):
        bundle = lax.dynamic_update_index_in_dim(bundle, pieces[kind], owner_row[kind], 0)
    landed = lax.all_to_all(bundle, "dp", 0, 0)
    full_grad = jnp.concatenate(
        [
            gain_one_grad,
            shift_one_grad,
            jnp.zeros((2 * width,), F32),
            out_bias_grad,
            gain_two_grad,
            shift_two_grad,
            jnp.zeros((FF,), F32),
            proj_bias_grad,
        ]
    )
    for grad, start, size in (
        (query_bias_grad, 2 * width, head_width),
        (value_bias_grad, 3 * width, head_width),
        (fc_bias_grad, 7 * width, ff_width),
    ):
        full_grad = lax.dynamic_update_slice_in_dim(full_grad, grad, start + tensor_idx * size, 0)
    small_grad = small_scatter(full_grad)
    first_new = beta_one * small_first + (1.0 - beta_one) * small_grad
    second_new = beta_two * small_second + (1.0 - beta_two) * small_grad * small_grad
    first_hat = first_new / (1.0 - beta_one**STEP)
    second_hat = second_new / (1.0 - beta_two**STEP)
    small_new = small_master - adam_rate * first_hat / (jnp.sqrt(second_hat) + adam_eps)

    row_limit = jnp.where(owned[1], head_width, jnp.where(jnp.any(owned), width, 0))
    col_limit = jnp.where(owned[0], 3 * head_width, width)
    limits = jnp.stack([row_limit, col_limit, owned[1].astype(jnp.int32)]).astype(jnp.int32)
    grad_slot, mom_slot, fresh_slot = muon_update(
        limits, landed, momentum_slots[0], slot_value, share_out
    )
    return (
        block_out,
        input_grad,
        grad_slot[None],
        mom_slot[None],
        fresh_slot[None],
        small_grad,
        second_new,
        small_new,
    )


def solution(mesh):
    return jax.shard_map(
        per_device,
        mesh=mesh,
        in_specs=(
            P(("dp", "tensor"), None),
            P(("dp", "tensor"), None),
            P(),
            P("dp", "tensor", None),
            P("dp", "tensor", None),
            P(("dp", "tensor")),
            P(("dp", "tensor")),
            P(("dp", "tensor")),
        ),
        out_specs=(
            P(("dp", "tensor"), None),
            P(("dp", "tensor"), None),
            P("dp", "tensor", None),
            P("dp", "tensor", None),
            P("dp", "tensor", None),
            P(("dp", "tensor")),
            P(("dp", "tensor")),
            P(("dp", "tensor")),
        ),
        check_vma=False,
    )
```

```python
from functools import partial

import jax
import jax.numpy as jnp
from jax import lax
from jax.experimental import pallas as pl
from jax.experimental.pallas import tpu as pltpu
from jax.sharding import PartitionSpec as P

HEADS = 16
FF = 4096
SEQ = 1024
NS_STEPS = 5
STEP = 10
HEAD_DIM = 64

ln_eps = 1e-05
mom_decay = 0.95
ns_a = 3.4445
ns_b = -4.775
ns_c = 2.0315
muon_rate = 0.5
muon_decay = 0.01
beta_one = 0.9
beta_two = 0.95
adam_rate = 0.2
adam_eps = 1e-08
masked_score = -1e30
gelu_in = 0.7978845608028654
gelu_cube = 0.044715

CHUNKS = 2
TILE = 256
VMEM_GRANT = 48 * 1024 * 1024
BF16 = jnp.bfloat16
F32 = jnp.float32

NN = (((1,), (0,)), ((), ()))
NT = (((1,), (1,)), ((), ()))
TN = (((0,), (0,)), ((), ()))


def mm(left, right, dims=NN):
    return lax.dot_general(left, right, dims, preferred_element_type=F32)


def rows2(value):
    return value.reshape(-1, value.shape[-1])


def head_ids(shape):
    return lax.broadcasted_iota(jnp.int32, shape, 1) // HEAD_DIM


def causal_tile(tile):
    row = lax.broadcasted_iota(jnp.int32, (tile, tile), 0)
    col = lax.broadcasted_iota(jnp.int32, (tile, tile), 1)
    return row >= col


def attend_kernel(core_ref, q_ref, k_ref, v_ref, o_ref, lse_ref, *, subs, heads):
    core = core_ref[0]
    place = (core, 1 - core)
    width = q_ref.shape[-1]
    col_head = head_ids((TILE, width))
    lane = lax.broadcasted_iota(jnp.int32, (TILE, 128), 1)
    causal = causal_tile(TILE)
    per_half = k_ref.shape[2] // TILE
    for half in range(2):
        for at, sub in enumerate(subs):
            blk = per_half * half + sub
            rows = slice(at * TILE, (at + 1) * TILE)
            q_blk = q_ref[place[half], 0, rows, :]
            acc = jnp.zeros((TILE, width), F32)
            lse = jnp.zeros((TILE, 128), F32)
            for head in range(heads):
                q_one = jnp.where(col_head == head, q_blk, jnp.zeros_like(q_blk))
                scores = []
                for j in range(blk + 1):
                    cols = slice((j % per_half) * TILE, (j % per_half + 1) * TILE)
                    s = mm(q_one, k_ref[place[j // per_half], 0, cols, :], NT)
                    if j == blk:
                        s = jnp.where(causal, s, masked_score)
                    scores.append(s)
                top = scores[0]
                for s in scores[1:]:
                    top = jnp.maximum(top, s)
                top = jnp.max(top, axis=1, keepdims=True)
                total = jnp.zeros((TILE, TILE), F32)
                out = jnp.zeros((TILE, width), F32)
                for j in range(blk + 1):
                    cols = slice((j % per_half) * TILE, (j % per_half + 1) * TILE)
                    p = jnp.exp(scores[j] - top)
                    total = total + p
                    out = out + mm(p.astype(BF16), v_ref[place[j // per_half], 0, cols, :])
                total = jnp.sum(total, axis=1, keepdims=True)
                acc = jnp.where(col_head == head, out * (1.0 / total), acc)
                lse = jnp.where(lane == head, top + jnp.log(total), lse)
            o_ref[place[half], 0, rows, :] = acc.astype(BF16)
            lse_ref[place[half], 0, rows, :] = lse


def attend(core, qk, v, chunk, chunks):
    _, seqs, rows, width = v.shape
    part = rows // chunks
    per = part // TILE
    subs = tuple(range(chunk * per, (chunk + 1) * per))
    return pl.pallas_call(
        partial(attend_kernel, subs=subs, heads=width // HEAD_DIM),
        grid_spec=pltpu.PrefetchScalarGridSpec(
            num_scalar_prefetch=1,
            grid=(seqs,),
            in_specs=[
                pl.BlockSpec((2, 1, part, width), lambda s, c: (0, s, chunk, 0)),
                pl.BlockSpec((2, 1, rows, width), lambda s, c: (0, s, 0, 1)),
                pl.BlockSpec((2, 1, rows, width), lambda s, c: (0, s, 0, 0)),
            ],
            out_specs=[
                pl.BlockSpec((2, 1, part, width), lambda s, c: (0, s, 0, 0)),
                pl.BlockSpec((2, 1, part, 128), lambda s, c: (0, s, 0, 0)),
            ],
        ),
        out_shape=[
            jax.ShapeDtypeStruct((2, seqs, part, width), BF16),
            jax.ShapeDtypeStruct((2, seqs, part, 128), F32),
        ],
        compiler_params=pltpu.CompilerParams(vmem_limit_bytes=VMEM_GRANT),
        cost_estimate=pl.CostEstimate(
            flops=10 * 10**9 // chunks, bytes_accessed=6 * 10**6, transcendentals=0
        ),
    )(core, qk, qk, v)


def attend_back_kernel(
    core_ref, q_ref, k_ref, v_ref, *refs, heads, chunks
):
    o_refs = refs[0:chunks]
    lse_refs = refs[chunks : 2 * chunks]
    do_refs = refs[2 * chunks : 3 * chunks]
    out_ref, v_out_ref, dk_acc, dv_acc = refs[-4:]
    core = core_ref[0]
    place = (core, 1 - core)
    width = q_ref.shape[-1]
    col_head = head_ids((TILE, width))
    causal = causal_tile(TILE)
    per_half = k_ref.shape[2] // TILE
    per_chunk = per_half // chunks
    dk_acc[...] = jnp.zeros_like(dk_acc)
    dv_acc[...] = jnp.zeros_like(dv_acc)
    for half in range(2):
        for sub in range(per_half):
            blk = per_half * half + sub
            rows = slice(sub * TILE, (sub + 1) * TILE)
            inner = slice((sub % per_chunk) * TILE, (sub % per_chunk + 1) * TILE)
            q_blk = q_ref[place[half], 0, rows, :]
            do_blk = do_refs[sub // per_chunk][place[half], 0, inner, :]
            o_blk = o_refs[sub // per_chunk][place[half], 0, inner, :]
            lse_blk = lse_refs[sub // per_chunk][place[half], 0, inner, :]
            overlap = do_blk.astype(F32) * o_blk.astype(F32)
            q_all, do_all, lse_all, delta_all = [], [], [], []
            for head in range(heads):
                mine = col_head == head
                q_all.append(jnp.where(mine, q_blk, jnp.zeros_like(q_blk)))
                do_all.append(jnp.where(mine, do_blk, jnp.zeros_like(do_blk)))
                lse_all.append(lse_blk[:, head : head + 1])
                delta_all.append(jnp.sum(jnp.where(mine, overlap, 0.0), axis=1, keepdims=True))
            q_cat = jnp.concatenate(q_all, axis=0)
            do_cat = jnp.concatenate(do_all, axis=0)
            dq = [jnp.zeros((TILE, width), F32) for _ in range(heads)]
            for j in range(blk + 1):
                cols = slice((j % per_half) * TILE, (j % per_half + 1) * TILE)
                k_blk = k_ref[place[j // per_half], 0, cols, :]
                v_blk = v_ref[place[j // per_half], 0, cols, :]
                p_all, ds_all = [], []
                for head in range(heads):
                    p = jnp.exp(mm(q_all[head], k_blk, NT) - lse_all[head])
                    if j == blk:
                        p = jnp.where(causal, p, 0.0)
                    dp = mm(do_all[head], v_blk, NT)
                    ds = (p * (dp - delta_all[head])).astype(BF16)
                    dq[head] = dq[head] + mm(ds, k_blk)
                    p_all.append(p.astype(BF16))
                    ds_all.append(ds)
                dk_acc[j] += mm(jnp.concatenate(ds_all, axis=0), q_cat, TN)
                dv_acc[j] += mm(jnp.concatenate(p_all, axis=0), do_cat, TN)
            total = dq[0]
            for head in range(1, heads):
                total = jnp.where(col_head == head, dq[head], total)
            out_ref[place[half], 0, rows, 0:width] = (total * HEAD_DIM**-0.5).astype(BF16)
    for j in range(2 * per_half):
        rows = slice((j % per_half) * TILE, (j % per_half + 1) * TILE)
        out_ref[place[j // per_half], 0, rows, width : 2 * width] = dk_acc[j].astype(BF16)
        v_out_ref[place[j // per_half], 0, rows, :] = dv_acc[j].astype(BF16)


def attend_back(core, qk, v, outs, lses, back, seq, before=()):
    _, _, rows, width = v.shape
    chunks = len(outs)
    part = rows // chunks

    def block(size, cols, at):
        return pl.BlockSpec((2, 1, size, cols), lambda s, c: (0, seq, 0, at))

    operands = (core, qk, qk, v, *outs, *lses, *back)
    return pl.pallas_call(
        partial(attend_back_kernel, heads=width // HEAD_DIM, chunks=chunks),
        grid_spec=pltpu.PrefetchScalarGridSpec(
            num_scalar_prefetch=1,
            grid=(1,),
            in_specs=[block(rows, width, 0), block(rows, width, 1), block(rows, width, 0)]
            + [block(part, width, 0)] * chunks
            + [block(part, 128, 0)] * chunks
            + [block(part, width, 0)] * chunks
            + [pl.BlockSpec(memory_space=pl.ANY)] * len(before),
            out_specs=[block(rows, 2 * width, 0), block(rows, width, 0)],
            scratch_shapes=[pltpu.VMEM((2 * rows // TILE, TILE, width), F32)] * 2,
        ),
        out_shape=[jax.ShapeDtypeStruct(qk.shape, BF16), jax.ShapeDtypeStruct(v.shape, BF16)],
        input_output_aliases={len(operands) + i: i for i in range(len(before))},
        compiler_params=pltpu.CompilerParams(vmem_limit_bytes=VMEM_GRANT),
        cost_estimate=pl.CostEstimate(
            flops=12 * 10**9, bytes_accessed=6 * 10**6, transcendentals=0
        ),
    )(*operands, *before)


def hidden_kernel(*refs):
    blocks = refs[:-7]
    w_ref, bias_ref, dact_ref, act_ref, back_ref, sum_ref, all_ref = refs[-7:]
    rows = blocks[0].shape[0]
    value = jnp.concatenate([block[...] for block in blocks], axis=0)
    hidden = mm(value, w_ref[...]) + bias_ref[...]
    square = hidden * hidden
    bent = jnp.tanh(gelu_in * hidden * (1.0 + gelu_cube * square))
    half = 0.5 * (1.0 + bent)
    act_ref[...] = (hidden * half).astype(BF16)
    slope = half + 0.5 * hidden * (1.0 - bent * bent) * (
        gelu_in * (1.0 + 3.0 * gelu_cube * square)
    )
    back = (dact_ref[...].astype(F32) * slope).astype(BF16)
    back_ref[...] = back
    sum_ref[...] = jnp.sum(back.astype(F32), axis=0, keepdims=True)

    @pl.when(pl.program_id(0) == 0)
    def _():
        for at in range(len(blocks)):
            all_ref[at * rows : (at + 1) * rows, :] = blocks[at][...]


def hidden_layer(blocks, weight, bias, dact):
    rows, width = blocks[0].shape
    cols = weight.shape[1]
    total = len(blocks) * rows
    tile = min(256, cols)
    whole = pl.BlockSpec((rows, width), lambda n: (0, 0))
    column = pl.BlockSpec((total, tile), lambda n: (0, n))
    return pl.pallas_call(
        hidden_kernel,
        grid=(cols // tile,),
        in_specs=[whole] * len(blocks)
        + [
            pl.BlockSpec((width, tile), lambda n: (0, n)),
            pl.BlockSpec((1, tile), lambda n: (0, n)),
            column,
        ],
        out_specs=[
            column,
            column,
            pl.BlockSpec((1, tile), lambda n: (0, n)),
            pl.BlockSpec((total, width), lambda n: (0, 0)),
        ],
        out_shape=[
            jax.ShapeDtypeStruct((total, cols), BF16),
            jax.ShapeDtypeStruct((total, cols), BF16),
            jax.ShapeDtypeStruct((1, cols), F32),
            jax.ShapeDtypeStruct((total, width), BF16),
        ],
        compiler_params=pltpu.CompilerParams(vmem_limit_bytes=VMEM_GRANT),
        cost_estimate=pl.CostEstimate(
            flops=2 * total * width * cols, bytes_accessed=12 * 10**6, transcendentals=0
        ),
    )(*blocks, weight, bias.reshape(1, -1), dact)


def mixed_kernel(*refs):
    blocks = refs[:-3]
    w_ref, out_ref, all_ref = refs[-3:]
    rows = blocks[0].shape[0]
    for at in range(len(blocks)):
        value = blocks[at][...]
        out_ref[at * rows : (at + 1) * rows, :] = mm(value, w_ref[...], NT).astype(BF16)
        all_ref[at * rows : (at + 1) * rows, :] = value


def back_mix(blocks, weight):
    rows, width = blocks[0].shape
    cols = weight.shape[0]
    total = len(blocks) * rows
    return pl.pallas_call(
        mixed_kernel,
        in_specs=[pl.BlockSpec(memory_space=pltpu.VMEM)] * (len(blocks) + 1),
        out_specs=[pl.BlockSpec(memory_space=pltpu.VMEM)] * 2,
        out_shape=[
            jax.ShapeDtypeStruct((total, cols), BF16),
            jax.ShapeDtypeStruct((total, width), BF16),
        ],
        compiler_params=pltpu.CompilerParams(vmem_limit_bytes=VMEM_GRANT),
        cost_estimate=pl.CostEstimate(
            flops=2 * total * width * cols, bytes_accessed=5 * 10**6, transcendentals=0
        ),
    )(*blocks, weight)


def muon_kernel(
    limit_ref,
    landed_ref,
    mom_hbm,
    master_hbm,
    grad_out,
    mom_out,
    master_out,
    grad_buf,
    mom_buf,
    master_buf,
    x_buf,
    gram,
    poly,
    sems,
    *,
    out_rows,
):
    count, share, size = landed_ref.shape
    tile = 512
    tiles = size // tile
    load_mom = pltpu.make_async_copy(mom_hbm, mom_buf, sems.at[0])
    load_master = pltpu.make_async_copy(master_hbm, master_buf, sems.at[1])
    store_grad = pltpu.make_async_copy(grad_buf, grad_out, sems.at[2])
    store_mom = pltpu.make_async_copy(mom_buf, mom_out, sems.at[3])
    store_master = pltpu.make_async_copy(master_buf, master_out, sems.at[4])
    load_mom.start()
    load_master.start()
    row_limit = limit_ref[0]
    col_limit = limit_ref[1]
    is_out = limit_ref[2] == 1

    @pl.when(is_out)
    def _():
        grad_buf[...] = jnp.zeros_like(grad_buf)
        for src in range(count):
            cols = size * out_rows // share
            piece = landed_ref[src].astype(F32)[:, size - cols :]
            for at in range(share // out_rows):
                grad_buf[
                    src * out_rows : (src + 1) * out_rows, at * cols : (at + 1) * cols
                ] = piece[at * out_rows : (at + 1) * out_rows]

    @pl.when(jnp.logical_not(is_out))
    def _():
        for src in range(count):
            grad_buf[src * share : (src + 1) * share, :] = landed_ref[src].astype(F32)

    store_grad.start()
    load_mom.wait()
    block = 128

    def valid(r):
        row = lax.broadcasted_iota(jnp.int32, (block, size), 0) + r * block
        col = lax.broadcasted_iota(jnp.int32, (block, size), 1)
        return (row < row_limit) & (col < col_limit)

    def at_rows(r, step):
        return pl.ds(pl.multiple_of(r * step, step), step)

    def momentum_rows(r, total):
        rows = at_rows(r, block)
        value = jnp.where(valid(r), mom_decay * mom_buf[rows, :] + grad_buf[rows, :], 0.0)
        mom_buf[rows, :] = value
        return total + value * value

    total = lax.fori_loop(0, size // block, momentum_rows, jnp.zeros((block, size), F32))
    store_mom.start()
    scale = 1.0 / (jnp.sqrt(jnp.sum(total)) + 1e-07)

    def first_rows(r, carry):
        rows = at_rows(r, block)
        x_buf[0, rows, :] = (mom_buf[rows, :] * scale).astype(BF16)
        return carry

    lax.fori_loop(0, size // block, first_rows, 0)

    def one_turn(turn, carry):
        now = lax.rem(turn, 2)
        later = 1 - now

        for r in range(size // TILE):
            rows, rest = slice(r * TILE, (r + 1) * TILE), slice(r * TILE, size)
            value = mm(x_buf[now, rows, :], x_buf[now, rest, :], NT).astype(BF16)
            gram[rows, rest] = value
            for c in range(r + 1, size // TILE):
                block_rows = slice(c * TILE, (c + 1) * TILE)
                gram[block_rows, rows] = value[:, (c - r) * TILE : (c - r + 1) * TILE].T

        for r in range(size // TILE):
            rows, rest = slice(r * TILE, (r + 1) * TILE), slice(r * TILE, size)
            square = mm(gram[rows, :], gram[:, rest])
            value = (ns_b * gram[rows, rest].astype(F32) + ns_c * square).astype(BF16)
            poly[rows, rest] = value
            for c in range(r + 1, size // TILE):
                block_rows = slice(c * TILE, (c + 1) * TILE)
                poly[block_rows, rows] = value[:, (c - r) * TILE : (c - r + 1) * TILE].T

        def next_rows(r, c):
            rows = at_rows(r, tile)
            x_buf[later, rows, :] = (
                ns_a * x_buf[now, rows, :].astype(F32) + mm(poly[rows, :], x_buf[now])
            ).astype(BF16)
            return c

        lax.fori_loop(0, tiles, next_rows, 0)
        return carry

    lax.fori_loop(0, jnp.where(row_limit > 0, NS_STEPS, 0), one_turn, 0)
    load_master.wait()

    def master_rows(r, carry):
        rows = at_rows(r, block)
        ortho = x_buf[NS_STEPS % 2, rows, :].astype(F32)
        fresh = master_buf[rows, :] * (1.0 - muon_rate * muon_decay) - muon_rate * ortho
        master_buf[rows, :] = jnp.where(valid(r), fresh, 0.0)
        return carry

    lax.fori_loop(0, size // block, master_rows, 0)
    store_master.start()
    store_grad.wait()
    store_mom.wait()
    store_master.wait()


def muon_update(limits, landed, momentum, master, out_rows):
    size = momentum.shape[0]
    shape = jax.ShapeDtypeStruct((size, size), F32)
    anywhere = pl.BlockSpec(memory_space=pl.ANY)
    return pl.pallas_call(
        partial(muon_kernel, out_rows=out_rows),
        in_specs=[
            pl.BlockSpec(memory_space=pltpu.SMEM),
            pl.BlockSpec(memory_space=pltpu.VMEM),
            anywhere,
            anywhere,
        ],
        out_specs=[anywhere] * 3,
        out_shape=[shape] * 3,
        scratch_shapes=[
            pltpu.VMEM((size, size), F32),
            pltpu.VMEM((size, size), F32),
            pltpu.VMEM((size, size), F32),
            pltpu.VMEM((2, size, size), BF16),
            pltpu.VMEM((size, size), BF16),
            pltpu.VMEM((size, size), BF16),
            pltpu.SemaphoreType.DMA((5,)),
        ],
        compiler_params=pltpu.CompilerParams(vmem_limit_bytes=VMEM_GRANT),
        cost_estimate=pl.CostEstimate(
            flops=6 * NS_STEPS * size**3, bytes_accessed=22 * size * size, transcendentals=0
        ),
    )(limits, landed, momentum, master)


def swap(value, bit):
    count = lax.axis_size("tensor")
    return lax.ppermute(value, "tensor", [(i, i ^ bit) for i in range(count)])


def gather_four(value):
    core_block = swap(value, 1)
    far_block = swap(value, 2)
    return value, far_block, core_block, swap(far_block, 1)


def scatter_begin(values, weights, dims):
    size = values[0].shape[0] // 4

    def product(first, last):
        return sum(mm(v[first * size : last * size], w, dims) for v, w in zip(values, weights))

    arrived = swap(product(2, 4).astype(BF16), 1)
    return product(0, 2) + arrived.astype(F32)


def scatter_end(part):
    size = part.shape[0] // 2
    return part[:size] + swap(part[size:].astype(BF16), 2).astype(F32)


def exchange(part):
    size = part.shape[0] // 2
    given = part.astype(BF16)
    given = jnp.concatenate([given[size:], given[:size]])
    return part + swap(given, 2).astype(F32)


def data_swap(value, bit):
    count = lax.axis_size("dp")
    return lax.ppermute(value, "dp", [(i, i ^ bit) for i in range(count)])


def after(value, *others):
    return lax.optimization_barrier((value, *others))[0]


def tie(value, *others):
    held = False
    for other in others:
        held = held | jnp.isinf(other.reshape(-1)[0])
    return jnp.where(held, jnp.zeros_like(value), value)


def last_bits(*bits):
    return [bit for bit in reversed(axis_bits("dp")) if bit not in bits] + list(bits)


def bit_axis(bit):
    return len(axis_bits("dp")) - bit.bit_length()


def spread(value):
    return value.reshape((2,) * len(axis_bits("dp")) + (-1, value.shape[-1]))


def double(piece, bit):
    upper = (lax.axis_index("dp") & bit) != 0
    other = data_swap(piece, bit)
    axis = bit_axis(bit)
    return jnp.where(
        upper,
        jnp.concatenate([other, piece], axis=axis),
        jnp.concatenate([piece, other], axis=axis),
    )


def open_piece(value):
    return value.reshape((1,) * len(axis_bits("dp")) + value.shape)


def gather_by(value, bits):
    piece = open_piece(value)
    for bit in bits:
        piece = double(piece, bit)
    return rows2(piece)


def halve(value, bit):
    upper = ((lax.axis_index("dp") & bit) != 0).astype(jnp.int32)
    axis = bit_axis(bit)
    give = lax.dynamic_slice_in_dim(value, 1 - upper, 1, axis)
    keep = lax.dynamic_slice_in_dim(value, upper, 1, axis)
    return (keep.astype(F32) + data_swap(give, bit).astype(F32)).astype(BF16)


def halve_by(value, bits):
    for bit in bits:
        value = halve(value, bit)
    return value


def axis_bits(name):
    count = lax.axis_size(name)
    bits = []
    bit = 1
    while bit < count:
        bits.append(bit)
        bit *= 2
    return bits


def small_gather(piece, name, axis):
    index = lax.axis_index(name)
    count = lax.axis_size(name)
    for bit in axis_bits(name):
        other = lax.ppermute(piece, name, [(i, i ^ bit) for i in range(count)])
        upper = (index & bit) != 0
        piece = jnp.where(
            upper,
            jnp.concatenate([other, piece], axis=axis),
            jnp.concatenate([piece, other], axis=axis),
        )
    return piece


def small_scatter(value):
    value = value.reshape(lax.axis_size("dp"), -1)
    for name, axis in (("tensor", 1), ("dp", 0)):
        index = lax.axis_index(name)
        count = lax.axis_size(name)
        for bit in reversed(axis_bits(name)):
            low, high = jnp.split(value, 2, axis=axis)
            upper = (index & bit) != 0
            give = jnp.where(upper, low, high)
            keep = jnp.where(upper, high, low)
            value = keep + lax.ppermute(give, name, [(i, i ^ bit) for i in range(count)])
    return value.reshape(-1)


def norm_parts(values):
    centred = values - jnp.mean(values, axis=-1, keepdims=True)
    spread = jnp.mean(centred * centred, axis=-1, keepdims=True)
    scale = lax.rsqrt(spread + ln_eps)
    return centred * scale, scale


def norm_back(unit, scale, gain_vec, grad):
    inner = grad * gain_vec
    return scale * (
        inner
        - jnp.mean(inner, axis=-1, keepdims=True)
        - unit * jnp.mean(inner * unit, axis=-1, keepdims=True)
    )


def per_device(
    inputs, out_grad, owners, master_slots, momentum_slots, small_master, small_first, small_second
):
    rows_dev, width = inputs.shape
    tensor_count = lax.axis_size("tensor")
    data_count = lax.axis_size("dp")
    tensor_idx = lax.axis_index("tensor")
    data_idx = lax.axis_index("dp")
    head_width = width // tensor_count
    ff_width = FF // tensor_count
    share = width // data_count
    share_out = head_width // data_count
    core = jnp.reshape(tensor_idx & 1, (1,)).astype(jnp.int32)
    owner_row = lax.dynamic_index_in_dim(owners, tensor_idx, 0, keepdims=False)
    owned = owner_row == data_idx
    slot_value = master_slots[0]

    group_params = small_gather(small_master.reshape(1, -1), "tensor", 1)
    params = small_gather(group_params, "dp", 0)
    slot_low = slot_value.astype(BF16)
    offer_out = slot_low[:head_width].reshape(data_count, share_out, tensor_count, head_width)
    offer_out = jnp.swapaxes(offer_out, 1, 2).reshape(data_count, share, head_width)
    offer_out = jnp.pad(offer_out, ((0, 0), (0, 0), (width - head_width, 0)))
    offer = jnp.where(owned[1], offer_out, slot_low.reshape(data_count, share, width))
    shares = lax.all_to_all(tie(offer, params), "dp", 0, 0)
    params = params.reshape(-1)

    def own_slice(start, size):
        return lax.dynamic_slice_in_dim(params, start + tensor_idx * size, size, 0)

    gain_one = params[0:width]
    shift_one = params[width : 2 * width]
    bias_query = own_slice(2 * width, head_width)
    bias_value = own_slice(3 * width, head_width)
    bias_out = params[4 * width : 5 * width]
    gain_two = params[5 * width : 6 * width]
    shift_two = params[6 * width : 7 * width]
    bias_fc = own_slice(7 * width, ff_width)
    bias_proj = params[7 * width + FF :]

    part = rows_dev // CHUNKS
    rows_of = [slice(chunk * part, (chunk + 1) * part) for chunk in range(CHUNKS)]
    rows_in = inputs.astype(F32)
    unit_one, scale_one = norm_parts(rows_in)
    inputs_four = gather_four(after(inputs, group_params))
    unit_all, _ = norm_parts(jnp.concatenate(inputs_four).astype(F32))
    normed_all = (unit_all * gain_one + shift_one).astype(BF16)
    dy_four = [gather_four(after(out_grad[rows], inputs_four[1])) for rows in rows_of]
    dy_all = [jnp.concatenate(four) for four in dy_four]

    shares = after(shares, normed_all, *dy_all)

    def share_of(kind):
        return lax.dynamic_index_in_dim(shares, owner_row[kind], 0, keepdims=False)

    split = 2 * head_width
    first = share_of(0)
    piece = open_piece(
        jnp.concatenate([first[:, : split + head_width], share_of(1)[:, width - head_width :]], axis=1)
    )
    for bit in last_bits(2, 1)[:-2]:
        piece = double(piece, bit)
    two_qk = double(piece[..., :split], 2)
    two_vo = double(piece[..., split:], 1)
    w_qk, w_vo = rows2(double(two_qk, 1)), rows2(double(two_vo, 2))
    w_v = w_vo[:, :head_width]
    w_out = w_vo[:, head_width:].reshape(data_count, tensor_count, share_out, head_width)
    w_out = jnp.swapaxes(w_out, 1, 2).reshape(head_width, width)
    bits_proj = last_bits(1, 2)
    bits_fc = last_bits(2, 1)
    w_proj = double(open_piece(tie(share_of(3), two_qk, two_vo)), bits_proj[0])
    w_fc = double(open_piece(tie(share_of(2), w_proj, w_qk)), bits_fc[0])
    bias_qk = jnp.concatenate([bias_query, jnp.zeros_like(bias_query)])
    scale_qk = jnp.where(jnp.arange(split) < head_width, HEAD_DIM**-0.5, 1.0)
    qk = ((mm(normed_all, w_qk) + bias_qk) * scale_qk).astype(BF16)
    values = (mm(normed_all, w_v) + bias_value).astype(BF16)
    qk = qk.reshape(2, 2, rows_dev, split)
    values = values.reshape(2, 2, rows_dev, head_width)

    first_steps = (w_proj, w_fc)
    for bit in bits_proj[1:-1]:
        w_proj = double(w_proj, bit)
    for bit in bits_fc[1:-1]:
        w_fc = double(w_fc, bit)
    mixed, log_sums, parts = [], [], []
    for chunk in range(CHUNKS):
        late = (qk, values) if chunk == 0 else after((qk, values), *first_steps)
        mixed_one, sums_one = attend(core, *late, chunk, CHUNKS)
        if chunk > 0:
            mixed_one = after(mixed_one, w_proj, w_fc)
        mixed.append(mixed_one)
        log_sums.append(sums_one)
        parts.append(scatter_begin([rows2(mixed_one)], [w_out], NN))
    w_proj = rows2(double(after(w_proj, mixed[-1]), bits_proj[-1]))
    w_fc = rows2(double(after(w_fc, mixed[-1]), bits_fc[-1]))
    back_act = [mm(after(dy, parts[-1]), w_proj, NT).astype(BF16) for dy in dy_all]
    middles, mine_two, normed_two = [], [], []
    branches = [exchange(value) for value in parts]
    for chunk in range(CHUNKS):
        rows = rows_of[chunk]
        branch = branches[chunk]
        if chunk > 0:
            branch = after(branch, normed_two[-1])
        residual = jnp.concatenate([inputs[rows], inputs_four[1][rows]]).astype(F32)
        middle = residual + branch + bias_out
        unit_two, scale_two = norm_parts(middle)
        normed_two.append((unit_two * gain_two + shift_two).astype(BF16))
        middles.append(middle[:part])
        mine_two.append((unit_two, scale_two))

    acts, backs, wholes, parts, sums_two = [], [], [], [], []
    grad_proj, grad_fc, fc_bias_grad = 0.0, 0.0, 0.0
    for chunk in range(CHUNKS):
        block = (normed_two[chunk], swap(normed_two[chunk], 1))
        if chunk > 0:
            block = after(block, parts[-1])
        act, back, sums, whole = hidden_layer(block, w_fc, bias_fc, back_act[chunk])
        parts.append(scatter_begin([after(back, *sums_two)], [w_fc], NT))
        sums_two.append(exchange(parts[-1]))
        acts.append(act)
        backs.append(back)
        wholes.append(whole)
        fc_bias_grad = fc_bias_grad + sums[0]
    back_middles, back_lows, back_mixed, mids = [], [], [], []
    gain_two_grad, shift_two_grad = 0.0, 0.0
    for chunk in range(CHUNKS):
        unit_two, scale_two = mine_two[chunk]
        grad = after(sums_two[chunk], parts[-1], *back_lows[-1:])
        dy = jnp.concatenate(dy_four[chunk][:2]).astype(F32)
        back_middle = dy + norm_back(unit_two, scale_two, gain_two, grad)
        back_lows.append(back_middle.astype(BF16))
        gain_two_grad = gain_two_grad + jnp.sum(grad[:part] * unit_two[:part], axis=0)
        shift_two_grad = shift_two_grad + jnp.sum(grad[:part], axis=0)
        back_middles.append(back_middle[:part])
        block = after((back_lows[-1], swap(back_lows[-1], 1)), parts[-1])
        grad_rows = (acts[chunk], wholes[chunk], backs[chunk])
        act, whole, back = after(grad_rows, parts[0] if chunk == 0 else back_lows[0])
        grad_proj = grad_proj + mm(act, dy_all[chunk], TN)
        grad_fc = grad_fc + mm(whole, back, TN)
        mixed_grad, mid = back_mix(block, w_out)
        back_mixed.append(mixed_grad.reshape(2, 2, part, head_width))
        mids.append(mid)
    middle = jnp.concatenate(middles)
    back_middle = jnp.concatenate(back_middles)
    proj_bias_grad = jnp.sum(out_grad, axis=0, dtype=F32)
    out_bias_grad = jnp.sum(back_middle, axis=0)

    grad_proj, grad_fc = grad_proj.astype(BF16), grad_fc.astype(BF16)
    half_proj = halve(spread(grad_proj), 1)
    half_fc = halve(spread(grad_fc), 2)
    back_mixed, half_proj, half_fc = lax.optimization_barrier((back_mixed, half_proj, half_fc))
    steps = axis_bits("dp")
    rest_proj, rest_fc = steps[1:], steps[2:] + [1]
    half_proj = halve(half_proj, rest_proj[0])
    half_fc = halve(half_fc, rest_fc[0])
    attend_grad = attend_back(core, qk, values, mixed, log_sums, back_mixed, 0)
    back_mixed = after(back_mixed, half_proj, half_fc)
    back_qk, back_v = attend_back(core, qk, values, mixed, log_sums, back_mixed, 1, attend_grad)
    share_proj = halve_by(half_proj, rest_proj[1:])
    share_fc = halve_by(half_fc, rest_fc[1:])
    grad_out = sum(mm(rows2(mixed[i]), mids[i], TN) for i in range(CHUNKS)).astype(BF16)
    grad_out = grad_out.reshape(data_count, share_out, tensor_count, head_width)
    grad_out = jnp.swapaxes(grad_out, 1, 2).reshape(width, head_width)
    grad_qk = mm(normed_all, rows2(back_qk), TN).astype(BF16)
    grad_v = mm(normed_all, rows2(back_v), TN).astype(BF16)
    grad_vo = jnp.concatenate([grad_v, grad_out], axis=1)
    half_qk = halve(spread(grad_qk), 1)
    half_vo = halve(spread(grad_vo), 2)
    share_attend = jnp.concatenate([halve(half_qk, 2), halve(half_vo, 1)], axis=-1)
    share_attend = rows2(halve_by(share_attend, steps[2:]))

    late_qk, late_v = after((back_qk, back_v), grad_qk, grad_vo)
    back_normed = scatter_end(scatter_begin([rows2(late_qk), rows2(late_v)], [w_qk, w_v], NT))
    acts = after(acts, back_normed)
    branches = [scatter_end(scatter_begin([act], [w_proj], NN)) for act in acts]
    block_out = (middle + jnp.concatenate(branches) + bias_proj).astype(BF16)
    input_grad = back_middle + norm_back(unit_one, scale_one, gain_one, back_normed)
    gain_one_grad = jnp.sum(back_normed * unit_one, axis=0)
    shift_one_grad = jnp.sum(back_normed, axis=0)
    query_bias_grad = jnp.sum(late_qk[..., :head_width], axis=(0, 1, 2), dtype=F32)
    value_bias_grad = jnp.sum(late_v, axis=(0, 1, 2), dtype=F32)

    bundle = jnp.zeros((data_count, share, width), BF16)
    pieces = (
        jnp.pad(share_attend[:, : 3 * head_width], ((0, 0), (0, width - 3 * head_width))),
        jnp.pad(share_attend[:, width - head_width :], ((0, 0), (width - head_width, 0))),
        rows2(share_fc),
        rows2(share_proj),
    )
    for kind in range(4):
        bundle = lax.dynamic_update_index_in_dim(bundle, pieces[kind], owner_row[kind], 0)
    landed = lax.all_to_all(bundle, "dp", 0, 0)
    full_grad = jnp.concatenate(
        [
            gain_one_grad,
            shift_one_grad,
            jnp.zeros((2 * width,), F32),
            out_bias_grad,
            gain_two_grad,
            shift_two_grad,
            jnp.zeros((FF,), F32),
            proj_bias_grad,
        ]
    )
    for grad, start, size in (
        (query_bias_grad, 2 * width, head_width),
        (value_bias_grad, 3 * width, head_width),
        (fc_bias_grad, 7 * width, ff_width),
    ):
        full_grad = lax.dynamic_update_slice_in_dim(full_grad, grad, start + tensor_idx * size, 0)
    small_grad = small_scatter(full_grad)
    first_new = beta_one * small_first + (1.0 - beta_one) * small_grad
    second_new = beta_two * small_second + (1.0 - beta_two) * small_grad * small_grad
    first_hat = first_new / (1.0 - beta_one**STEP)
    second_hat = second_new / (1.0 - beta_two**STEP)
    small_new = small_master - adam_rate * first_hat / (jnp.sqrt(second_hat) + adam_eps)

    row_limit = jnp.where(owned[1], head_width, jnp.where(jnp.any(owned), width, 0))
    col_limit = jnp.where(owned[0], 3 * head_width, width)
    limits = jnp.stack([row_limit, col_limit, owned[1].astype(jnp.int32)]).astype(jnp.int32)
    grad_slot, mom_slot, fresh_slot = muon_update(
        limits, landed, momentum_slots[0], slot_value, share_out
    )
    return (
        block_out,
        input_grad,
        grad_slot[None],
        mom_slot[None],
        fresh_slot[None],
        small_grad,
        second_new,
        small_new,
    )


def solution(mesh):
    return jax.shard_map(
        per_device,
        mesh=mesh,
        in_specs=(
            P(("dp", "tensor"), None),
            P(("dp", "tensor"), None),
            P(),
            P("dp", "tensor", None),
            P("dp", "tensor", None),
            P(("dp", "tensor")),
            P(("dp", "tensor")),
            P(("dp", "tensor")),
        ),
        out_specs=(
            P(("dp", "tensor"), None),
            P(("dp", "tensor"), None),
            P("dp", "tensor", None),
            P("dp", "tensor", None),
            P("dp", "tensor", None),
            P(("dp", "tensor")),
            P(("dp", "tensor")),
            P(("dp", "tensor")),
        ),
        check_vma=False,
    )
```

```python
from functools import partial

import jax
import jax.numpy as jnp
from jax import lax
from jax.experimental import pallas as pl
from jax.experimental.pallas import tpu as pltpu
from jax.sharding import PartitionSpec as P

HEADS = 16
FF = 4096
SEQ = 1024
NS_STEPS = 5
STEP = 10
HEAD_DIM = 64

ln_eps = 1e-05
mom_decay = 0.95
ns_a = 3.4445
ns_b = -4.775
ns_c = 2.0315
muon_rate = 0.5
muon_decay = 0.01
beta_one = 0.9
beta_two = 0.95
adam_rate = 0.2
adam_eps = 1e-08
masked_score = -1e30
gelu_in = 0.7978845608028654
gelu_cube = 0.044715

CHUNKS = 2
TILE = 256
VMEM_GRANT = 48 * 1024 * 1024
BF16 = jnp.bfloat16
F32 = jnp.float32

NN = (((1,), (0,)), ((), ()))
NT = (((1,), (1,)), ((), ()))
TN = (((0,), (0,)), ((), ()))


def mm(left, right, dims=NN):
    return lax.dot_general(left, right, dims, preferred_element_type=F32)


def rows2(value):
    return value.reshape(-1, value.shape[-1])


def head_ids(shape):
    return lax.broadcasted_iota(jnp.int32, shape, 1) // HEAD_DIM


def causal_tile(tile):
    row = lax.broadcasted_iota(jnp.int32, (tile, tile), 0)
    col = lax.broadcasted_iota(jnp.int32, (tile, tile), 1)
    return row >= col


def attend_kernel(core_ref, q_ref, k_ref, v_ref, o_ref, lse_ref, *, subs, heads):
    core = core_ref[0]
    place = (core, 1 - core)
    width = q_ref.shape[-1]
    col_head = head_ids((TILE, width))
    lane = lax.broadcasted_iota(jnp.int32, (TILE, 128), 1)
    causal = causal_tile(TILE)
    per_half = k_ref.shape[2] // TILE
    for half in range(2):
        for at, sub in enumerate(subs):
            blk = per_half * half + sub
            rows = slice(at * TILE, (at + 1) * TILE)
            q_blk = q_ref[place[half], 0, rows, :]
            acc = jnp.zeros((TILE, width), F32)
            lse = jnp.zeros((TILE, 128), F32)
            for head in range(heads):
                q_one = jnp.where(col_head == head, q_blk, jnp.zeros_like(q_blk))
                scores = []
                for j in range(blk + 1):
                    cols = slice((j % per_half) * TILE, (j % per_half + 1) * TILE)
                    s = mm(q_one, k_ref[place[j // per_half], 0, cols, :], NT)
                    if j == blk:
                        s = jnp.where(causal, s, masked_score)
                    scores.append(s)
                top = scores[0]
                for s in scores[1:]:
                    top = jnp.maximum(top, s)
                top = jnp.max(top, axis=1, keepdims=True)
                total = jnp.zeros((TILE, TILE), F32)
                out = jnp.zeros((TILE, width), F32)
                for j in range(blk + 1):
                    cols = slice((j % per_half) * TILE, (j % per_half + 1) * TILE)
                    p = jnp.exp(scores[j] - top)
                    total = total + p
                    out = out + mm(p.astype(BF16), v_ref[place[j // per_half], 0, cols, :])
                total = jnp.sum(total, axis=1, keepdims=True)
                acc = jnp.where(col_head == head, out * (1.0 / total), acc)
                lse = jnp.where(lane == head, top + jnp.log(total), lse)
            o_ref[place[half], 0, rows, :] = acc.astype(BF16)
            lse_ref[place[half], 0, rows, :] = lse


def attend(core, qk, v, chunk, chunks):
    _, seqs, rows, width = v.shape
    part = rows // chunks
    per = part // TILE
    subs = tuple(range(chunk * per, (chunk + 1) * per))
    return pl.pallas_call(
        partial(attend_kernel, subs=subs, heads=width // HEAD_DIM),
        grid_spec=pltpu.PrefetchScalarGridSpec(
            num_scalar_prefetch=1,
            grid=(seqs,),
            in_specs=[
                pl.BlockSpec((2, 1, part, width), lambda s, c: (0, s, chunk, 0)),
                pl.BlockSpec((2, 1, rows, width), lambda s, c: (0, s, 0, 1)),
                pl.BlockSpec((2, 1, rows, width), lambda s, c: (0, s, 0, 0)),
            ],
            out_specs=[
                pl.BlockSpec((2, 1, part, width), lambda s, c: (0, s, 0, 0)),
                pl.BlockSpec((2, 1, part, 128), lambda s, c: (0, s, 0, 0)),
            ],
        ),
        out_shape=[
            jax.ShapeDtypeStruct((2, seqs, part, width), BF16),
            jax.ShapeDtypeStruct((2, seqs, part, 128), F32),
        ],
        compiler_params=pltpu.CompilerParams(vmem_limit_bytes=VMEM_GRANT),
        cost_estimate=pl.CostEstimate(
            flops=10 * 10**9 // chunks, bytes_accessed=6 * 10**6, transcendentals=0
        ),
    )(core, qk, qk, v)


def attend_back_kernel(
    core_ref, q_ref, k_ref, v_ref, *refs, heads, chunks
):
    o_refs = refs[0:chunks]
    lse_refs = refs[chunks : 2 * chunks]
    do_refs = refs[2 * chunks : 3 * chunks]
    out_ref, v_out_ref, dk_acc, dv_acc = refs[-4:]
    core = core_ref[0]
    place = (core, 1 - core)
    width = q_ref.shape[-1]
    col_head = head_ids((TILE, width))
    causal = causal_tile(TILE)
    per_half = k_ref.shape[2] // TILE
    per_chunk = per_half // chunks
    dk_acc[...] = jnp.zeros_like(dk_acc)
    dv_acc[...] = jnp.zeros_like(dv_acc)
    for half in range(2):
        for sub in range(per_half):
            blk = per_half * half + sub
            rows = slice(sub * TILE, (sub + 1) * TILE)
            inner = slice((sub % per_chunk) * TILE, (sub % per_chunk + 1) * TILE)
            q_blk = q_ref[place[half], 0, rows, :]
            do_blk = do_refs[sub // per_chunk][place[half], 0, inner, :]
            o_blk = o_refs[sub // per_chunk][place[half], 0, inner, :]
            lse_blk = lse_refs[sub // per_chunk][place[half], 0, inner, :]
            overlap = do_blk.astype(F32) * o_blk.astype(F32)
            q_all, do_all, lse_all, delta_all = [], [], [], []
            for head in range(heads):
                mine = col_head == head
                q_all.append(jnp.where(mine, q_blk, jnp.zeros_like(q_blk)))
                do_all.append(jnp.where(mine, do_blk, jnp.zeros_like(do_blk)))
                lse_all.append(lse_blk[:, head : head + 1])
                delta_all.append(jnp.sum(jnp.where(mine, overlap, 0.0), axis=1, keepdims=True))
            q_cat = jnp.concatenate(q_all, axis=0)
            do_cat = jnp.concatenate(do_all, axis=0)
            dq = [jnp.zeros((TILE, width), F32) for _ in range(heads)]
            for j in range(blk + 1):
                cols = slice((j % per_half) * TILE, (j % per_half + 1) * TILE)
                k_blk = k_ref[place[j // per_half], 0, cols, :]
                v_blk = v_ref[place[j // per_half], 0, cols, :]
                p_all, ds_all = [], []
                for head in range(heads):
                    p = jnp.exp(mm(q_all[head], k_blk, NT) - lse_all[head])
                    if j == blk:
                        p = jnp.where(causal, p, 0.0)
                    dp = mm(do_all[head], v_blk, NT)
                    ds = (p * (dp - delta_all[head])).astype(BF16)
                    dq[head] = dq[head] + mm(ds, k_blk)
                    p_all.append(p.astype(BF16))
                    ds_all.append(ds)
                dk_acc[j] += mm(jnp.concatenate(ds_all, axis=0), q_cat, TN)
                dv_acc[j] += mm(jnp.concatenate(p_all, axis=0), do_cat, TN)
            total = dq[0]
            for head in range(1, heads):
                total = jnp.where(col_head == head, dq[head], total)
            out_ref[place[half], 0, rows, 0:width] = (total * HEAD_DIM**-0.5).astype(BF16)
    for j in range(2 * per_half):
        rows = slice((j % per_half) * TILE, (j % per_half + 1) * TILE)
        out_ref[place[j // per_half], 0, rows, width : 2 * width] = dk_acc[j].astype(BF16)
        v_out_ref[place[j // per_half], 0, rows, :] = dv_acc[j].astype(BF16)


def attend_back(core, qk, v, outs, lses, back, seq, before=()):
    _, _, rows, width = v.shape
    chunks = len(outs)
    part = rows // chunks

    def block(size, cols, at):
        return pl.BlockSpec((2, 1, size, cols), lambda s, c: (0, seq, 0, at))

    operands = (core, qk, qk, v, *outs, *lses, *back)
    return pl.pallas_call(
        partial(attend_back_kernel, heads=width // HEAD_DIM, chunks=chunks),
        grid_spec=pltpu.PrefetchScalarGridSpec(
            num_scalar_prefetch=1,
            grid=(1,),
            in_specs=[block(rows, width, 0), block(rows, width, 1), block(rows, width, 0)]
            + [block(part, width, 0)] * chunks
            + [block(part, 128, 0)] * chunks
            + [block(part, width, 0)] * chunks
            + [pl.BlockSpec(memory_space=pl.ANY)] * len(before),
            out_specs=[block(rows, 2 * width, 0), block(rows, width, 0)],
            scratch_shapes=[pltpu.VMEM((2 * rows // TILE, TILE, width), F32)] * 2,
        ),
        out_shape=[jax.ShapeDtypeStruct(qk.shape, BF16), jax.ShapeDtypeStruct(v.shape, BF16)],
        input_output_aliases={len(operands) + i: i for i in range(len(before))},
        compiler_params=pltpu.CompilerParams(vmem_limit_bytes=VMEM_GRANT),
        cost_estimate=pl.CostEstimate(
            flops=12 * 10**9, bytes_accessed=6 * 10**6, transcendentals=0
        ),
    )(*operands, *before)


def hidden_kernel(*refs):
    blocks = refs[:-7]
    w_ref, bias_ref, dact_ref, act_ref, back_ref, sum_ref, all_ref = refs[-7:]
    rows = blocks[0].shape[0]
    value = jnp.concatenate([block[...] for block in blocks], axis=0)
    hidden = mm(value, w_ref[...]) + bias_ref[...]
    square = hidden * hidden
    bent = jnp.tanh(gelu_in * hidden * (1.0 + gelu_cube * square))
    half = 0.5 * (1.0 + bent)
    act_ref[...] = (hidden * half).astype(BF16)
    slope = half + 0.5 * hidden * (1.0 - bent * bent) * (
        gelu_in * (1.0 + 3.0 * gelu_cube * square)
    )
    back = (dact_ref[...].astype(F32) * slope).astype(BF16)
    back_ref[...] = back
    sum_ref[...] = jnp.sum(back.astype(F32), axis=0, keepdims=True)

    @pl.when(pl.program_id(0) == 0)
    def _():
        for at in range(len(blocks)):
            all_ref[at * rows : (at + 1) * rows, :] = blocks[at][...]


def hidden_layer(blocks, weight, bias, dact):
    rows, width = blocks[0].shape
    cols = weight.shape[1]
    total = len(blocks) * rows
    tile = min(256, cols)
    whole = pl.BlockSpec((rows, width), lambda n: (0, 0))
    column = pl.BlockSpec((total, tile), lambda n: (0, n))
    return pl.pallas_call(
        hidden_kernel,
        grid=(cols // tile,),
        in_specs=[whole] * len(blocks)
        + [
            pl.BlockSpec((width, tile), lambda n: (0, n)),
            pl.BlockSpec((1, tile), lambda n: (0, n)),
            column,
        ],
        out_specs=[
            column,
            column,
            pl.BlockSpec((1, tile), lambda n: (0, n)),
            pl.BlockSpec((total, width), lambda n: (0, 0)),
        ],
        out_shape=[
            jax.ShapeDtypeStruct((total, cols), BF16),
            jax.ShapeDtypeStruct((total, cols), BF16),
            jax.ShapeDtypeStruct((1, cols), F32),
            jax.ShapeDtypeStruct((total, width), BF16),
        ],
        compiler_params=pltpu.CompilerParams(vmem_limit_bytes=VMEM_GRANT),
        cost_estimate=pl.CostEstimate(
            flops=2 * total * width * cols, bytes_accessed=12 * 10**6, transcendentals=0
        ),
    )(*blocks, weight, bias.reshape(1, -1), dact)


def mixed_kernel(*refs):
    blocks = refs[:-3]
    w_ref, out_ref, all_ref = refs[-3:]
    rows = blocks[0].shape[0]
    for at in range(len(blocks)):
        value = blocks[at][...]
        out_ref[at * rows : (at + 1) * rows, :] = mm(value, w_ref[...], NT).astype(BF16)
        all_ref[at * rows : (at + 1) * rows, :] = value


def back_mix(blocks, weight):
    rows, width = blocks[0].shape
    cols = weight.shape[0]
    total = len(blocks) * rows
    return pl.pallas_call(
        mixed_kernel,
        in_specs=[pl.BlockSpec(memory_space=pltpu.VMEM)] * (len(blocks) + 1),
        out_specs=[pl.BlockSpec(memory_space=pltpu.VMEM)] * 2,
        out_shape=[
            jax.ShapeDtypeStruct((total, cols), BF16),
            jax.ShapeDtypeStruct((total, width), BF16),
        ],
        compiler_params=pltpu.CompilerParams(vmem_limit_bytes=VMEM_GRANT),
        cost_estimate=pl.CostEstimate(
            flops=2 * total * width * cols, bytes_accessed=5 * 10**6, transcendentals=0
        ),
    )(*blocks, weight)


def muon_kernel(
    limit_ref,
    landed_ref,
    mom_hbm,
    master_hbm,
    grad_out,
    mom_out,
    master_out,
    grad_buf,
    mom_buf,
    master_buf,
    x_buf,
    gram,
    poly,
    sems,
    *,
    out_rows,
):
    count, share, size = landed_ref.shape
    tile = 512
    tiles = size // tile
    load_mom = pltpu.make_async_copy(mom_hbm, mom_buf, sems.at[0])
    load_master = pltpu.make_async_copy(master_hbm, master_buf, sems.at[1])
    store_grad = pltpu.make_async_copy(grad_buf, grad_out, sems.at[2])
    store_mom = pltpu.make_async_copy(mom_buf, mom_out, sems.at[3])
    store_master = pltpu.make_async_copy(master_buf, master_out, sems.at[4])
    load_mom.start()
    load_master.start()
    row_limit = limit_ref[0]
    col_limit = limit_ref[1]
    is_out = limit_ref[2] == 1

    @pl.when(is_out)
    def _():
        grad_buf[...] = jnp.zeros_like(grad_buf)
        for src in range(count):
            cols = size * out_rows // share
            piece = landed_ref[src].astype(F32)[:, size - cols :]
            for at in range(share // out_rows):
                grad_buf[
                    src * out_rows : (src + 1) * out_rows, at * cols : (at + 1) * cols
                ] = piece[at * out_rows : (at + 1) * out_rows]

    @pl.when(jnp.logical_not(is_out))
    def _():
        for src in range(count):
            grad_buf[src * share : (src + 1) * share, :] = landed_ref[src].astype(F32)

    store_grad.start()
    load_mom.wait()
    block = 128

    def valid(r):
        row = lax.broadcasted_iota(jnp.int32, (block, size), 0) + r * block
        col = lax.broadcasted_iota(jnp.int32, (block, size), 1)
        return (row < row_limit) & (col < col_limit)

    def at_rows(r, step):
        return pl.ds(pl.multiple_of(r * step, step), step)

    def momentum_rows(r, total):
        rows = at_rows(r, block)
        value = jnp.where(valid(r), mom_decay * mom_buf[rows, :] + grad_buf[rows, :], 0.0)
        mom_buf[rows, :] = value
        return total + value * value

    total = lax.fori_loop(0, size // block, momentum_rows, jnp.zeros((block, size), F32))
    store_mom.start()
    scale = 1.0 / (jnp.sqrt(jnp.sum(total)) + 1e-07)

    def first_rows(r, carry):
        rows = at_rows(r, block)
        x_buf[0, rows, :] = (mom_buf[rows, :] * scale).astype(BF16)
        return carry

    lax.fori_loop(0, size // block, first_rows, 0)

    def one_turn(turn, carry):
        now = lax.rem(turn, 2)
        later = 1 - now

        for r in range(size // TILE):
            rows, rest = slice(r * TILE, (r + 1) * TILE), slice(r * TILE, size)
            value = mm(x_buf[now, rows, :], x_buf[now, rest, :], NT).astype(BF16)
            gram[rows, rest] = value
            for c in range(r + 1, size // TILE):
                block_rows = slice(c * TILE, (c + 1) * TILE)
                gram[block_rows, rows] = value[:, (c - r) * TILE : (c - r + 1) * TILE].T

        for r in range(size // TILE):
            rows, rest = slice(r * TILE, (r + 1) * TILE), slice(r * TILE, size)
            square = mm(gram[rows, :], gram[:, rest])
            value = (ns_b * gram[rows, rest].astype(F32) + ns_c * square).astype(BF16)
            poly[rows, rest] = value
            for c in range(r + 1, size // TILE):
                block_rows = slice(c * TILE, (c + 1) * TILE)
                poly[block_rows, rows] = value[:, (c - r) * TILE : (c - r + 1) * TILE].T

        def next_rows(r, c):
            rows = at_rows(r, tile)
            x_buf[later, rows, :] = (
                ns_a * x_buf[now, rows, :].astype(F32) + mm(poly[rows, :], x_buf[now])
            ).astype(BF16)
            return c

        lax.fori_loop(0, tiles, next_rows, 0)
        return carry

    lax.fori_loop(0, jnp.where(row_limit > 0, NS_STEPS, 0), one_turn, 0)
    load_master.wait()

    def master_rows(r, carry):
        rows = at_rows(r, block)
        ortho = x_buf[NS_STEPS % 2, rows, :].astype(F32)
        fresh = master_buf[rows, :] * (1.0 - muon_rate * muon_decay) - muon_rate * ortho
        master_buf[rows, :] = jnp.where(valid(r), fresh, 0.0)
        return carry

    lax.fori_loop(0, size // block, master_rows, 0)
    store_master.start()
    store_grad.wait()
    store_mom.wait()
    store_master.wait()


def muon_update(limits, landed, momentum, master, out_rows):
    size = momentum.shape[0]
    shape = jax.ShapeDtypeStruct((size, size), F32)
    anywhere = pl.BlockSpec(memory_space=pl.ANY)
    return pl.pallas_call(
        partial(muon_kernel, out_rows=out_rows),
        in_specs=[
            pl.BlockSpec(memory_space=pltpu.SMEM),
            pl.BlockSpec(memory_space=pltpu.VMEM),
            anywhere,
            anywhere,
        ],
        out_specs=[anywhere] * 3,
        out_shape=[shape] * 3,
        scratch_shapes=[
            pltpu.VMEM((size, size), F32),
            pltpu.VMEM((size, size), F32),
            pltpu.VMEM((size, size), F32),
            pltpu.VMEM((2, size, size), BF16),
            pltpu.VMEM((size, size), BF16),
            pltpu.VMEM((size, size), BF16),
            pltpu.SemaphoreType.DMA((5,)),
        ],
        compiler_params=pltpu.CompilerParams(vmem_limit_bytes=VMEM_GRANT),
        cost_estimate=pl.CostEstimate(
            flops=6 * NS_STEPS * size**3, bytes_accessed=22 * size * size, transcendentals=0
        ),
    )(limits, landed, momentum, master)


def swap(value, bit):
    count = lax.axis_size("tensor")
    return lax.ppermute(value, "tensor", [(i, i ^ bit) for i in range(count)])


def gather_four(value):
    core_block = swap(value, 1)
    far_block = swap(value, 2)
    return value, far_block, core_block, swap(far_block, 1)


def scatter_begin(values, weights, dims):
    size = values[0].shape[0] // 4

    def product(first, last):
        return sum(mm(v[first * size : last * size], w, dims) for v, w in zip(values, weights))

    arrived = swap(product(2, 4).astype(BF16), 1)
    return product(0, 2) + arrived.astype(F32)


def scatter_end(part):
    size = part.shape[0] // 2
    return part[:size] + swap(part[size:].astype(BF16), 2).astype(F32)


def exchange(part):
    size = part.shape[0] // 2
    given = part.astype(BF16)
    given = jnp.concatenate([given[size:], given[:size]])
    return part + swap(given, 2).astype(F32)


def data_swap(value, bit):
    count = lax.axis_size("dp")
    return lax.ppermute(value, "dp", [(i, i ^ bit) for i in range(count)])


def after(value, *others):
    return lax.optimization_barrier((value, *others))[0]


def tie(value, *others):
    held = False
    for other in others:
        held = held | jnp.isinf(other.reshape(-1)[0])
    return jnp.where(held, jnp.zeros_like(value), value)


def last_bits(*bits):
    return [bit for bit in reversed(axis_bits("dp")) if bit not in bits] + list(bits)


def bit_axis(bit):
    return len(axis_bits("dp")) - bit.bit_length()


def spread(value):
    return value.reshape((2,) * len(axis_bits("dp")) + (-1, value.shape[-1]))


def double(piece, bit):
    upper = (lax.axis_index("dp") & bit) != 0
    other = data_swap(piece, bit)
    axis = bit_axis(bit)
    return jnp.where(
        upper,
        jnp.concatenate([other, piece], axis=axis),
        jnp.concatenate([piece, other], axis=axis),
    )


def open_piece(value):
    return value.reshape((1,) * len(axis_bits("dp")) + value.shape)


def gather_by(value, bits):
    piece = open_piece(value)
    for bit in bits:
        piece = double(piece, bit)
    return rows2(piece)


def halve(value, bit):
    upper = ((lax.axis_index("dp") & bit) != 0).astype(jnp.int32)
    axis = bit_axis(bit)
    give = lax.dynamic_slice_in_dim(value, 1 - upper, 1, axis)
    keep = lax.dynamic_slice_in_dim(value, upper, 1, axis)
    return (keep.astype(F32) + data_swap(give, bit).astype(F32)).astype(BF16)


def halve_by(value, bits):
    for bit in bits:
        value = halve(value, bit)
    return value


def axis_bits(name):
    count = lax.axis_size(name)
    bits = []
    bit = 1
    while bit < count:
        bits.append(bit)
        bit *= 2
    return bits


def small_gather(piece, name, axis):
    index = lax.axis_index(name)
    count = lax.axis_size(name)
    for bit in axis_bits(name):
        other = lax.ppermute(piece, name, [(i, i ^ bit) for i in range(count)])
        upper = (index & bit) != 0
        piece = jnp.where(
            upper,
            jnp.concatenate([other, piece], axis=axis),
            jnp.concatenate([piece, other], axis=axis),
        )
    return piece


def small_scatter(value):
    value = value.reshape(lax.axis_size("dp"), -1)
    for name, axis in (("tensor", 1), ("dp", 0)):
        index = lax.axis_index(name)
        count = lax.axis_size(name)
        for bit in reversed(axis_bits(name)):
            low, high = jnp.split(value, 2, axis=axis)
            upper = (index & bit) != 0
            give = jnp.where(upper, low, high)
            keep = jnp.where(upper, high, low)
            value = keep + lax.ppermute(give, name, [(i, i ^ bit) for i in range(count)])
    return value.reshape(-1)


def norm_parts(values):
    centred = values - jnp.mean(values, axis=-1, keepdims=True)
    spread = jnp.mean(centred * centred, axis=-1, keepdims=True)
    scale = lax.rsqrt(spread + ln_eps)
    return centred * scale, scale


def norm_back(unit, scale, gain_vec, grad):
    inner = grad * gain_vec
    return scale * (
        inner
        - jnp.mean(inner, axis=-1, keepdims=True)
        - unit * jnp.mean(inner * unit, axis=-1, keepdims=True)
    )


def per_device(
    inputs, out_grad, owners, master_slots, momentum_slots, small_master, small_first, small_second
):
    rows_dev, width = inputs.shape
    tensor_count = lax.axis_size("tensor")
    data_count = lax.axis_size("dp")
    tensor_idx = lax.axis_index("tensor")
    data_idx = lax.axis_index("dp")
    head_width = width // tensor_count
    ff_width = FF // tensor_count
    share = width // data_count
    share_out = head_width // data_count
    core = jnp.reshape(tensor_idx & 1, (1,)).astype(jnp.int32)
    owner_row = lax.dynamic_index_in_dim(owners, tensor_idx, 0, keepdims=False)
    owned = owner_row == data_idx
    slot_value = master_slots[0]

    group_params = small_gather(small_master.reshape(1, -1), "tensor", 1)
    params = small_gather(group_params, "dp", 0)
    slot_low = slot_value.astype(BF16)
    offer_out = slot_low[:head_width].reshape(data_count, share_out, tensor_count, head_width)
    offer_out = jnp.swapaxes(offer_out, 1, 2).reshape(data_count, share, head_width)
    offer_out = jnp.pad(offer_out, ((0, 0), (0, 0), (width - head_width, 0)))
    offer = jnp.where(owned[1], offer_out, slot_low.reshape(data_count, share, width))
    offer = tie(offer, params)
    shares = lax.all_to_all(offer, "dp", 0, 0)
    params = params.reshape(-1)

    def own_slice(start, size):
        return lax.dynamic_slice_in_dim(params, start + tensor_idx * size, size, 0)

    gain_one = params[0:width]
    shift_one = params[width : 2 * width]
    bias_query = own_slice(2 * width, head_width)
    bias_value = own_slice(3 * width, head_width)
    bias_out = params[4 * width : 5 * width]
    gain_two = params[5 * width : 6 * width]
    shift_two = params[6 * width : 7 * width]
    bias_fc = own_slice(7 * width, ff_width)
    bias_proj = params[7 * width + FF :]

    part = rows_dev // CHUNKS
    rows_of = [slice(chunk * part, (chunk + 1) * part) for chunk in range(CHUNKS)]
    rows_in = inputs.astype(F32)
    unit_one, scale_one = norm_parts(rows_in)
    inputs_four = gather_four(tie(inputs, offer))
    unit_all, _ = norm_parts(jnp.concatenate(inputs_four).astype(F32))
    normed_all = (unit_all * gain_one + shift_one).astype(BF16)
    dy_four = [gather_four(after(out_grad[rows], inputs_four[1])) for rows in rows_of]
    dy_all = [jnp.concatenate(four) for four in dy_four]

    shares = after(shares, normed_all, *dy_all)

    def share_of(kind):
        return lax.dynamic_index_in_dim(shares, owner_row[kind], 0, keepdims=False)

    split = 2 * head_width
    first = share_of(0)
    piece = open_piece(
        jnp.concatenate([first[:, : split + head_width], share_of(1)[:, width - head_width :]], axis=1)
    )
    for bit in last_bits(2, 1)[:-2]:
        piece = double(piece, bit)
    two_qk = double(piece[..., :split], 2)
    two_vo = double(piece[..., split:], 1)
    w_qk, w_vo = rows2(double(two_qk, 1)), rows2(double(two_vo, 2))
    w_v = w_vo[:, :head_width]
    w_out = w_vo[:, head_width:].reshape(data_count, tensor_count, share_out, head_width)
    w_out = jnp.swapaxes(w_out, 1, 2).reshape(head_width, width)
    bits_proj = last_bits(1, 2)
    bits_fc = last_bits(2, 1)
    w_proj = double(open_piece(tie(share_of(3), two_qk, two_vo)), bits_proj[0])
    w_fc = double(open_piece(tie(share_of(2), w_proj, w_qk)), bits_fc[0])
    bias_qk = jnp.concatenate([bias_query, jnp.zeros_like(bias_query)])
    scale_qk = jnp.where(jnp.arange(split) < head_width, HEAD_DIM**-0.5, 1.0)
    qk = ((mm(normed_all, w_qk) + bias_qk) * scale_qk).astype(BF16)
    values = (mm(normed_all, w_v) + bias_value).astype(BF16)
    qk = qk.reshape(2, 2, rows_dev, split)
    values = values.reshape(2, 2, rows_dev, head_width)

    first_steps = (w_proj, w_fc)
    for bit in bits_proj[1:-1]:
        w_proj = double(w_proj, bit)
    for bit in bits_fc[1:-1]:
        w_fc = double(w_fc, bit)
    mixed, log_sums, parts = [], [], []
    for chunk in range(CHUNKS):
        late = (qk, values) if chunk == 0 else after((qk, values), *first_steps)
        mixed_one, sums_one = attend(core, *late, chunk, CHUNKS)
        if chunk > 0:
            mixed_one = after(mixed_one, w_proj, w_fc)
        mixed.append(mixed_one)
        log_sums.append(sums_one)
        parts.append(scatter_begin([rows2(mixed_one)], [w_out], NN))
    w_proj = rows2(double(after(w_proj, mixed[-1]), bits_proj[-1]))
    w_fc = rows2(double(after(w_fc, mixed[-1]), bits_fc[-1]))
    back_act = [mm(after(dy, parts[-1]), w_proj, NT).astype(BF16) for dy in dy_all]
    middles, mine_two, normed_two = [], [], []
    branches = [exchange(value) for value in parts]
    for chunk in range(CHUNKS):
        rows = rows_of[chunk]
        branch = branches[chunk]
        if chunk > 0:
            branch = after(branch, normed_two[-1])
        residual = jnp.concatenate([inputs[rows], inputs_four[1][rows]]).astype(F32)
        middle = residual + branch + bias_out
        unit_two, scale_two = norm_parts(middle)
        normed_two.append((unit_two * gain_two + shift_two).astype(BF16))
        middles.append(middle[:part])
        mine_two.append((unit_two, scale_two))

    acts, backs, wholes, parts, sums_two = [], [], [], [], []
    grad_proj, grad_fc, fc_bias_grad = 0.0, 0.0, 0.0
    for chunk in range(CHUNKS):
        block = (normed_two[chunk], swap(normed_two[chunk], 1))
        if chunk > 0:
            block = after(block, parts[-1])
        act, back, sums, whole = hidden_layer(block, w_fc, bias_fc, back_act[chunk])
        parts.append(scatter_begin([after(back, *sums_two)], [w_fc], NT))
        sums_two.append(exchange(parts[-1]))
        acts.append(act)
        backs.append(back)
        wholes.append(whole)
        fc_bias_grad = fc_bias_grad + sums[0]
    back_middles, back_lows, back_mixed, mids = [], [], [], []
    gain_two_grad, shift_two_grad = 0.0, 0.0
    for chunk in range(CHUNKS):
        unit_two, scale_two = mine_two[chunk]
        grad = after(sums_two[chunk], parts[-1], *back_lows[-1:])
        dy = jnp.concatenate(dy_four[chunk][:2]).astype(F32)
        back_middle = dy + norm_back(unit_two, scale_two, gain_two, grad)
        back_lows.append(back_middle.astype(BF16))
        gain_two_grad = gain_two_grad + jnp.sum(grad[:part] * unit_two[:part], axis=0)
        shift_two_grad = shift_two_grad + jnp.sum(grad[:part], axis=0)
        back_middles.append(back_middle[:part])
        block = after((back_lows[-1], swap(back_lows[-1], 1)), parts[-1])
        grad_rows = (acts[chunk], wholes[chunk], backs[chunk])
        act, whole, back = after(grad_rows, parts[0] if chunk == 0 else back_lows[0])
        grad_proj = grad_proj + mm(act, dy_all[chunk], TN)
        grad_fc = grad_fc + mm(whole, back, TN)
        mixed_grad, mid = back_mix(block, w_out)
        back_mixed.append(mixed_grad.reshape(2, 2, part, head_width))
        mids.append(mid)
    middle = jnp.concatenate(middles)
    back_middle = jnp.concatenate(back_middles)
    proj_bias_grad = jnp.sum(out_grad, axis=0, dtype=F32)
    out_bias_grad = jnp.sum(back_middle, axis=0)

    grad_proj, grad_fc = grad_proj.astype(BF16), grad_fc.astype(BF16)
    half_proj = halve(spread(grad_proj), 1)
    half_fc = halve(spread(grad_fc), 2)
    back_mixed, half_proj, half_fc = lax.optimization_barrier((back_mixed, half_proj, half_fc))
    steps = axis_bits("dp")
    rest_proj, rest_fc = steps[1:], steps[2:] + [1]
    half_proj = halve(half_proj, rest_proj[0])
    half_fc = halve(half_fc, rest_fc[0])
    attend_grad = attend_back(core, qk, values, mixed, log_sums, back_mixed, 0)
    acts = after(acts, attend_grad[0])
    branch_parts = [scatter_begin([act], [w_proj], NN) for act in acts]
    back_mixed = after(back_mixed, half_proj, half_fc, *branch_parts)
    back_qk, back_v = attend_back(core, qk, values, mixed, log_sums, back_mixed, 1, attend_grad)
    share_proj = halve_by(half_proj, rest_proj[1:])
    share_fc = halve_by(half_fc, rest_fc[1:])
    grad_out = sum(mm(rows2(mixed[i]), mids[i], TN) for i in range(CHUNKS)).astype(BF16)
    grad_out = grad_out.reshape(data_count, share_out, tensor_count, head_width)
    grad_out = jnp.swapaxes(grad_out, 1, 2).reshape(width, head_width)
    grad_qk = mm(normed_all, rows2(back_qk), TN).astype(BF16)
    grad_v = mm(normed_all, rows2(back_v), TN).astype(BF16)
    grad_vo = jnp.concatenate([grad_v, grad_out], axis=1)
    half_qk = halve(spread(grad_qk), 1)
    half_vo = halve(spread(grad_vo), 2)
    share_attend = jnp.concatenate([halve(half_qk, 2), halve(half_vo, 1)], axis=-1)
    share_attend = rows2(halve_by(share_attend, steps[2:]))

    late_qk, late_v = after((back_qk, back_v), grad_qk, grad_vo)
    back_normed = scatter_end(scatter_begin([rows2(late_qk), rows2(late_v)], [w_qk, w_v], NT))
    branches = [scatter_end(value) for value in branch_parts]
    block_out = (middle + jnp.concatenate(branches) + bias_proj).astype(BF16)
    input_grad = back_middle + norm_back(unit_one, scale_one, gain_one, back_normed)
    gain_one_grad = jnp.sum(back_normed * unit_one, axis=0)
    shift_one_grad = jnp.sum(back_normed, axis=0)
    query_bias_grad = jnp.sum(late_qk[..., :head_width], axis=(0, 1, 2), dtype=F32)
    value_bias_grad = jnp.sum(late_v, axis=(0, 1, 2), dtype=F32)

    bundle = jnp.zeros((data_count, share, width), BF16)
    pieces = (
        jnp.pad(share_attend[:, : 3 * head_width], ((0, 0), (0, width - 3 * head_width))),
        jnp.pad(share_attend[:, width - head_width :], ((0, 0), (width - head_width, 0))),
        rows2(share_fc),
        rows2(share_proj),
    )
    for kind in range(4):
        bundle = lax.dynamic_update_index_in_dim(bundle, pieces[kind], owner_row[kind], 0)
    landed = lax.all_to_all(bundle, "dp", 0, 0)
    full_grad = jnp.concatenate(
        [
            gain_one_grad,
            shift_one_grad,
            jnp.zeros((2 * width,), F32),
            out_bias_grad,
            gain_two_grad,
            shift_two_grad,
            jnp.zeros((FF,), F32),
            proj_bias_grad,
        ]
    )
    for grad, start, size in (
        (query_bias_grad, 2 * width, head_width),
        (value_bias_grad, 3 * width, head_width),
        (fc_bias_grad, 7 * width, ff_width),
    ):
        full_grad = lax.dynamic_update_slice_in_dim(full_grad, grad, start + tensor_idx * size, 0)
    small_grad = small_scatter(full_grad)
    first_new = beta_one * small_first + (1.0 - beta_one) * small_grad
    second_new = beta_two * small_second + (1.0 - beta_two) * small_grad * small_grad
    first_hat = first_new / (1.0 - beta_one**STEP)
    second_hat = second_new / (1.0 - beta_two**STEP)
    small_new = small_master - adam_rate * first_hat / (jnp.sqrt(second_hat) + adam_eps)

    row_limit = jnp.where(owned[1], head_width, jnp.where(jnp.any(owned), width, 0))
    col_limit = jnp.where(owned[0], 3 * head_width, width)
    limits = jnp.stack([row_limit, col_limit, owned[1].astype(jnp.int32)]).astype(jnp.int32)
    grad_slot, mom_slot, fresh_slot = muon_update(
        limits, landed, momentum_slots[0], slot_value, share_out
    )
    return (
        block_out,
        input_grad,
        grad_slot[None],
        mom_slot[None],
        fresh_slot[None],
        small_grad,
        second_new,
        small_new,
    )


def solution(mesh):
    return jax.shard_map(
        per_device,
        mesh=mesh,
        in_specs=(
            P(("dp", "tensor"), None),
            P(("dp", "tensor"), None),
            P(),
            P("dp", "tensor", None),
            P("dp", "tensor", None),
            P(("dp", "tensor")),
            P(("dp", "tensor")),
            P(("dp", "tensor")),
        ),
        out_specs=(
            P(("dp", "tensor"), None),
            P(("dp", "tensor"), None),
            P("dp", "tensor", None),
            P("dp", "tensor", None),
            P("dp", "tensor", None),
            P(("dp", "tensor")),
            P(("dp", "tensor")),
            P(("dp", "tensor")),
        ),
        check_vma=False,
    )
```
